32 devices in a mesh: grp: 2 (over x), fsdp: 4 (over y, core), dp: 4 (over z).
Axes of the slice: x: 2, y: 2, z: 4, core: 2. Of those that a mesh axis runs over, the one named last changes fastest.
Arguments:
- tokens: bfloat16 [2, 34816, 1024], P(None, ('grp', 'fsdp', 'dp')), may hold values from -6 to 6
- cotangent: bfloat16 [2, 34816, 1024], P(None, ('grp', 'fsdp', 'dp')), may hold values from -6 to 6
- lengths: int32 [2, 32, 8], P(None, ('grp', 'fsdp', 'dp')), may hold values from 0 to 1088, as said below
- selected: int32 [2, 32, 136], P(None, ('grp', 'fsdp', 'dp')), may hold values from 0 to 1087, as said below
- weights: float32 [12288, 1024], P(('fsdp', 'dp')), may hold values from -0.25 to 0.25
- vectors: float32 [3, 1024], replicated, may hold values from -0.09375 to 1.1
- first_moment: float32 [2, 12288, 1024], P('grp', ('fsdp', 'dp')), may hold values from -7.836799 to 7.836799
- second_moment: float32 [2, 12288, 1024], P('grp', ('fsdp', 'dp')), may hold values from 4.352 to 43.52
- vec_first: float32 [2, 3, 1024], P('grp'), may hold values from -186.59046 to 186.59046
- vec_second: float32 [2, 3, 1024], P('grp'), may hold values from 12.6208 to 55705.6
- outer_moment: float32 [12288, 1024], P(('fsdp', 'dp'), 'grp'), may hold values from -0.3125 to 0.3125
- smoothed_matrix_mean: float32 [12288, 1024], P(('fsdp', 'dp'), 'grp'), may hold values from -0.1875 to 0.1875
- vec_outer: float32 [3, 1024], replicated, may hold values from -1.25 to 1.25
- vec_average: float32 [3, 1024], replicated, may hold values from -0.3125 to 0.3125
Outputs:
- activations: bfloat16 [2, 34816, 1024], P(None, ('grp', 'fsdp', 'dp'))
- input_grad: bfloat16 [2, 34816, 1024], P(None, ('grp', 'fsdp', 'dp'))
- weights_new: float32 [12288, 1024], P(('fsdp', 'dp'))
- weights_low: bfloat16 [12288, 1024], P(('fsdp', 'dp'))
- first_new: float32 [2, 12288, 1024], P('grp', ('fsdp', 'dp'))
- second_new: float32 [2, 12288, 1024], P('grp', ('fsdp', 'dp'))
- outer_new: float32 [12288, 1024], P(('fsdp', 'dp'), 'grp')
- diff_mean: float32 [12288, 1024], P(('fsdp', 'dp'), 'grp')
- average_new: float32 [12288, 1024], P(('fsdp', 'dp'), 'grp')
- vectors_new: float32 [3, 1024], replicated
- vec_first_new: float32 [2, 3, 1024], P('grp')
- gains_second_new: float32 [2, 2, 1024], P('grp')
- router_second_new: float32 [2, 1024], P('grp')
- vec_outer_new: float32 [3, 1024], replicated
- vec_average_new: float32 [3, 1024], replicated
The draws below stay inside these ranges and needn't reach their ends.
Inputs may be any that keep to these rules, and one draw needn't show every extreme that they name: Each device's 8 lengths are multiples of 8 that sum to 1088; zero marks an unused slot; in every draw some device holds a single sequence of 1088 tokens. Each device's selected positions ascend; a sequence of length L on it has exactly L / 8 of them, all inside it; the device's first and last positions are always among them.
All inputs are finite; a program needn't handle non-finite values.
Results may differ from the reference program's by a relative error of at most 0.018.
Values may be sent and summed in bfloat16 or wider, within the bound.
No kernel may reach another device: no remote copies, remote signals or barrier semaphores. Data moves between devices by JAX's collectives and lax.ppermute only.
A program may use at most 384 MiB of HBM per device.

```python
import jax
import jax.numpy as jnp
from jax import lax

D = 1024
HEAD = 64
FF = 4096
LOCAL_BATCH_SIZE = 1088
SLOTS = 8
INNER = 2
STEP = 5
WROWS = 12288
TOKENS = 34816
N_GRP = 2
N_FSDP = 4
N_DP = 4
DEVICES = 32


def layout(key):
    units = LOCAL_BATCH_SIZE // 8
    count_rows = INNER * DEVICES
    key_cut, key_long, key_pick = jax.random.split(key, 3)
    sorted_indices = jax.random.randint(key_cut, (count_rows, units - 1), 0, 1 << 20) * units + jnp.arange(units - 1, dtype=jnp.int32)[None, :]
    order = jnp.argsort(sorted_indices, axis=1).astype(jnp.int32)
    cuts = jnp.sort(order[:, :SLOTS - 1] + 1, axis=1)
    edges = jnp.concatenate([jnp.zeros((count_rows, 1), jnp.int32), cuts, jnp.full((count_rows, 1), units, jnp.int32)], axis=1)
    parts = edges[:, 1:] - edges[:, :-1]
    single = (jnp.arange(SLOTS) == 0).astype(jnp.int32) * units
    flagged = (jax.random.randint(key_long, (count_rows,), 0, 4) == 0) | (jnp.arange(count_rows) == jax.random.randint(key_pick, (), 0, count_rows))
    parts = jnp.where(flagged[:, None], single[None, :], parts)
    return (parts * 8).astype(jnp.int32).reshape(INNER, DEVICES, SLOTS)


def group_scale():
    return (LOCAL_BATCH_SIZE // 8 * N_FSDP * N_DP) ** 0.5


def draw_lengths(key, part):
    return layout(key)


def draw_selected(key, part):
    seq_lengths = layout(key).reshape(INNER * DEVICES, SLOTS)
    key = jax.random.fold_in(key, 2)
    sequence_indices = jnp.arange(LOCAL_BATCH_SIZE, dtype=jnp.int32)
    selection_logits = jax.random.randint(key, (INNER * DEVICES, LOCAL_BATCH_SIZE), 0, 1 << 16) * LOCAL_BATCH_SIZE + sequence_indices[None, :]
    priority_offset = (1 << 16) * LOCAL_BATCH_SIZE + LOCAL_BATCH_SIZE
    selection_logits = jnp.where((sequence_indices == 0) | (sequence_indices == LOCAL_BATCH_SIZE - 1), priority_offset, selection_logits)

    def one_device(pieces):
        length_per_row, score_row = pieces
        ends = jnp.cumsum(length_per_row).astype(jnp.int32)
        segment_ids = jnp.sum((ends[None, :] <= sequence_indices[:, None]).astype(jnp.int32), axis=1)
        quota = jnp.sum((segment_ids[:, None] == jnp.arange(SLOTS)[None, :]).astype(jnp.int32) * length_per_row[None, :], axis=1) // 8
        same = segment_ids[:, None] == segment_ids[None, :]
        above = same & (score_row[None, :] > score_row[:, None])
        ranks = jnp.sum(above.astype(jnp.int32), axis=1)
        return jnp.nonzero(ranks < quota, size=LOCAL_BATCH_SIZE // 8)[0].astype(jnp.int32)
    picked = lax.map(one_device, (seq_lengths, selection_logits))
    return picked.reshape(INNER, DEVICES, LOCAL_BATCH_SIZE // 8)


def draw_tokens(key, part):
    key = jax.random.fold_in(key, 7)
    values = jnp.clip(jax.random.normal(key, (INNER, TOKENS, D), jnp.float32), -6.0, 6.0)
    return values.astype(jnp.bfloat16)


def draw_cotangent(key, part):
    key = jax.random.fold_in(key, 8)
    values = jnp.clip(jax.random.normal(key, (INNER, TOKENS, D), jnp.float32), -6.0, 6.0)
    return values.astype(jnp.bfloat16)


def draw_first_moment(key, part):
    key = jax.random.fold_in(key, 9)
    base = jnp.clip(jax.random.normal(key, (N_GRP, WROWS, D), jnp.float32), -6.0, 6.0)
    return 0.028 * group_scale() * base


def draw_second_moment(key, part):
    key = jax.random.fold_in(key, 10)
    spread = jnp.exp(jax.random.uniform(key, (N_GRP, WROWS, D), jnp.float32, jnp.log(0.002), jnp.log(0.02)))
    return spread * (group_scale() * group_scale())


def draw_weights(key, part):
    key = jax.random.fold_in(key, 3)
    row_ids = jnp.arange(WROWS)[:, None]
    inverse = D ** (-0.5)
    scale = jnp.where(row_ids < 3 * D, inverse, jnp.where(row_ids < 4 * D, 2.0 * inverse, jnp.where(row_ids < 4 * D + FF, inverse, 1.5 * FF ** (-0.5))))
    base = jnp.clip(jax.random.normal(key, (WROWS, D), jnp.float32), -4.0, 4.0)
    return base * scale


def draw_vectors(key, part):
    key = jax.random.fold_in(key, 4)
    key_gain, key_router = jax.random.split(key)
    gains = 1.0 + 0.1 * jax.random.uniform(key_gain, (2, D), jnp.float32, -1.0, 1.0)
    router = 0.75 * D ** (-0.5) * jnp.clip(jax.random.normal(key_router, (1, D), jnp.float32), -4.0, 4.0)
    return jnp.concatenate([gains, router], axis=0)


def draw_vec_first(key, part):
    key = jax.random.fold_in(key, 5)
    rows = jnp.array([0.4, 0.45, 9.0], jnp.float32)[None, :, None] * group_scale()
    base = jnp.clip(jax.random.normal(key, (N_GRP, 3, D), jnp.float32), -4.0, 4.0)
    return 0.111 * rows * base


def draw_vec_second(key, part):
    key = jax.random.fold_in(key, 6)
    rows = jnp.array([0.4, 0.45, 9.0], jnp.float32)[None, :, None] * group_scale()
    spread = jnp.exp(jax.random.uniform(key, (N_GRP, 3, D), jnp.float32, jnp.log(0.7), jnp.log(6.0)))
    return 0.0526 * rows * rows * spread


def block_levels(rng, dims, cuts, low, high):
    loudness, own = 1.0, jax.random.fold_in(rng, 6)
    for dim, blocks in cuts:
        heights = jnp.exp(jax.random.uniform(jax.random.fold_in(own, dim), (blocks,), jnp.float32, low / len(cuts), high / len(cuts)))
        loudness = loudness * jnp.repeat(heights, dims[dim] // blocks).reshape([-1 if axis == dim else 1 for axis in range(len(dims))])
    return loudness


def noise(stream_key, extent, scale, bound, cuts=(), held_as=jnp.bfloat16):
    entries = jax.random.normal(stream_key, extent, jnp.float32) * scale
    if len(cuts) > 0:
        entries = block_levels(stream_key, extent, cuts, -0.22, 0.18) * entries
    return jnp.clip(entries, min=-bound, max=bound).astype(held_as)


def setup_inputs(seed: int = 0) -> dict:
    key_list = jax.random.split(jax.random.key(seed), 15)
    return {
        "tokens": draw_tokens(jax.random.fold_in(key_list[14], 71), 0),
        "cotangent": draw_cotangent(jax.random.fold_in(key_list[14], 71), 0),
        "lengths": draw_lengths(jax.random.fold_in(key_list[14], 71), 0),
        "selected": draw_selected(jax.random.fold_in(key_list[14], 71), 0),
        "weights": draw_weights(jax.random.fold_in(key_list[14], 71), 0),
        "vectors": draw_vectors(jax.random.fold_in(key_list[14], 71), 0),
        "first_moment": draw_first_moment(jax.random.fold_in(key_list[14], 71), 0),
        "second_moment": draw_second_moment(jax.random.fold_in(key_list[14], 71), 0),
        "vec_first": draw_vec_first(jax.random.fold_in(key_list[14], 71), 0),
        "vec_second": draw_vec_second(jax.random.fold_in(key_list[14], 71), 0),
        "outer_moment": noise(key_list[10], (WROWS, D), 0.05, 0.3125, ((0, 16), (1, 2)), jnp.float32),
        "smoothed_matrix_mean": noise(key_list[11], (WROWS, D), 0.03, 0.1875, ((0, 16), (1, 2)), jnp.float32),
        "vec_outer": noise(key_list[12], (3, D), 0.2, 1.25, (), jnp.float32),
        "vec_average": noise(key_list[13], (3, D), 0.05, 0.3125, (), jnp.float32),
    }


EPS_NORM = 1e-06
EPS_ADAM = 1e-08
BETA_ONE = 0.9
BETA_TWO = 0.95
INNER_RATE = 0.03
DECAY_RATE = 0.1
OUTER_RATE = 0.7
OUTER_MOMENTUM = 0.9
AVERAGE_KEEP = 0.9

@jax.custom_vjp
def low(v):
    return lax.optimization_barrier(v.astype(jnp.bfloat16)).astype(jnp.float32)

@jax.custom_vjp
def lowered_backward(v):
    return v

def low_keep(v):
    return (low(v), None)

def low_pass(kept, grad):
    return (grad,)

def back_keep(v):
    return (v, None)

def back_low(kept, grad):
    return (low(grad),)
low.defvjp(low_keep, low_pass)
lowered_backward.defvjp(back_keep, back_low)

def matmul(left, right):
    return jnp.dot(left, right, precision=lax.Precision.HIGHEST)

def apply_norm(values):
    return values * lax.rsqrt(lax.optimization_barrier(jnp.mean(values * values, axis=-1, keepdims=True)) + EPS_NORM)

def segments_of(seq_lengths, positions):
    ends = jnp.cumsum(seq_lengths).astype(jnp.int32)
    sequence_indices = jnp.arange(positions, dtype=jnp.int32)
    return lax.optimization_barrier(jnp.sum((ends[None, :] <= sequence_indices[:, None]).astype(jnp.int32), axis=1)).astype(jnp.int32)

def device_forward(w_low, vectors_now, tokens_dev, seq_lengths, picked):
    count_of_heads = D // HEAD
    picked_count = picked.shape[0]
    segment_ids = segments_of(seq_lengths, tokens_dev.shape[0])
    seg_picked = segment_ids[picked]
    sel_rows = tokens_dev[picked]
    w_qkv = w_low[:3 * D]
    w_out = w_low[3 * D:4 * D]
    w_up = w_low[4 * D:4 * D + FF]
    w_down = w_low[4 * D + FF:]
    gate_value = jax.nn.sigmoid(matmul(sel_rows, vectors_now[2]))
    normed_one = apply_norm(sel_rows) * vectors_now[0]
    projected = lowered_backward(low(matmul(low(normed_one), w_qkv.T)))
    query_rows = projected[:, :D].reshape(picked_count, count_of_heads, HEAD)
    key_rows = projected[:, D:2 * D].reshape(picked_count, count_of_heads, HEAD)
    value_rows = projected[:, 2 * D:].reshape(picked_count, count_of_heads, HEAD)
    allowed = (seg_picked[:, None] == seg_picked[None, :]) & (picked[None, :] <= picked[:, None])
    selection_logits = lowered_backward(jnp.einsum('qhe,khe->hqk', query_rows, key_rows, precision=lax.Precision.HIGHEST) * HEAD ** (-0.5))
    selection_logits = jnp.where(allowed[None], selection_logits, -1e+30)
    attn_probs = jax.nn.softmax(selection_logits, axis=-1)
    mixed = jnp.einsum('hqk,khe->qhe', low(attn_probs), value_rows, precision=lax.Precision.HIGHEST)
    mixed = lowered_backward(low(mixed.reshape(picked_count, D)))
    attn_out = lowered_backward(matmul(mixed, w_out.T))
    first_sum = sel_rows + attn_out
    normed_two = apply_norm(first_sum) * vectors_now[1]
    pre_act = lowered_backward(matmul(low(normed_two), w_up.T))
    activated = jax.nn.gelu(pre_act, approximate=True)
    down_out = lowered_backward(matmul(low(activated), w_down))
    out_rows = sel_rows + gate_value[:, None] * (attn_out + down_out)
    return tokens_dev.at[picked].set(out_rows)

def group_pass(weights_now, vectors_now, tokens_grp, cot_grp, lengths_grp, selected_grp):

    def forward(weights_in, vectors_in, tokens_in):
        w_low = low(weights_in)

        def one_device(pieces):
            return device_forward(w_low, vectors_in, pieces[0], pieces[1], pieces[2])
        return lax.map(jax.checkpoint(one_device), (tokens_in, lengths_grp, selected_grp))
    outputs, pull = jax.vjp(forward, weights_now, vectors_now, tokens_grp)
    grad_w, grad_v, grad_x = pull(cot_grp)
    return (outputs, grad_w, grad_v, grad_x)

def adamw(param, grad, first, second, step_count, rate, decay):
    first = BETA_ONE * first + (1.0 - BETA_ONE) * grad
    second = BETA_TWO * second + (1.0 - BETA_TWO) * grad * grad
    fixed_one = 1.0 - BETA_ONE ** step_count
    fixed_two = 1.0 - BETA_TWO ** step_count
    direction = first / fixed_one / (jnp.sqrt(second / fixed_two) + EPS_ADAM)
    return (param - rate * (direction + decay * param), first, second)

def vector_rates():
    return jnp.array([[0.1], [0.1], [0.02]], dtype=jnp.float32)

def reference(tokens, cotangent, lengths, selected, weights, vectors, first_moment, second_moment, vec_first, vec_second, outer_moment, smoothed_matrix_mean, vec_outer, vec_average):
    group_devices = N_FSDP * N_DP
    group_tokens = LOCAL_BATCH_SIZE * group_devices
    states = []
    for group in range(N_GRP):
        states.append([weights, vectors, first_moment[group], second_moment[group], vec_first[group], vec_second[group]])
    forward_steps = []
    backward_steps = []
    for inner_step in range(INNER):
        forward_rows = []
        backward_rows = []
        for group in range(N_GRP):
            lower = group * group_tokens
            tokens_grp = tokens[inner_step, lower:lower + group_tokens].astype(jnp.float32).reshape(group_devices, LOCAL_BATCH_SIZE, D)
            cot_grp = cotangent[inner_step, lower:lower + group_tokens].astype(jnp.float32).reshape(group_devices, LOCAL_BATCH_SIZE, D)
            first_dev = group * group_devices
            lengths_grp = lengths[inner_step, first_dev:first_dev + group_devices]
            selected_grp = selected[inner_step, first_dev:first_dev + group_devices]
            w_now, v_now, m_now, s_now, p_now, q_now = states[group]
            outputs, grad_w, grad_v, grad_x = group_pass(w_now, v_now, tokens_grp, cot_grp, lengths_grp, selected_grp)
            step_count = STEP + inner_step
            w_now, m_now, s_now = adamw(w_now, grad_w, m_now, s_now, step_count, INNER_RATE, DECAY_RATE)
            v_now, p_now, q_now = adamw(v_now, grad_v, p_now, q_now, step_count, vector_rates(), 0.0)
            states[group] = [w_now, v_now, m_now, s_now, p_now, q_now]
            forward_rows.append(outputs.reshape(group_tokens, D))
            backward_rows.append(grad_x.reshape(group_tokens, D))
        forward_steps.append(jnp.concatenate(forward_rows, axis=0))
        backward_steps.append(jnp.concatenate(backward_rows, axis=0))
    activations = jnp.stack(forward_steps).astype(jnp.bfloat16)
    input_grad = jnp.stack(backward_steps).astype(jnp.bfloat16)
    diff_total = jnp.zeros_like(weights)
    vec_total = jnp.zeros_like(vectors)
    for group in range(N_GRP):
        diff_total = diff_total + (weights - states[group][0])
        vec_total = vec_total + (vectors - states[group][1])
    diff_mean = diff_total / N_GRP
    vec_diff = vec_total / N_GRP
    outer_new = OUTER_MOMENTUM * outer_moment + diff_mean
    weights_new = weights - OUTER_RATE * (diff_mean + OUTER_MOMENTUM * outer_new)
    average_new = AVERAGE_KEEP * smoothed_matrix_mean + (1.0 - AVERAGE_KEEP) * weights_new
    vec_outer_new = OUTER_MOMENTUM * vec_outer + vec_diff
    vectors_new = vectors - OUTER_RATE * (vec_diff + OUTER_MOMENTUM * vec_outer_new)
    vec_average_new = AVERAGE_KEEP * vec_average + (1.0 - AVERAGE_KEEP) * vectors_new
    first_new = jnp.stack([states[group][2] for group in range(N_GRP)])
    second_new = jnp.stack([states[group][3] for group in range(N_GRP)])
    vec_first_new = jnp.stack([states[group][4] for group in range(N_GRP)])
    vec_second_new = jnp.stack([states[group][5] for group in range(N_GRP)])
    return (activations, input_grad, weights_new, weights_new.astype(jnp.bfloat16), first_new, second_new, outer_new, diff_mean, average_new, vectors_new, vec_first_new, vec_second_new[:, :2], vec_second_new[:, 2], vec_outer_new, vec_average_new)
```

```python
import jax
import jax.numpy as jnp
import numpy as np
from jax import lax
from jax.sharding import PartitionSpec as P

HEAD = 64
INNER = 2
STEP = 5


EPS_NORM = 1e-06
EPS_ADAM = 1e-08
BETA_ONE = 0.9
BETA_TWO = 0.95
INNER_RATE = 0.03
DECAY_RATE = 0.1
OUTER_RATE = 0.7
OUTER_MOMENTUM = 0.9
AVERAGE_KEEP = 0.9


def segments_of(seq_lengths, positions):
    ends = jnp.cumsum(seq_lengths)
    sequence_indices = jnp.arange(positions, dtype=jnp.int32)
    return jnp.sum((ends[None, :] <= sequence_indices[:, None]).astype(jnp.int32), axis=1)


def contract_last(left, right):
    return lax.dot_general(
        left, right, (((1,), (1,)), ((), ())), preferred_element_type=jnp.float32
    )


def contract_first(left, right):
    return lax.dot_general(
        left, right, (((0,), (0,)), ((), ())), preferred_element_type=jnp.float32
    )


def split_rows(gathered, model_width):
    hidden_units = (gathered.shape[0] - 4 * model_width) // 2
    w_qkv = gathered[: 3 * model_width]
    w_out = gathered[3 * model_width : 4 * model_width]
    w_up = gathered[4 * model_width : 4 * model_width + hidden_units]
    w_down = gathered[4 * model_width + hidden_units :]
    return (w_qkv, w_out, w_up, w_down)


def attention_scores(query_rows, key_rows, allowed):
    selection_logits = jnp.einsum(
        "qhe,khe->hqk", query_rows, key_rows, preferred_element_type=jnp.float32
    ) * HEAD ** (-0.5)
    return jnp.where(allowed[None], selection_logits, -1e30)


def gelu_tanh(values):
    return jax.nn.gelu(values, approximate=True)


def norm_back(d_normed, normed, inverse):
    return inverse * (d_normed - normed * jnp.mean(d_normed * normed, axis=-1, keepdims=True))


def forward_pass(gathered, vec_now, tokens_now, seq_lengths, picked):
    model_width = tokens_now.shape[1]
    count_of_heads = model_width // HEAD
    picked_count = picked.shape[0]
    w_qkv, w_out, w_up, w_down = split_rows(gathered, model_width)
    segment_ids = segments_of(seq_lengths, tokens_now.shape[0])
    seg_picked = segment_ids[picked]
    sel_rows = tokens_now[picked].astype(jnp.float32)
    gate_value = jax.nn.sigmoid(jnp.dot(sel_rows, vec_now[2], precision=lax.Precision.HIGHEST))
    inv_one = lax.rsqrt(jnp.mean(sel_rows * sel_rows, axis=-1, keepdims=True) + EPS_NORM)
    normed_one = sel_rows * inv_one
    h1_low = (normed_one * vec_now[0]).astype(jnp.bfloat16)
    projected = contract_last(h1_low, w_qkv).astype(jnp.bfloat16)
    heads_view = projected.reshape(picked_count, 3, count_of_heads, HEAD)
    allowed = (seg_picked[:, None] == seg_picked[None, :]) & (picked[None, :] <= picked[:, None])
    selection_logits = attention_scores(heads_view[:, 0], heads_view[:, 1], allowed)
    row_max = jnp.max(selection_logits, axis=-1, keepdims=True)
    log_total = row_max + jnp.log(
        jnp.sum(jnp.exp(selection_logits - row_max), axis=-1, keepdims=True)
    )
    probs_low = jnp.exp(selection_logits - log_total).astype(jnp.bfloat16)
    mixed = jnp.einsum(
        "hqk,khe->qhe", probs_low, heads_view[:, 2], preferred_element_type=jnp.float32
    )
    mixed = mixed.reshape(picked_count, model_width).astype(jnp.bfloat16)
    attn_out = contract_last(mixed, w_out)
    first_sum = sel_rows + attn_out
    inv_two = lax.rsqrt(jnp.mean(first_sum * first_sum, axis=-1, keepdims=True) + EPS_NORM)
    normed_two = first_sum * inv_two
    h2_low = (normed_two * vec_now[1]).astype(jnp.bfloat16)
    pre_act = contract_last(h2_low, w_up)
    act_low = gelu_tanh(pre_act).astype(jnp.bfloat16)
    down_out = jnp.dot(act_low, w_down, preferred_element_type=jnp.float32)
    branch = attn_out + down_out
    out_rows = sel_rows + gate_value[:, None] * branch
    return {
        "gate_value": gate_value,
        "sel_rows": sel_rows,
        "inv_one": inv_one,
        "normed_one": normed_one,
        "h1_low": h1_low,
        "projected": projected,
        "allowed": allowed,
        "log_total": log_total,
        "mixed": mixed,
        "inv_two": inv_two,
        "normed_two": normed_two,
        "h2_low": h2_low,
        "pre_act": pre_act,
        "act_low": act_low,
        "branch": branch,
        "out_rows": out_rows,
    }


def backward_pass(gathered, vec_now, saved, cot_now, picked):
    model_width = cot_now.shape[1]
    count_of_heads = model_width // HEAD
    picked_count = picked.shape[0]
    w_qkv, w_out, w_up, w_down = split_rows(gathered, model_width)
    cot_rows = cot_now[picked].astype(jnp.float32)
    gate_value = saved["gate_value"]
    d_branch = gate_value[:, None] * cot_rows
    d_logit = jnp.sum(cot_rows * saved["branch"], axis=-1) * gate_value * (1.0 - gate_value)
    d_down = d_branch.astype(jnp.bfloat16)
    d_act = contract_last(d_down, w_down)
    gelu_pull = jax.vjp(gelu_tanh, saved["pre_act"])[1]
    d_pre = gelu_pull(d_act)[0].astype(jnp.bfloat16)
    d_h2 = jnp.dot(d_pre, w_up, preferred_element_type=jnp.float32)
    grad_gain_two = jnp.sum(d_h2 * saved["normed_two"], axis=0)
    d_first = norm_back(d_h2 * vec_now[1], saved["normed_two"], saved["inv_two"])
    d_attn_low = (d_branch + d_first).astype(jnp.bfloat16)
    d_mixed = jnp.dot(d_attn_low, w_out, preferred_element_type=jnp.float32).astype(jnp.bfloat16)
    d_mixed = d_mixed.reshape(picked_count, count_of_heads, HEAD)
    heads_view = saved["projected"].reshape(picked_count, 3, count_of_heads, HEAD)
    query_rows = heads_view[:, 0]
    key_rows = heads_view[:, 1]
    value_rows = heads_view[:, 2]
    selection_logits = attention_scores(query_rows, key_rows, saved["allowed"])
    attn_probs = jnp.exp(selection_logits - saved["log_total"])
    probs_low = attn_probs.astype(jnp.bfloat16)
    d_probs = jnp.einsum("qhe,khe->hqk", d_mixed, value_rows, preferred_element_type=jnp.float32)
    d_scores = attn_probs * (d_probs - jnp.sum(d_probs * attn_probs, axis=-1, keepdims=True))
    d_scores = d_scores.astype(jnp.bfloat16)
    grad_query = jnp.einsum(
        "hqk,khe->qhe", d_scores, key_rows, preferred_element_type=jnp.float32
    ) * HEAD ** (-0.5)
    grad_key = jnp.einsum(
        "hqk,qhe->khe", d_scores, query_rows, preferred_element_type=jnp.float32
    ) * HEAD ** (-0.5)
    grad_value = jnp.einsum("hqk,qhe->khe", probs_low, d_mixed, preferred_element_type=jnp.float32)
    d_proj = jnp.stack([grad_query, grad_key, grad_value], axis=1).reshape(
        picked_count, 3 * model_width
    )
    d_proj = d_proj.astype(jnp.bfloat16)
    d_h1 = jnp.dot(d_proj, w_qkv, preferred_element_type=jnp.float32)
    derivative_first_gain_factor = jnp.sum(d_h1 * saved["normed_one"], axis=0)
    d_zero = norm_back(d_h1 * vec_now[0], saved["normed_one"], saved["inv_one"])
    d_rows = cot_rows + d_first + d_zero + d_logit[:, None] * vec_now[2][None, :]
    grad_router = jnp.dot(d_logit, saved["sel_rows"], precision=lax.Precision.HIGHEST)
    grad_vec = jnp.stack([derivative_first_gain_factor, grad_gain_two, grad_router])
    columns = jnp.concatenate([d_proj, d_attn_low, d_pre, saved["act_low"]], axis=1)
    operands = (saved["h1_low"], saved["mixed"], saved["h2_low"], d_down)
    return (d_rows, grad_vec, columns, operands)


def pad_rows(rows):
    return jnp.pad(rows, ((0, -rows.shape[0] % 16), (0, 0)))


def swap(values, axis, delta):
    size = lax.axis_size(axis)
    return lax.ppermute(values, axis, [(i, i ^ delta) for i in range(size)])


def sum_over(values, axes):
    for axis in axes:
        delta = 1
        while delta < lax.axis_size(axis):
            values = values + swap(values, axis, delta)
            delta *= 2
    return values


def line_order(line):
    due = np.zeros((line, line), np.int32)
    for here in range(line):
        for there in range(line):
            if there > here:
                due[here, there] = line - 1 - there + here
            elif there < here:
                due[here, there] = there - here + line - 1
            else:
                due[here, there] = line
    return np.argsort(due, axis=1, kind="stable").astype(np.int32)


def line_slots(line, order):
    ups = np.zeros((line - 1, line), np.int32)
    downs = np.zeros((line - 1, line), np.int32)
    for step in range(line - 1):
        for here in range(line):
            if here <= step:
                ups[step, here] = list(order[here]).index(line - 1 - step + here)
            if line - 1 - here <= step:
                downs[step, here] = list(order[here]).index(step - (line - 1) + here)
    return ups, downs


def choose(terms, slots, here):
    used = sorted(set(int(slot) for slot in slots))
    picked = terms[used[0]]
    for slot in used[1:]:
        picked = jnp.where(jnp.asarray(slots)[here] == slot, terms[slot], picked)
    return picked


def gradient_share(columns, operands, shard_rows, model_width):
    planes, line = lax.axis_size("fsdp"), lax.axis_size("dp")
    plane, here = lax.axis_index("fsdp"), lax.axis_index("dp")
    columns = pad_rows(columns)
    tokens = columns.shape[0]
    hidden_units = (columns.shape[1] - 4 * model_width) // 2
    edges = (3 * model_width, 4 * model_width, 4 * model_width + hidden_units)
    stacked = jnp.stack([pad_rows(operand) for operand in operands])[:, None]
    deltas = [0]
    bit = planes // 2
    while bit >= 1:
        stacked = jnp.concatenate([stacked, swap(stacked, "fsdp", bit)], axis=1)
        deltas = deltas + [delta ^ bit for delta in deltas]
        bit //= 2
    stacked = stacked.reshape(4, planes * tokens, model_width)
    order = line_order(line)
    ups, downs = line_slots(line, order)
    pieces = 3
    piece = shard_rows // pieces
    terms = []
    for slot in range(line):
        there = jnp.asarray(order[:, slot])[here]
        parts = []
        for delta in deltas:
            start = ((plane ^ delta) * line + there) * shard_rows
            part = lax.dynamic_slice_in_dim(columns, start, shard_rows, axis=1)
            parts.append(part if delta == 0 else swap(part, "fsdp", delta))
        factors = jnp.concatenate(parts, axis=0)
        first_row = (plane * line + there) * shard_rows
        made = []
        for index in range(pieces):
            row = first_row + index * piece
            which = sum((row >= edge).astype(jnp.int32) for edge in edges)
            made.append(
                contract_first(
                    factors[:, index * piece : (index + 1) * piece],
                    lax.dynamic_index_in_dim(stacked, which, 0, keepdims=False),
                )
            )
        terms.append(made)
    zero = jnp.zeros((piece, model_width), jnp.bfloat16)
    from_below = [zero] * pieces
    from_above = [zero] * pieces
    for step in range(line - 1):
        for index in range(pieces):
            made = [terms[slot][index] for slot in range(line)]
            up = (choose(made, ups[step], here) + from_below[index].astype(jnp.float32)).astype(
                jnp.bfloat16
            )
            down = (choose(made, downs[step], here) + from_above[index].astype(jnp.float32)).astype(
                jnp.bfloat16
            )
            from_below[index] = lax.ppermute(up, "dp", [(p, p + 1) for p in range(step + 1)])
            from_above[index] = lax.ppermute(
                down, "dp", [(line - 1 - p, line - 2 - p) for p in range(step + 1)]
            )
    return jnp.concatenate(
        [
            terms[line - 1][index]
            + from_below[index].astype(jnp.float32)
            + from_above[index].astype(jnp.float32)
            for index in range(pieces)
        ],
        axis=0,
    )


def adamw(param, grad, first, second, step_count, rate, decay):
    first = BETA_ONE * first + (1.0 - BETA_ONE) * grad
    second = BETA_TWO * second + (1.0 - BETA_TWO) * grad * grad
    fixed_one = 1.0 - BETA_ONE**step_count
    fixed_two = 1.0 - BETA_TWO**step_count
    direction = first / fixed_one / (jnp.sqrt(second / fixed_two) + EPS_ADAM)
    return (param - rate * (direction + decay * param), first, second)


def vector_rates():
    return jnp.array([[0.1], [0.1], [0.02]], dtype=jnp.float32)


def on_device(
    tokens,
    cotangent,
    lengths,
    selected,
    weights,
    vectors,
    first_moment,
    second_moment,
    vec_first,
    vec_second,
    outer_moment,
    smoothed_matrix_mean,
    vec_outer,
    vec_average,
):
    master = weights
    vec_now = vectors
    first_now = first_moment[0]
    second_now = second_moment[0]
    vfirst_now = vec_first[0]
    vsecond_now = vec_second[0]
    model_width = tokens.shape[2]
    forward_steps = []
    backward_steps = []
    for inner_step in range(INNER):
        tokens_now = tokens[inner_step]
        cot_now = cotangent[inner_step]
        seq_lengths = lengths[inner_step, 0]
        picked = selected[inner_step, 0]
        shard_low = master.astype(jnp.bfloat16)
        gathered = lax.all_gather(shard_low, ("fsdp", "dp"), axis=0, tiled=True)
        saved = forward_pass(gathered, vec_now, tokens_now, seq_lengths, picked)
        forward_steps.append(tokens_now.at[picked].set(saved["out_rows"].astype(jnp.bfloat16)))
        d_rows, grad_vec, columns, operands = backward_pass(
            gathered, vec_now, saved, cot_now, picked
        )
        backward_steps.append(cot_now.at[picked].set(d_rows.astype(jnp.bfloat16)))
        grad_shard = gradient_share(columns, operands, weights.shape[0], model_width)
        grad_vec = sum_over(grad_vec, ("fsdp", "dp"))
        step_count = STEP + inner_step
        master, first_now, second_now = adamw(
            master, grad_shard, first_now, second_now, step_count, INNER_RATE, DECAY_RATE
        )
        vec_now, vfirst_now, vsecond_now = adamw(
            vec_now, grad_vec, vfirst_now, vsecond_now, step_count, vector_rates(), 0.0
        )
    groups = lax.axis_size("grp")
    delta = weights - master
    vector_change = vectors - vec_now
    col_width = weights.shape[1] // groups
    col_start = lax.axis_index("grp") * col_width
    here = lax.axis_index("grp")
    diff_share = lax.dynamic_slice_in_dim(delta, col_start, col_width, 1)
    for step in range(1, groups):
        there = lax.rem(here + step, groups)
        part = lax.dynamic_slice_in_dim(delta, there * col_width, col_width, 1)
        part = lax.ppermute(
            part.astype(jnp.bfloat16), "grp", [(i, (i + step) % groups) for i in range(groups)]
        )
        diff_share = diff_share + part.astype(jnp.float32)
    diff_share = diff_share / groups
    vec_diff = sum_over(vector_change, ("grp",)) / groups
    moment_share = OUTER_MOMENTUM * outer_moment + diff_share
    base_share = lax.dynamic_slice_in_dim(weights, col_start, col_width, 1)
    new_share = base_share - OUTER_RATE * (diff_share + OUTER_MOMENTUM * moment_share)
    low_share = new_share.astype(jnp.bfloat16)
    weights_low = jnp.zeros(weights.shape, jnp.bfloat16)
    weights_low = lax.dynamic_update_slice_in_dim(weights_low, low_share, col_start, 1)
    for step in range(1, groups):
        there = lax.rem(here + groups - step, groups)
        part = lax.ppermute(low_share, "grp", [(i, (i + step) % groups) for i in range(groups)])
        weights_low = lax.dynamic_update_slice_in_dim(weights_low, part, there * col_width, 1)
    weights_new = weights_low.astype(jnp.float32)
    average_new = AVERAGE_KEEP * smoothed_matrix_mean + (1.0 - AVERAGE_KEEP) * new_share
    vec_moment = OUTER_MOMENTUM * vec_outer + vec_diff
    vectors_new = vectors - OUTER_RATE * (vec_diff + OUTER_MOMENTUM * vec_moment)
    vec_average_new = AVERAGE_KEEP * vec_average + (1.0 - AVERAGE_KEEP) * vectors_new
    return (
        jnp.stack(forward_steps),
        jnp.stack(backward_steps),
        weights_new,
        weights_low,
        first_now[None],
        second_now[None],
        moment_share,
        diff_share,
        average_new,
        vectors_new,
        vfirst_now[None],
        vsecond_now[None, :2],
        vsecond_now[None, 2],
        vec_moment,
        vec_average_new,
    )


def solution(mesh):
    placed = (
        P(None, ("grp", "fsdp", "dp"), None),
        P(None, ("grp", "fsdp", "dp"), None),
        P(None, ("grp", "fsdp", "dp"), None),
        P(None, ("grp", "fsdp", "dp"), None),
        P(("fsdp", "dp"), None),
        P(),
        P("grp", ("fsdp", "dp"), None),
        P("grp", ("fsdp", "dp"), None),
        P("grp", None, None),
        P("grp", None, None),
        P(("fsdp", "dp"), "grp"),
        P(("fsdp", "dp"), "grp"),
        P(),
        P(),
    )
    return jax.shard_map(
        on_device,
        mesh=mesh,
        in_specs=placed,
        out_specs=(
            P(None, ("grp", "fsdp", "dp"), None),
            P(None, ("grp", "fsdp", "dp"), None),
            P(("fsdp", "dp"), None),
            P(("fsdp", "dp"), None),
            P("grp", ("fsdp", "dp"), None),
            P("grp", ("fsdp", "dp"), None),
            P(("fsdp", "dp"), "grp"),
            P(("fsdp", "dp"), "grp"),
            P(("fsdp", "dp"), "grp"),
            P(),
            P("grp", None, None),
            P("grp", None, None),
            P("grp", None),
            P(),
            P(),
        ),
        check_vma=False,
    )
```

```python
import functools

import jax
import jax.numpy as jnp
import numpy as np
from jax import lax
from jax.experimental import pallas as pl
from jax.experimental.pallas import tpu as pltpu
from jax.sharding import PartitionSpec as P

HEAD = 64
INNER = 2
STEP = 5


EPS_NORM = 1e-06
EPS_ADAM = 1e-08
BETA_ONE = 0.9
BETA_TWO = 0.95
INNER_RATE = 0.03
DECAY_RATE = 0.1
OUTER_RATE = 0.7
OUTER_MOMENTUM = 0.9
AVERAGE_KEEP = 0.9
GELU_SCALE = float(np.sqrt(2.0 / np.pi))
GELU_CUBE = 0.044715
PIECES = 3
LINE_FLOPS = 10**10
NOWHERE = 1 << 20


def nt(left, right):
    return lax.dot_general(
        left, right, (((1,), (1,)), ((), ())), preferred_element_type=jnp.float32
    )


def nn(left, right):
    return lax.dot_general(
        left, right, (((1,), (0,)), ((), ())), preferred_element_type=jnp.float32
    )


def tn(left, right):
    return lax.dot_general(
        left, right, (((0,), (0,)), ((), ())), preferred_element_type=jnp.float32
    )


def weight_copies(weights, held, sems, sources, rows):
    return [
        pltpu.make_async_copy(
            weights.at[pl.ds(source * rows, rows)], held.at[pl.ds(target * rows, rows)], sems.at[target]
        )
        for target, source in enumerate(sources)
    ]


def two_heads(values):
    low = lax.broadcasted_iota(jnp.int32, values.shape, 1) < HEAD
    zero = jnp.zeros_like(values)
    return jnp.concatenate([jnp.where(low, values, zero), jnp.where(low, zero, values)], axis=0)


def one_block(values):
    rows = values.shape[0] // 2
    low = lax.broadcasted_iota(jnp.int32, (rows, values.shape[1]), 1) < HEAD
    return jnp.where(low, values[:rows], values[rows:])


def row_mean(values):
    return jnp.mean(values, axis=-1, keepdims=True)


def gelu_and_slope(pre):
    square = pre * pre
    tanh = jnp.tanh(GELU_SCALE * pre * (1.0 + GELU_CUBE * square))
    half = 0.5 * (1.0 + tanh)
    slope = half + 0.5 * pre * (1.0 - tanh * tanh) * (
        GELU_SCALE * (1.0 + 3.0 * GELU_CUBE * square)
    )
    return ((pre * half).astype(jnp.bfloat16), slope)


def gather_kernel(lengths, picked_ref, across_ref, tokens_hbm, cot_hbm, *refs, steps):
    both_refs, mask_refs = refs[:steps], refs[steps : 2 * steps]
    held, sems = refs[2 * steps :]
    copies = [
        [
            pltpu.make_async_copy(source.at[step], held.at[step, at], sems.at[step, at])
            for at, source in enumerate((tokens_hbm, cot_hbm))
        ]
        for step in range(steps)
    ]
    for some in copies:
        for copy in some:
            copy.start()
    for step in range(steps):
        down, across = picked_ref[step], across_ref[step]
        segment_down, segment_across = jnp.zeros_like(down), jnp.zeros_like(across)
        end = jnp.int32(0)
        for slot in range(lengths.shape[1]):
            end = end + lengths[step, slot]
            segment_down += (down >= end).astype(jnp.int32)
            segment_across += (across >= end).astype(jnp.int32)
        allowed = (segment_down == segment_across) & (across <= down)
        allowed = allowed.astype(jnp.int32)
        mask_refs[step][...] = jnp.concatenate([allowed, allowed], axis=0)
        places = lax.broadcasted_iota(jnp.int32, (down.shape[0], held.shape[2]), 1)
        chosen = jnp.where(places == down, 1.0, 0.0).astype(jnp.bfloat16)
        for at in range(2):
            copies[step][at].wait()
            both_refs[step][at] = nn(chosen, held[step, at]).astype(jnp.bfloat16)


def scatter_kernel(across_ref, base_ref, rows_ref, out_ref):
    base = base_ref[0]
    across = across_ref[0]
    places = lax.broadcasted_iota(jnp.int32, (base.shape[0], across.shape[1]), 0)
    chosen = jnp.where(places == across, 1.0, 0.0)
    replaced = jnp.sum(chosen, axis=-1, keepdims=True) > 0.0
    rows = nn(chosen.astype(jnp.bfloat16), rows_ref[0]).astype(jnp.bfloat16)
    out_ref[0] = jnp.where(replaced, rows, base)


def attention_kernel(
    weights, info, needs, moves, both_ref, vec_ref, mask_ref, proj_ref, lse_ref, pair_ref, first_ref, held, sems
):
    rows_ref = both_ref.at[0]
    width = both_ref.shape[2]
    copies = weight_copies(weights, held, sems, range(4), width)
    for copy in copies:
        copy.start()
    xs = rows_ref[...].astype(jnp.float32)
    h1 = (xs * lax.rsqrt(row_mean(xs * xs) + EPS_NORM) * vec_ref[0:1, :]).astype(jnp.bfloat16)
    for index in range(3):
        copies[index].wait()
        proj_ref[:, index * width : (index + 1) * width] = nt(
            h1, held[pl.ds(index * width, width), :]
        ).astype(jnp.bfloat16)
    allowed = mask_ref[...] > 0
    lane = lax.broadcasted_iota(jnp.int32, lse_ref.shape, 1)
    lse = jnp.zeros(lse_ref.shape, jnp.float32)
    for pair in range(width // 128):
        at = pair * 128
        queries = two_heads(proj_ref[:, at : at + 128])
        keys = proj_ref[:, width + at : width + at + 128]
        values = proj_ref[:, 2 * width + at : 2 * width + at + 128]
        scores = jnp.where(allowed, nt(queries, keys) * HEAD ** (-0.5), -1e30)
        top = jnp.max(scores, axis=-1, keepdims=True)
        total = top + jnp.log(jnp.sum(jnp.exp(scores - top), axis=-1, keepdims=True))
        lse = jnp.where(lane == pair, total, lse)
        probs_low = jnp.exp(scores - total).astype(jnp.bfloat16)
        pair_ref[0, :, at : at + 128] = one_block(nn(probs_low, values)).astype(jnp.bfloat16)
    lse_ref[...] = lse
    copies[3].wait()
    first_sum = xs + nt(pair_ref[0], held[pl.ds(3 * width, width), :])
    first_ref[...] = first_sum
    inverse = lax.rsqrt(row_mean(first_sum * first_sum) + EPS_NORM)
    pair_ref[1] = (first_sum * inverse * vec_ref[1:2, :]).astype(jnp.bfloat16)


def feed_forward_kernel(
    weights,
    both_ref,
    vec_ref,
    first_ref,
    d_attn_ref,
    out_ref,
    base_ref,
    grad_ref,
    *refs,
    keep,
):
    held, sems = refs[-2:]
    rows_ref, cot_ref = both_ref.at[0], both_ref.at[1]
    width = both_ref.shape[2]
    hidden = (weights.shape[0] - 4 * width) // 2
    parts = hidden // width
    order = []
    for part in range(parts):
        order += [4 + part, 4 + parts + part]
    copies = weight_copies(weights, held, sems, order, width)
    for copy in copies:
        copy.start()

    def matrix(index):
        return held[pl.ds(index * width, width), :]

    xs = rows_ref[...].astype(jnp.float32)
    cot = cot_ref[...].astype(jnp.float32)
    gate = jax.nn.sigmoid(jnp.sum(xs * vec_ref[2:3, :], axis=-1, keepdims=True))
    first_sum = first_ref[...]
    inverse = lax.rsqrt(row_mean(first_sum * first_sum) + EPS_NORM)
    normed = first_sum * inverse
    h2 = (normed * vec_ref[1:2, :]).astype(jnp.bfloat16)
    d_branch = gate * cot
    d_down = d_branch.astype(jnp.bfloat16)
    branch = first_sum - xs
    d_h2 = jnp.zeros_like(branch)
    for part in range(parts):
        at = part * width
        copies[2 * part].wait()
        act, slope = gelu_and_slope(nt(h2, matrix(2 * part)))
        copies[2 * part + 1].wait()
        branch = branch + nn(act, matrix(2 * part + 1))
        d_pre = (nt(d_down, matrix(2 * part + 1)) * slope).astype(jnp.bfloat16)
        if keep:
            refs[0][:, at : at + width] = d_pre
            refs[0][:, at + hidden : at + hidden + width] = act
        d_h2 = d_h2 + nn(d_pre, matrix(2 * part))
    out_ref[...] = (xs + gate * branch).astype(jnp.bfloat16)
    d_logit = jnp.sum(cot * branch, axis=-1, keepdims=True) * gate * (1.0 - gate)
    grad_ref[0:1, :] = jnp.sum(d_h2 * normed, axis=0, keepdims=True)
    grad_ref[1:2, :] = jnp.sum(d_logit * xs, axis=0, keepdims=True)
    d_normed = d_h2 * vec_ref[1:2, :]
    d_first = inverse * (d_normed - normed * row_mean(d_normed * normed))
    d_attn_ref[...] = (d_branch + d_first).astype(jnp.bfloat16)
    base_ref[...] = cot + d_first + d_logit * vec_ref[2:3, :]


def attention_back_kernel(
    weights,
    d_attn_ref,
    proj_ref,
    lse_ref,
    mask_ref,
    both_ref,
    vec_ref,
    base_hbm,
    pair_hbm,
    got_hbm,
    late_ref,
    d_rows_ref,
    grad_ref,
    pairs_hbm,
    held,
    base_ref,
    sems,
    base_sem,
    pair_sems,
):
    rows_ref = both_ref.at[0]
    width = both_ref.shape[2]
    copies = weight_copies(weights, held, sems, [3, 0, 1, 2], width)
    for copy in copies:
        copy.start()
    base_copy = pltpu.make_async_copy(base_hbm, base_ref, base_sem)
    base_copy.start()
    pair_copies = [
        pltpu.make_async_copy(pair_hbm, pairs_hbm.at[0], pair_sems.at[0]),
        pltpu.make_async_copy(got_hbm.at[0], pairs_hbm.at[1], pair_sems.at[1]),
    ]
    for copy in pair_copies:
        copy.start()
    copies[0].wait()
    d_mixed = nn(d_attn_ref[...], held[pl.ds(0, width), :]).astype(jnp.bfloat16)
    allowed = mask_ref[...] > 0
    for pair in range(width // 128):
        at = pair * 128
        queries = two_heads(proj_ref[:, at : at + 128])
        keys = proj_ref[:, width + at : width + at + 128]
        values = proj_ref[:, 2 * width + at : 2 * width + at + 128]
        d_pair = two_heads(d_mixed[:, at : at + 128])
        scores = jnp.where(allowed, nt(queries, keys) * HEAD ** (-0.5), -1e30)
        probs = jnp.exp(scores - lse_ref[:, pair : pair + 1])
        probs_low = probs.astype(jnp.bfloat16)
        d_probs = nt(d_pair, values)
        d_scores = probs * (d_probs - jnp.sum(d_probs * probs, axis=-1, keepdims=True))
        d_scores = d_scores.astype(jnp.bfloat16)
        late_ref[:, at : at + 128] = (one_block(nn(d_scores, keys)) * HEAD ** (-0.5)).astype(
            jnp.bfloat16
        )
        late_ref[:, width + at : width + at + 128] = (
            tn(d_scores, queries) * HEAD ** (-0.5)
        ).astype(jnp.bfloat16)
        late_ref[:, 2 * width + at : 2 * width + at + 128] = tn(probs_low, d_pair).astype(
            jnp.bfloat16
        )
    xs = rows_ref[...].astype(jnp.float32)
    inverse = lax.rsqrt(row_mean(xs * xs) + EPS_NORM)
    normed = xs * inverse
    d_h1 = jnp.zeros(xs.shape, jnp.float32)
    for index in range(3):
        copies[1 + index].wait()
        d_h1 = d_h1 + nn(
            late_ref[:, index * width : (index + 1) * width], held[pl.ds((1 + index) * width, width), :]
        )
    grad_ref[...] = jnp.sum(d_h1 * normed, axis=0, keepdims=True)
    d_normed = d_h1 * vec_ref[0:1, :]
    base_copy.wait()
    d_rows_ref[...] = (
        base_ref[...] + inverse * (d_normed - normed * row_mean(d_normed * normed))
    ).astype(jnp.bfloat16)
    for copy in pair_copies:
        copy.wait()


def plane_copies(refs, target, sems, tokens):
    return [
        pltpu.make_async_copy(ref, target.at[pl.ds(at * tokens, tokens)], sems.at[at])
        for at, ref in enumerate(refs)
    ]


def pair_refs_of(refs, index):
    return [ref.at[at, index] for ref in refs for at in range(ref.shape[0])]


def feed_forward_products_kernel(info, needs, weights, d_down_ref, *refs):
    pair_refs = refs[:-7]
    out_ref, held, uppers, lowers, held_sems, upper_sems, lower_sems = refs[-7:]
    count, piece, _ = out_ref.shape
    sources, tokens, _ = d_down_ref.shape

    def row_copy(index, at, target, sems):
        start = pl.multiple_of(info[index, at], 16)
        return pltpu.make_async_copy(
            weights.at[pl.ds(start, piece)], target.at[index], sems.at[index]
        )

    def each_row_copy(index, act):
        @pl.when(info[index, 0] >= 2)
        def _():
            act(row_copy(index, 1, uppers, upper_sems))

        @pl.when(info[index, 0] == 2)
        def _():
            act(row_copy(index, 2, lowers, lower_sems))

    def each_held(act):
        @pl.when(needs[2] > 0)
        def _():
            copies = plane_copies(
                pair_refs_of(pair_refs, 1), held.at[0], held_sems.at[0], tokens
            ) + plane_copies(
                [d_down_ref.at[at] for at in range(sources)], held.at[1], held_sems.at[1], tokens
            )
            for copy in copies:
                act(copy)

    each_held(lambda copy: copy.start())

    @pl.loop(0, count)
    def _(index):
        each_row_copy(index, lambda copy: copy.start())

    each_held(lambda copy: copy.wait())

    @pl.loop(0, count)
    def _(index):
        each_row_copy(index, lambda copy: copy.wait())

        @pl.when(info[index, 0] == 2)
        def _():
            slope = gelu_and_slope(nt(held[0], uppers[index]))[1]
            d_pre = (nt(held[1], lowers[index]) * slope).astype(jnp.bfloat16)
            out_ref[index] = tn(d_pre, held[0]).astype(jnp.bfloat16)

        @pl.when(info[index, 0] == 3)
        def _():
            act = gelu_and_slope(nt(held[0], uppers[index]))[0]
            out_ref[index] = tn(act, held[1]).astype(jnp.bfloat16)


def attention_products_kernel(info, needs, h1_ref, *refs, sources):
    proj_refs, attn_refs = refs[:sources], refs[sources : 2 * sources]
    pair_refs = refs[2 * sources : -8]
    _, out_ref, held, factors, made, held_sems, factor_sems, out_sems = refs[-8:]
    count, piece, _ = made.shape
    tokens = h1_ref.shape[1]

    def factor_copies(index, parts):
        start = pl.multiple_of(info[index, 1], 128)
        return plane_copies(
            [part.at[:, pl.ds(start, piece)] for part in parts],
            factors.at[index],
            factor_sems.at[index],
            tokens,
        )

    def each_copy(index, act):
        for kind, parts in enumerate((proj_refs, attn_refs)):

            @pl.when(info[index, 0] == kind)
            def _(parts=parts):
                for copy in factor_copies(index, parts):
                    act(copy)

    def each_held(act):
        for kind in range(2):
            found = pair_refs_of(pair_refs, 0) if kind else [h1_ref.at[at] for at in range(sources)]

            @pl.when(needs[kind] > 0)
            def _(kind=kind, found=found):
                for copy in plane_copies(found, held.at[kind], held_sems.at[kind], tokens):
                    act(copy)

    def out_copy(index):
        return pltpu.make_async_copy(made.at[index], out_ref.at[index], out_sems.at[index])

    each_held(lambda copy: copy.start())

    @pl.loop(0, count)
    def _(index):
        each_copy(index, lambda copy: copy.start())

    each_held(lambda copy: copy.wait())

    @pl.loop(0, count)
    def _(index):
        each_copy(index, lambda copy: copy.wait())

        @pl.when(info[index, 0] < 2)
        def _():
            made[index] = tn(factors[index], held[info[index, 0]]).astype(jnp.bfloat16)
            out_copy(index).start()

    @pl.loop(0, count)
    def _(index):
        @pl.when(info[index, 0] < 2)
        def _():
            out_copy(index).wait()


def line_kernel(moves, below_ref, above_ref, terms_ref, up_ref, down_ref, held, sems, *, step, piece):
    pieces = terms_ref.shape[0] // (moves.shape[0] + 1)
    copies = [
        pltpu.make_async_copy(
            terms_ref.at[moves[step, way] * pieces + piece], held.at[way], sems.at[way]
        )
        for way in range(2)
    ]
    for copy in copies:
        copy.start()
    for way, (came, leaves) in enumerate(((below_ref, up_ref), (above_ref, down_ref))):
        copies[way].wait()
        leaves[...] = (held[way].astype(jnp.float32) + came[...].astype(jnp.float32)).astype(
            jnp.bfloat16
        )


def vmem(count):
    return [pl.BlockSpec(memory_space=pltpu.VMEM)] * count


def run_gather(lengths, picked, tokens_in, cot_in):
    steps, count = picked.shape
    _, places, width = tokens_in.shape
    tokens = count + -count % 16
    padded = jnp.pad(picked, ((0, 0), (0, tokens - count)), constant_values=NOWHERE)
    shape = jax.ShapeDtypeStruct
    made = pl.pallas_call(
        functools.partial(gather_kernel, steps=steps),
        in_specs=[pl.BlockSpec(memory_space=pltpu.SMEM)] + vmem(2) + anywhere(2),
        out_specs=vmem(2 * steps),
        out_shape=[shape((2, tokens, width), jnp.bfloat16)] * steps
        + [shape((2 * tokens, tokens), jnp.int32)] * steps,
        scratch_shapes=[
            pltpu.VMEM((steps, 2, places, width), jnp.bfloat16),
            pltpu.SemaphoreType.DMA((steps, 2)),
        ],
        compiler_params=pltpu.CompilerParams(vmem_limit_bytes=44 << 20),
        name="gather_rows",
    )(lengths, padded[:, :, None], padded[:, None, :], tokens_in, cot_in)
    return (made[:steps], made[steps:], padded[:, None, :])


def run_scatter(across, base, rows):
    steps, places, width = base.shape
    tokens = rows.shape[1]
    return pl.pallas_call(
        scatter_kernel,
        grid=(steps,),
        in_specs=[
            pl.BlockSpec((1, 1, tokens), lambda step: (step, 0, 0)),
            pl.BlockSpec((1, places, width), lambda step: (step, 0, 0)),
            pl.BlockSpec((1, tokens, width), lambda step: (step, 0, 0)),
        ],
        out_specs=pl.BlockSpec((1, places, width), lambda step: (step, 0, 0)),
        out_shape=jax.ShapeDtypeStruct(base.shape, base.dtype),
        compiler_params=pltpu.CompilerParams(vmem_limit_bytes=44 << 20),
        name="scatter_rows",
    )(across, base, rows)


def run_attention(gathered, info, needs, moves, both, vec_now, mask):
    _, tokens, width = both.shape
    shape = jax.ShapeDtypeStruct
    return pl.pallas_call(
        attention_kernel,
        in_specs=anywhere(1) + smem(3) + vmem(3),
        out_specs=vmem(4),
        out_shape=[
            shape((tokens, 3 * width), jnp.bfloat16),
            shape((2 * tokens, 128), jnp.float32),
            shape((2, tokens, width), jnp.bfloat16),
            shape((tokens, width), jnp.float32),
        ],
        scratch_shapes=[
            pltpu.VMEM((4 * width, width), jnp.bfloat16),
            pltpu.SemaphoreType.DMA((4,)),
        ],
        compiler_params=pltpu.CompilerParams(vmem_limit_bytes=44 << 20),
        cost_estimate=pl.CostEstimate(
            flops=8 * tokens * width * width, bytes_accessed=8 * width * width, transcendentals=0
        ),
        name="attention",
    )(gathered, info, needs, moves, both, vec_now, mask)


def run_feed_forward(gathered, both, vec_now, first_sum, keep):
    _, tokens, width = both.shape
    wide = gathered.shape[0]
    shape = jax.ShapeDtypeStruct
    kept = [shape((tokens, wide - 4 * width), jnp.bfloat16)] if keep else []
    return pl.pallas_call(
        functools.partial(feed_forward_kernel, keep=keep),
        in_specs=anywhere(1) + vmem(3),
        out_specs=vmem(4 + len(kept)),
        out_shape=[
            shape((tokens, width), jnp.bfloat16),
            shape((tokens, width), jnp.bfloat16),
            shape((tokens, width), jnp.float32),
            shape((2, width), jnp.float32),
        ]
        + kept,
        scratch_shapes=[
            pltpu.VMEM((wide - 4 * width, width), jnp.bfloat16),
            pltpu.SemaphoreType.DMA(((wide - 4 * width) // width,)),
        ],
        compiler_params=pltpu.CompilerParams(vmem_limit_bytes=44 << 20),
        cost_estimate=pl.CostEstimate(
            flops=8 * tokens * (wide - 4 * width) * width,
            bytes_accessed=2 * wide * width,
            transcendentals=0,
        ),
        name="feed_forward",
    )(gathered, both, vec_now, first_sum)


def smem(count):
    return [pl.BlockSpec(memory_space=pltpu.SMEM)] * count


def anywhere(count):
    return [pl.BlockSpec(memory_space=pl.ANY)] * count


def run_attention_back(gathered, d_attn_low, proj, lse, mask, both, vec_now, base, pair, got):
    _, tokens, width = both.shape
    shape = jax.ShapeDtypeStruct
    return pl.pallas_call(
        attention_back_kernel,
        in_specs=anywhere(1) + vmem(6) + anywhere(3),
        out_specs=vmem(3) + anywhere(1),
        out_shape=[
            shape((tokens, 3 * width), jnp.bfloat16),
            shape((tokens, width), jnp.bfloat16),
            shape((1, width), jnp.float32),
            shape((2,) + pair.shape, jnp.bfloat16),
        ],
        scratch_shapes=[
            pltpu.VMEM((4 * width, width), jnp.bfloat16),
            pltpu.VMEM((tokens, width), jnp.float32),
            pltpu.SemaphoreType.DMA((4,)),
            pltpu.SemaphoreType.DMA,
            pltpu.SemaphoreType.DMA((2,)),
        ],
        compiler_params=pltpu.CompilerParams(vmem_limit_bytes=44 << 20),
        cost_estimate=pl.CostEstimate(
            flops=16 * tokens * width * width, bytes_accessed=8 * width * width, transcendentals=0
        ),
        name="attention_back",
    )(gathered, d_attn_low, proj, lse, mask, both, vec_now, base, pair, got)


def run_line(moves, below, above, terms, step, piece):
    shape = jax.ShapeDtypeStruct(below.shape, jnp.bfloat16)
    return pl.pallas_call(
        functools.partial(line_kernel, step=step, piece=piece),
        in_specs=smem(1) + vmem(2) + anywhere(1),
        out_specs=vmem(2),
        out_shape=[shape, shape],
        scratch_shapes=[
            pltpu.VMEM((2,) + below.shape, jnp.bfloat16),
            pltpu.SemaphoreType.DMA((2,)),
        ],
        compiler_params=pltpu.CompilerParams(vmem_limit_bytes=16 << 20),
        cost_estimate=pl.CostEstimate(
            flops=LINE_FLOPS, bytes_accessed=6 * below.size * 2, transcendentals=0
        ),
        name="line",
    )(moves, below, above, terms)


def run_products(info, needs, gathered, proj_parts, attn_parts, plane_h1, plane_d_down, pairs, piece):
    count = info.shape[0]
    sources, tokens, width = plane_h1.shape
    shape = jax.ShapeDtypeStruct((count, piece, width), jnp.bfloat16)
    made = pl.pallas_call(
        feed_forward_products_kernel,
        in_specs=smem(2) + anywhere(2 + len(pairs)),
        out_specs=vmem(1)[0],
        out_shape=shape,
        scratch_shapes=[
            pltpu.VMEM((2, sources * tokens, width), jnp.bfloat16),
            pltpu.VMEM((count, piece, width), jnp.bfloat16),
            pltpu.VMEM((count, piece, width), jnp.bfloat16),
            pltpu.SemaphoreType.DMA((2, sources)),
            pltpu.SemaphoreType.DMA((count,)),
            pltpu.SemaphoreType.DMA((count,)),
        ],
        compiler_params=pltpu.CompilerParams(vmem_limit_bytes=44 << 20),
        cost_estimate=pl.CostEstimate(
            flops=6 * count * sources * tokens * piece * width,
            bytes_accessed=6 * count * piece * width,
            transcendentals=0,
        ),
        name="feed_forward_products",
    )(info, needs, gathered, plane_d_down, *pairs)
    operands = (info, needs, plane_h1, *proj_parts, *attn_parts, *pairs, made)
    return pl.pallas_call(
        functools.partial(attention_products_kernel, sources=sources),
        in_specs=smem(2) + anywhere(len(operands) - 2),
        out_specs=anywhere(1)[0],
        out_shape=shape,
        scratch_shapes=[
            pltpu.VMEM((2, sources * tokens, width), jnp.bfloat16),
            pltpu.VMEM((count, sources * tokens, piece), jnp.bfloat16),
            pltpu.VMEM((count, piece, width), jnp.bfloat16),
            pltpu.SemaphoreType.DMA((2, sources)),
            pltpu.SemaphoreType.DMA((count, sources)),
            pltpu.SemaphoreType.DMA((count,)),
        ],
        input_output_aliases={len(operands) - 1: 0},
        compiler_params=pltpu.CompilerParams(vmem_limit_bytes=44 << 20),
        cost_estimate=pl.CostEstimate(
            flops=2 * count * sources * tokens * piece * width,
            bytes_accessed=2 * count * piece * width,
            transcendentals=0,
        ),
        name="attention_products",
    )(*operands)


def pad_rows(rows):
    return jnp.pad(rows, ((0, -rows.shape[0] % 16), (0, 0)))


def swap(values, axis, delta):
    size = lax.axis_size(axis)
    return lax.ppermute(values, axis, [(i, i ^ delta) for i in range(size)])


def sum_over(values, axes):
    for axis in axes:
        delta = 1
        while delta < lax.axis_size(axis):
            values = values + swap(values, axis, delta)
            delta *= 2
    return values


def line_order(line):
    due = np.zeros((line, line), np.int32)
    for here in range(line):
        for there in range(line):
            if there > here:
                due[here, there] = line - 1 - there + here
            elif there < here:
                due[here, there] = there - here + line - 1
            else:
                due[here, there] = line
    return np.argsort(due, axis=1, kind="stable").astype(np.int32)


def line_slots(line, order):
    ups = np.zeros((line - 1, line), np.int32)
    downs = np.zeros((line - 1, line), np.int32)
    for step in range(line - 1):
        for here in range(line):
            if here <= step:
                ups[step, here] = list(order[here]).index(line - 1 - step + here)
            if line - 1 - here <= step:
                downs[step, here] = list(order[here]).index(step - (line - 1) + here)
    return ups, downs


def added(*parts):
    return sum(part.astype(jnp.float32) for part in parts)


def due_after(value, *marks):
    flag = sum(mark[(-1,) * mark.ndim].astype(jnp.float32) for mark in marks)
    return value + (flag != flag).astype(value.dtype)


def plane_order(planes):
    deltas = [0]
    bit = planes // 2
    while bit >= 1:
        deltas = deltas + [delta ^ bit for delta in deltas]
        bit //= 2
    return deltas


def plane_gather(values):
    values = values[None]
    bit = lax.axis_size("fsdp") // 2
    while bit >= 1:
        values = jnp.concatenate([values, swap(values, "fsdp", bit)], axis=0)
        bit //= 2
    return values


def plane_operands(plane_rows, vec_now):
    sel_rows = plane_rows[:, 0].astype(jnp.float32)
    cot_rows = plane_rows[:, 1].astype(jnp.float32)
    gate = jax.nn.sigmoid(jnp.sum(sel_rows * vec_now[2], axis=-1, keepdims=True))
    inverse = lax.rsqrt(row_mean(sel_rows * sel_rows) + EPS_NORM)
    h1 = (sel_rows * inverse * vec_now[0]).astype(jnp.bfloat16)
    return (h1, (gate * cot_rows).astype(jnp.bfloat16))


def send_window(values, start, block):
    planes = lax.axis_size("fsdp")
    plane = lax.axis_index("fsdp")
    span = min(block, values.shape[1])
    stop = start + values.shape[1]

    def first(target):
        return jnp.clip(target * block - start, 0, values.shape[1] - span)

    def window(target):
        if span == values.shape[1]:
            return values
        return lax.dynamic_slice_in_dim(values, first(target), span, axis=1)

    def goes(target):
        return target * block < stop and (target + 1) * block > start

    parts = [window(plane)]
    for delta in plane_order(planes)[1:]:
        pairs = [(i, i ^ delta) for i in range(planes) if goes(i ^ delta)]
        parts.append(lax.ppermute(window(plane ^ delta), "fsdp", pairs))
    return parts


def window_start(width, start, block):
    return start + jnp.clip(
        lax.axis_index("fsdp") * block - start, 0, width - min(block, width)
    )


def gradient_plan(shard_rows, model_width, columns):
    planes, line = lax.axis_size("fsdp"), lax.axis_size("dp")
    plane, here = lax.axis_index("fsdp"), lax.axis_index("dp")
    hidden_units = (columns - 4 * model_width) // 2
    edges = (3 * model_width, 4 * model_width, 4 * model_width + hidden_units)

    def kind_of(row):
        return sum((row >= edge).astype(jnp.int32) for edge in edges)

    block = line * shard_rows
    proj_start = window_start(3 * model_width, 0, block)
    attn_start = window_start(model_width, 3 * model_width, block)
    piece = shard_rows // PIECES
    theres = jnp.asarray(line_order(line))[here]
    rows = (plane * line + theres)[:, None] * shard_rows + jnp.arange(PIECES) * piece
    rows = rows.reshape(-1)
    kinds = kind_of(rows)
    at = jnp.select(
        [kinds == 0, kinds == 1, kinds == 2],
        [rows - proj_start, rows - attn_start, rows],
        rows - hidden_units,
    )
    info = jnp.stack([kinds, at, jnp.minimum(rows + hidden_units, columns - piece)], axis=1)
    low, high = kind_of(plane * line * shard_rows), kind_of((plane + 1) * line * shard_rows - 1)
    ff = (high >= 2).astype(jnp.int32)
    has_proj = (low == 0).astype(jnp.int32)
    has_attn = ((low <= 1) & (high >= 1)).astype(jnp.int32)
    moves = jnp.asarray(np.stack(line_slots(line, line_order(line)), axis=-1))[:, here]
    return (info.astype(jnp.int32), jnp.stack([has_proj, has_attn, ff, ff]), moves)


def in_planes(shard_rows):
    return (shard_rows // PIECES) % 128 == 0


def gradient_whole(columns, operands):
    hidden_units = columns[2].shape[1] // 2
    factors = (*columns[:2], columns[2][:, :hidden_units], columns[2][:, hidden_units:])
    products = [tn(factor, operand) for factor, operand in zip(factors, operands)]
    low = jnp.concatenate(products, axis=0).astype(jnp.bfloat16)
    share = lax.psum_scatter(low, ("fsdp", "dp"), scatter_dimension=0, tiled=True)
    return share.astype(jnp.float32)


def plane_terms(
    gathered, late, d_attn_low, pairs, plane_h1, plane_d_down, info, needs, shard_rows
):
    planes, line = lax.axis_size("fsdp"), lax.axis_size("dp")
    block = line * shard_rows
    attn_parts = send_window(d_attn_low, late.shape[1], block)
    pairs = [pairs]
    bit = planes // 4
    while bit >= 1:
        pairs.append(swap(jnp.concatenate(pairs, axis=0), "fsdp", bit))
        bit //= 2
    proj_parts = send_window(late, 0, block)
    return run_products(
        info,
        needs,
        gathered,
        proj_parts,
        attn_parts,
        plane_h1,
        plane_d_down,
        pairs,
        shard_rows // PIECES,
    )


def gradient_share(terms, moves):
    line = lax.axis_size("dp")
    below, above = [None] * PIECES, [None] * PIECES
    for step in range(line - 1):
        for index in range(PIECES):
            if step == 0:
                up = down = terms[index]
            else:
                up, down = run_line(moves, below[index], above[index], terms, step, index)
            below[index] = lax.ppermute(up, "dp", [(p, p + 1) for p in range(step + 1)])
            above[index] = lax.ppermute(
                down, "dp", [(line - 1 - p, line - 2 - p) for p in range(step + 1)]
            )
    own = (line - 1) * PIECES
    sums = [added(terms[own + index], below[index], above[index]) for index in range(PIECES)]
    return jnp.concatenate(sums, axis=0)


def adamw(param, grad, first, second, step_count, rate, decay):
    first = BETA_ONE * first + (1.0 - BETA_ONE) * grad
    second = BETA_TWO * second + (1.0 - BETA_TWO) * grad * grad
    fixed_one = 1.0 - BETA_ONE**step_count
    fixed_two = 1.0 - BETA_TWO**step_count
    direction = first / fixed_one / (jnp.sqrt(second / fixed_two) + EPS_ADAM)
    return (param - rate * (direction + decay * param), first, second)


def vector_rates():
    return jnp.array([[0.1], [0.1], [0.02]], dtype=jnp.float32)


def on_device(
    tokens,
    cotangent,
    lengths,
    selected,
    weights,
    vectors,
    first_moment,
    second_moment,
    vec_first,
    vec_second,
    outer_moment,
    smoothed_matrix_mean,
    vec_outer,
    vec_average,
):
    master = weights
    vec_now = vectors
    first_now = first_moment[0]
    second_now = second_moment[0]
    vfirst_now = vec_first[0]
    vsecond_now = vec_second[0]
    model_width = tokens.shape[2]
    forward_steps = []
    backward_steps = []
    planes, line = lax.axis_size("fsdp"), lax.axis_size("dp")
    shard_rows = weights.shape[0]
    info, needs, moves = gradient_plan(shard_rows, model_width, weights.shape[0] * planes * line)
    boths, masks, across = run_gather(lengths[:, 0], selected[:, 0], tokens, cotangent)
    for inner_step in range(INNER):
        both, mask = boths[inner_step], masks[inner_step]
        plane_rows = plane_gather(both)
        shard_low = master.astype(jnp.bfloat16)
        gathered = lax.all_gather(shard_low, ("fsdp", "dp"), axis=0, tiled=True)
        plane_h1, plane_d_down = plane_operands(plane_rows, vec_now)
        proj, lse, pair, first_sum = run_attention(gathered, info, needs, moves, both, vec_now, mask)
        split = in_planes(shard_rows)
        d_attn_low, out_rows, base, grad_two, *kept = run_feed_forward(
            gathered, both, vec_now, first_sum, not split
        )
        got = swap(pair[None], "fsdp", planes // 2)
        late, d_rows, grad_one, pairs = run_attention_back(
            gathered, d_attn_low, proj, lse, mask, both, vec_now, base, pair, got
        )
        grad_vec = jnp.concatenate([grad_one, grad_two], axis=0)
        forward_steps.append(out_rows)
        backward_steps.append(d_rows)
        if split:
            terms = plane_terms(
                gathered, late, d_attn_low, pairs, plane_h1, plane_d_down, info, needs, shard_rows
            )
            grad_shard = gradient_share(terms, moves)
        else:
            grad_shard = gradient_whole(
                (late, d_attn_low, *kept), (plane_h1[0], pair[0], pair[1], plane_d_down[0])
            )
        grad_vec = sum_over(due_after(grad_vec, grad_shard), ("fsdp", "dp"))
        step_count = STEP + inner_step
        master, first_now, second_now = adamw(
            master, grad_shard, first_now, second_now, step_count, INNER_RATE, DECAY_RATE
        )
        vec_now, vfirst_now, vsecond_now = adamw(
            vec_now, grad_vec, vfirst_now, vsecond_now, step_count, vector_rates(), 0.0
        )
    groups = lax.axis_size("grp")
    delta = weights - master
    vector_change = vectors - vec_now
    col_width = weights.shape[1] // groups
    col_start = lax.axis_index("grp") * col_width
    here = lax.axis_index("grp")
    diff_share = lax.dynamic_slice_in_dim(delta, col_start, col_width, 1)
    for step in range(1, groups):
        there = lax.rem(here + step, groups)
        part = lax.dynamic_slice_in_dim(delta, there * col_width, col_width, 1)
        part = lax.ppermute(
            part.astype(jnp.bfloat16), "grp", [(i, (i + step) % groups) for i in range(groups)]
        )
        diff_share = diff_share + part.astype(jnp.float32)
    diff_share = diff_share / groups
    vec_diff = sum_over(vector_change, ("grp",)) / groups
    moment_share = OUTER_MOMENTUM * outer_moment + diff_share
    base_share = lax.dynamic_slice_in_dim(weights, col_start, col_width, 1)
    new_share = base_share - OUTER_RATE * (diff_share + OUTER_MOMENTUM * moment_share)
    low_share = new_share.astype(jnp.bfloat16)
    weights_low = jnp.zeros(weights.shape, jnp.bfloat16)
    weights_low = lax.dynamic_update_slice_in_dim(weights_low, low_share, col_start, 1)
    for step in range(1, groups):
        there = lax.rem(here + groups - step, groups)
        part = lax.ppermute(low_share, "grp", [(i, (i + step) % groups) for i in range(groups)])
        weights_low = lax.dynamic_update_slice_in_dim(weights_low, part, there * col_width, 1)
    weights_new = weights_low.astype(jnp.float32)
    average_new = AVERAGE_KEEP * smoothed_matrix_mean + (1.0 - AVERAGE_KEEP) * new_share
    vec_moment = OUTER_MOMENTUM * vec_outer + vec_diff
    vectors_new = vectors - OUTER_RATE * (vec_diff + OUTER_MOMENTUM * vec_moment)
    vec_average_new = AVERAGE_KEEP * vec_average + (1.0 - AVERAGE_KEEP) * vectors_new
    return (
        run_scatter(across, tokens, jnp.stack(forward_steps)),
        run_scatter(across, cotangent, jnp.stack(backward_steps)),
        weights_new,
        weights_low,
        first_now[None],
        second_now[None],
        moment_share,
        diff_share,
        average_new,
        vectors_new,
        vfirst_now[None],
        vsecond_now[None, :2],
        vsecond_now[None, 2],
        vec_moment,
        vec_average_new,
    )


def solution(mesh):
    placed = (
        P(None, ("grp", "fsdp", "dp"), None),
        P(None, ("grp", "fsdp", "dp"), None),
        P(None, ("grp", "fsdp", "dp"), None),
        P(None, ("grp", "fsdp", "dp"), None),
        P(("fsdp", "dp"), None),
        P(),
        P("grp", ("fsdp", "dp"), None),
        P("grp", ("fsdp", "dp"), None),
        P("grp", None, None),
        P("grp", None, None),
        P(("fsdp", "dp"), "grp"),
        P(("fsdp", "dp"), "grp"),
        P(),
        P(),
    )
    return jax.shard_map(
        on_device,
        mesh=mesh,
        in_specs=placed,
        out_specs=(
            P(None, ("grp", "fsdp", "dp"), None),
            P(None, ("grp", "fsdp", "dp"), None),
            P(("fsdp", "dp"), None),
            P(("fsdp", "dp"), None),
            P("grp", ("fsdp", "dp"), None),
            P("grp", ("fsdp", "dp"), None),
            P(("fsdp", "dp"), "grp"),
            P(("fsdp", "dp"), "grp"),
            P(("fsdp", "dp"), "grp"),
            P(),
            P("grp", None, None),
            P("grp", None, None),
            P("grp", None),
            P(),
            P(),
        ),
        check_vma=False,
    )
```

```python
import functools
import math

import jax
import jax.numpy as jnp
import numpy as np
from jax import lax
from jax.experimental import pallas as pl
from jax.experimental.pallas import tpu as pltpu
from jax.sharding import PartitionSpec as P

HEAD = 64
INNER = 2
STEP = 5


EPS_NORM = 1e-06
EPS_ADAM = 1e-08
BETA_ONE = 0.9
BETA_TWO = 0.95
INNER_RATE = 0.03
DECAY_RATE = 0.1
OUTER_RATE = 0.7
OUTER_MOMENTUM = 0.9
AVERAGE_KEEP = 0.9
GELU_SCALE = float(np.sqrt(2.0 / np.pi))
GELU_CUBE = 0.044715
PIECES = 3
LINE_FLOPS = 10**10
SMALL_COST = pl.CostEstimate(flops=10**6, bytes_accessed=10**5, transcendentals=0)
NOWHERE = 1 << 20


def nt(left, right):
    return lax.dot_general(
        left, right, (((1,), (1,)), ((), ())), preferred_element_type=jnp.float32
    )


def nn(left, right):
    return lax.dot_general(
        left, right, (((1,), (0,)), ((), ())), preferred_element_type=jnp.float32
    )


def tn(left, right):
    return lax.dot_general(
        left, right, (((0,), (0,)), ((), ())), preferred_element_type=jnp.float32
    )


def gathered_row(row, order):
    planes, line, shard_rows = order
    shard = row // shard_rows
    return ((shard % line) * planes + shard // line) * shard_rows + row % shard_rows


class WeightCopy:
    def __init__(self, weights, held, sem, source, target, rows, order):
        unit = math.gcd(order[2], rows)
        self.parts = [
            pltpu.make_async_copy(
                weights.at[pl.ds(gathered_row(source * rows + at, order), unit)],
                held.at[pl.ds(target * rows + at, unit)],
                sem,
            )
            for at in range(0, rows, unit)
        ]
        self.whole = pltpu.make_async_copy(
            weights.at[pl.ds(0, rows)], held.at[pl.ds(target * rows, rows)], sem
        )

    def start(self):
        for part in self.parts:
            part.start()

    def wait(self):
        self.whole.wait()


def weight_copies(weights, held, sems, sources, rows, order):
    return [
        WeightCopy(weights, held, sems.at[target], source, target, rows, order)
        for target, source in enumerate(sources)
    ]


def two_heads(values):
    low = lax.broadcasted_iota(jnp.int32, values.shape, 1) < HEAD
    zero = jnp.zeros_like(values)
    return jnp.concatenate([jnp.where(low, values, zero), jnp.where(low, zero, values)], axis=0)


def one_block(values):
    rows = values.shape[0] // 2
    low = lax.broadcasted_iota(jnp.int32, (rows, values.shape[1]), 1) < HEAD
    return jnp.where(low, values[:rows], values[rows:])


def row_mean(values):
    return jnp.mean(values, axis=-1, keepdims=True)


def gelu_and_slope(pre):
    square = pre * pre
    tanh = jnp.tanh(GELU_SCALE * pre * (1.0 + GELU_CUBE * square))
    half = 0.5 * (1.0 + tanh)
    slope = half + 0.5 * pre * (1.0 - tanh * tanh) * (
        GELU_SCALE * (1.0 + 3.0 * GELU_CUBE * square)
    )
    return ((pre * half).astype(jnp.bfloat16), slope)


def gather_kernel(lengths, picked_ref, across_ref, tokens_hbm, cot_hbm, *refs, steps):
    both_refs, mask_refs = refs[:steps], refs[steps : 2 * steps]
    held, sems = refs[2 * steps :]
    copies = [
        [
            pltpu.make_async_copy(source.at[step], held.at[step, at], sems.at[step, at])
            for at, source in enumerate((tokens_hbm, cot_hbm))
        ]
        for step in range(steps)
    ]
    for some in copies:
        for copy in some:
            copy.start()
    for step in range(steps):
        down, across = picked_ref[step], across_ref[step]
        segment_down, segment_across = jnp.zeros_like(down), jnp.zeros_like(across)
        end = jnp.int32(0)
        for slot in range(lengths.shape[1]):
            end = end + lengths[step, slot]
            segment_down += (down >= end).astype(jnp.int32)
            segment_across += (across >= end).astype(jnp.int32)
        allowed = (segment_down == segment_across) & (across <= down)
        allowed = allowed.astype(jnp.int32)
        mask_refs[step][...] = jnp.concatenate([allowed, allowed], axis=0)
        places = lax.broadcasted_iota(jnp.int32, (down.shape[0], held.shape[2]), 1)
        chosen = jnp.where(places == down, 1.0, 0.0).astype(jnp.bfloat16)
        for at in range(2):
            copies[step][at].wait()
            both_refs[step][at] = nn(chosen, held[step, at]).astype(jnp.bfloat16)


def scatter_kernel(across_ref, base_ref, rows_ref, *refs):
    out_ref = refs[-1]
    base = base_ref[0]
    across = across_ref[0]
    places = lax.broadcasted_iota(jnp.int32, (base.shape[0], across.shape[1]), 0)
    chosen = jnp.where(places == across, 1.0, 0.0)
    replaced = jnp.sum(chosen, axis=-1, keepdims=True) > 0.0
    rows = nn(chosen.astype(jnp.bfloat16), rows_ref[...]).astype(jnp.bfloat16)
    out_ref[0] = jnp.where(replaced, rows, base)


def attention_kernel(
    weights, info, needs, moves, starts, rows, both_ref, vec_ref, mask_ref, *refs, order, extra
):
    proj_ref, lse_ref, pair_ref, first_ref, held, sems = refs[extra:]
    rows_ref = both_ref.at[0]
    width = both_ref.shape[2]
    copies = weight_copies(weights, held, sems, range(4), width, order)
    for copy in copies:
        copy.start()
    xs = rows_ref[...].astype(jnp.float32)
    h1 = (xs * lax.rsqrt(row_mean(xs * xs) + EPS_NORM) * vec_ref[0:1, :]).astype(jnp.bfloat16)
    for index in range(3):
        copies[index].wait()
        proj_ref[:, index * width : (index + 1) * width] = nt(
            h1, held[pl.ds(index * width, width), :]
        ).astype(jnp.bfloat16)
    allowed = mask_ref[...] > 0
    lane = lax.broadcasted_iota(jnp.int32, lse_ref.shape, 1)
    lse = jnp.zeros(lse_ref.shape, jnp.float32)
    for pair in range(width // 128):
        at = pair * 128
        queries = two_heads(proj_ref[:, at : at + 128])
        keys = proj_ref[:, width + at : width + at + 128]
        values = proj_ref[:, 2 * width + at : 2 * width + at + 128]
        scores = jnp.where(allowed, nt(queries, keys) * HEAD ** (-0.5), -1e30)
        top = jnp.max(scores, axis=-1, keepdims=True)
        total = top + jnp.log(jnp.sum(jnp.exp(scores - top), axis=-1, keepdims=True))
        lse = jnp.where(lane == pair, total, lse)
        probs_low = jnp.exp(scores - total).astype(jnp.bfloat16)
        pair_ref[0, :, at : at + 128] = one_block(nn(probs_low, values)).astype(jnp.bfloat16)
    lse_ref[...] = lse
    copies[3].wait()
    first_sum = xs + nt(pair_ref[0], held[pl.ds(3 * width, width), :])
    first_ref[...] = first_sum
    inverse = lax.rsqrt(row_mean(first_sum * first_sum) + EPS_NORM)
    pair_ref[1] = (first_sum * inverse * vec_ref[1:2, :]).astype(jnp.bfloat16)


def feed_forward_kernel(
    weights,
    both_ref,
    vec_ref,
    first_ref,
    d_attn_ref,
    out_ref,
    base_ref,
    grad_ref,
    *refs,
    keep,
    order,
):
    held, sems = refs[-2:]
    rows_ref, cot_ref = both_ref.at[0], both_ref.at[1]
    width = both_ref.shape[2]
    hidden = (weights.shape[0] - 4 * width) // 2
    parts = hidden // width
    matrices = []
    for part in range(parts):
        matrices += [4 + part, 4 + parts + part]
    copies = weight_copies(weights, held, sems, matrices, width, order)
    for copy in copies:
        copy.start()

    def matrix(index):
        return held[pl.ds(index * width, width), :]

    xs = rows_ref[...].astype(jnp.float32)
    cot = cot_ref[...].astype(jnp.float32)
    gate = jax.nn.sigmoid(jnp.sum(xs * vec_ref[2:3, :], axis=-1, keepdims=True))
    first_sum = first_ref[...]
    inverse = lax.rsqrt(row_mean(first_sum * first_sum) + EPS_NORM)
    normed = first_sum * inverse
    h2 = (normed * vec_ref[1:2, :]).astype(jnp.bfloat16)
    d_branch = gate * cot
    d_down = d_branch.astype(jnp.bfloat16)
    branch = first_sum - xs
    d_h2 = jnp.zeros_like(branch)
    for part in range(parts):
        at = part * width
        copies[2 * part].wait()
        act, slope = gelu_and_slope(nt(h2, matrix(2 * part)))
        copies[2 * part + 1].wait()
        branch = branch + nn(act, matrix(2 * part + 1))
        d_pre = (nt(d_down, matrix(2 * part + 1)) * slope).astype(jnp.bfloat16)
        if keep:
            refs[0][:, at : at + width] = d_pre
            refs[0][:, at + hidden : at + hidden + width] = act
        d_h2 = d_h2 + nn(d_pre, matrix(2 * part))
    out_ref[...] = (xs + gate * branch).astype(jnp.bfloat16)
    d_logit = jnp.sum(cot * branch, axis=-1, keepdims=True) * gate * (1.0 - gate)
    grad_ref[0:1, :] = jnp.sum(d_h2 * normed, axis=0, keepdims=True)
    grad_ref[1:2, :] = jnp.sum(d_logit * xs, axis=0, keepdims=True)
    d_normed = d_h2 * vec_ref[1:2, :]
    d_first = inverse * (d_normed - normed * row_mean(d_normed * normed))
    d_attn_ref[...] = (d_branch + d_first).astype(jnp.bfloat16)
    base_ref[...] = cot + d_first + d_logit * vec_ref[2:3, :]


def attention_back_kernel(
    weights,
    starts,
    d_attn_ref,
    proj_ref,
    lse_ref,
    mask_ref,
    pair_hbm,
    got_hbm,
    cuts_hbm,
    pairs_hbm,
    held,
    late_ref,
    weight_sems,
    pair_sems,
    cut_sems,
    *,
    order,
):
    width = held.shape[1]
    copies = weight_copies(weights, held, weight_sems, [3], width, order)
    pair_copies = [
        pltpu.make_async_copy(pair_hbm, pairs_hbm.at[0], pair_sems.at[0]),
        pltpu.make_async_copy(got_hbm.at[0], pairs_hbm.at[1], pair_sems.at[1]),
    ]
    for copy in copies + pair_copies:
        copy.start()
    copies[0].wait()
    d_mixed = nn(d_attn_ref[...], held[pl.ds(0, width), :]).astype(jnp.bfloat16)
    allowed = mask_ref[...] > 0
    for pair in range(width // 128):
        at = pair * 128
        queries = two_heads(proj_ref[:, at : at + 128])
        keys = proj_ref[:, width + at : width + at + 128]
        values = proj_ref[:, 2 * width + at : 2 * width + at + 128]
        d_pair = two_heads(d_mixed[:, at : at + 128])
        scores = jnp.where(allowed, nt(queries, keys) * HEAD ** (-0.5), -1e30)
        probs = jnp.exp(scores - lse_ref[:, pair : pair + 1])
        probs_low = probs.astype(jnp.bfloat16)
        d_probs = nt(d_pair, values)
        d_scores = probs * (d_probs - jnp.sum(d_probs * probs, axis=-1, keepdims=True))
        d_scores = d_scores.astype(jnp.bfloat16)
        late_ref[:, at : at + 128] = (one_block(nn(d_scores, keys)) * HEAD ** (-0.5)).astype(
            jnp.bfloat16
        )
        late_ref[:, width + at : width + at + 128] = (
            tn(d_scores, queries) * HEAD ** (-0.5)
        ).astype(jnp.bfloat16)
        late_ref[:, 2 * width + at : 2 * width + at + 128] = tn(probs_low, d_pair).astype(
            jnp.bfloat16
        )
    cuts = starts.shape[0]
    span = late_ref.shape[1] // cuts
    cut_copies = []
    for cut in range(cuts):
        start = pl.multiple_of(starts[cut], 128)
        cut_copies.append(
            pltpu.make_async_copy(
                late_ref.at[:, pl.ds(start, span)],
                cuts_hbm.at[:, pl.ds(cut * span, span)],
                cut_sems.at[cut],
            )
        )
    for copy in cut_copies:
        copy.start()
    for copy in cut_copies + pair_copies:
        copy.wait()


def input_back_kernel(
    weights, rows, cuts_ref, both_ref, vec_ref, base_ref, *refs, extra, order
):
    d_rows_ref, grad_ref, held, sems = refs[extra:]
    cuts, span, width = held.shape
    if order is None:
        copies = [
            pltpu.make_async_copy(
                weights.at[pl.ds(pl.multiple_of(rows[cut], 128), span)], held.at[cut], sems.at[cut]
            )
            for cut in range(cuts)
        ]
    else:
        copies = [
            WeightCopy(weights, held.at[cut], sems.at[cut], cut, 0, span, order)
            for cut in range(cuts)
        ]
    for copy in copies:
        copy.start()
    xs = both_ref[0].astype(jnp.float32)
    inverse = lax.rsqrt(row_mean(xs * xs) + EPS_NORM)
    normed = xs * inverse
    d_h1 = jnp.zeros(xs.shape, jnp.float32)
    for cut in range(cuts):
        copies[cut].wait()
        d_h1 = d_h1 + nn(cuts_ref[:, cut * span : (cut + 1) * span], held[cut])
    grad_ref[...] = jnp.sum(d_h1 * normed, axis=0, keepdims=True)
    d_normed = d_h1 * vec_ref[0:1, :]
    d_rows_ref[...] = (
        base_ref[...] + inverse * (d_normed - normed * row_mean(d_normed * normed))
    ).astype(jnp.bfloat16)


def plane_copies(refs, target, sems, tokens):
    return [
        pltpu.make_async_copy(ref, target.at[pl.ds(at * tokens, tokens)], sems.at[at])
        for at, ref in enumerate(refs)
    ]


def pair_refs_of(refs, index):
    return [ref.at[at, index] for ref in refs for at in range(ref.shape[0])]


def feed_forward_products_kernel(info, needs, weights, d_down_ref, *refs, extra):
    pair_refs = refs[: -7 - extra]
    out_ref, held, uppers, lowers, held_sems, upper_sems, lower_sems = refs[-7:]
    count, piece, _ = out_ref.shape
    sources, tokens, _ = d_down_ref.shape

    def row_copy(index, at, target, sems):
        start = pl.multiple_of(info[index, at], 16)
        return pltpu.make_async_copy(
            weights.at[pl.ds(start, piece)], target.at[index], sems.at[index]
        )

    def each_row_copy(index, act):
        @pl.when(info[index, 0] >= 2)
        def _():
            act(row_copy(index, 1, uppers, upper_sems))

        @pl.when(info[index, 0] == 2)
        def _():
            act(row_copy(index, 2, lowers, lower_sems))

    def each_held(act):
        @pl.when(needs[2] > 0)
        def _():
            copies = plane_copies(
                pair_refs_of(pair_refs, 1), held.at[0], held_sems.at[0], tokens
            ) + plane_copies(
                [d_down_ref.at[at] for at in range(sources)], held.at[1], held_sems.at[1], tokens
            )
            for copy in copies:
                act(copy)

    each_held(lambda copy: copy.start())

    @pl.loop(0, count)
    def _(index):
        each_row_copy(index, lambda copy: copy.start())

    each_held(lambda copy: copy.wait())

    @pl.loop(0, count)
    def _(index):
        each_row_copy(index, lambda copy: copy.wait())

        @pl.when(info[index, 0] == 2)
        def _():
            slope = gelu_and_slope(nt(uppers[index], held[0]))[1]
            d_pre = (nt(lowers[index], held[1]) * slope).astype(jnp.bfloat16)
            out_ref[index] = nn(d_pre, held[0]).astype(jnp.bfloat16)

        @pl.when(info[index, 0] == 3)
        def _():
            act = gelu_and_slope(nt(uppers[index], held[0]))[0]
            out_ref[index] = nn(act, held[1]).astype(jnp.bfloat16)


def attention_products_kernel(info, needs, h1_ref, *refs, sources, extra):
    proj_refs, attn_refs = refs[:sources], refs[sources : 2 * sources]
    pair_refs = refs[2 * sources : -9 - extra]
    out_ref, held, projs, attns, made, held_sems, factor_sems, out_sems = refs[-8:]
    count, piece, _ = made.shape
    tokens = h1_ref.shape[1]
    rights = ([h1_ref.at[at] for at in range(sources)], pair_refs_of(pair_refs, 0))

    def each_operand(act):
        for kind, (lefts, target) in enumerate(((proj_refs, projs), (attn_refs, attns))):

            @pl.when(needs[kind] > 0)
            def _(kind=kind, lefts=lefts, target=target):
                copies = plane_copies(rights[kind], held.at[kind], held_sems.at[kind], tokens)
                copies += plane_copies(lefts, target, factor_sems.at[kind], tokens)
                for copy in copies:
                    act(copy)

    def out_copy(index):
        return pltpu.make_async_copy(made.at[index], out_ref.at[index], out_sems.at[index])

    each_operand(lambda copy: copy.start())
    each_operand(lambda copy: copy.wait())
    for index in range(count):

        @pl.when(info[index, 0] == 0)
        def _(index=index):
            left = projs[:, index * piece : (index + 1) * piece]
            made[index] = tn(left, held[0]).astype(jnp.bfloat16)
            out_copy(index).start()

        @pl.when(info[index, 0] == 1)
        def _(index=index):
            left = attns[:, pl.ds(pl.multiple_of(info[index, 1], 128), piece)]
            made[index] = tn(left, held[1]).astype(jnp.bfloat16)
            out_copy(index).start()

    for index in range(count):

        @pl.when(info[index, 0] < 2)
        def _(index=index):
            out_copy(index).wait()


def line_kernel(moves, below_ref, above_ref, terms_ref, *refs, step, piece, passed):
    up_ref, down_ref = refs[-4 - passed : -2 - passed]
    held, sems = refs[-2:]
    for source, target in zip(refs[:passed], refs[-2 - passed : -2]):
        target[...] = source[...]

    def each_copy(way, act):
        source = terms_ref.at[moves[step, way] * PIECES + piece]
        act(pltpu.make_async_copy(source, held.at[way], sems.at[way]))

    for way in range(2):
        each_copy(way, lambda copy: copy.start())
    for way, (came, leaves) in enumerate(((below_ref, up_ref), (above_ref, down_ref))):
        each_copy(way, lambda copy: copy.wait())
        leaves[...] = (held[way].astype(jnp.float32) + came[...].astype(jnp.float32)).astype(
            jnp.bfloat16
        )


def update_kernel(place, below_ref, above_ref, *refs, piece, own, step_count, last, chained, extra):
    arrays = refs[: 5 if last else 4]
    results = refs[len(arrays) + chained + extra : len(arrays) + chained + extra + 4]
    held, term, made, low, in_sems, out_sems = refs[-6:]
    rows = below_ref.shape[0]
    blocks = in_sems.shape[0]
    block = rows // blocks
    loads, stores = [], []
    for index in range(blocks):
        here = pl.ds(index * block, block)
        there = pl.ds(piece * rows + index * block, block)
        sources = [arrays[0].at[own, here]] + [array.at[there] for array in arrays[1:]]
        targets = [term.at[here]] + [held.at[at, here] for at in range(len(arrays) - 1)]
        loads.append(
            [
                pltpu.make_async_copy(source, target, in_sems.at[index, at])
                for at, (source, target) in enumerate(zip(sources, targets))
            ]
        )
        outs = [(made.at[1, here], results[0]), (made.at[2, here], results[1])]
        if not last:
            outs += [(made.at[0, here], results[2]), (low.at[here], results[3])]
        stores.append(
            [
                pltpu.make_async_copy(source, target.at[there], out_sems.at[index, at])
                for at, (source, target) in enumerate(outs)
            ]
        )
    for copies in loads:
        for copy in copies:
            copy.start()
    fixed_one = 1.0 / (1.0 - BETA_ONE**step_count)
    fixed_two = 1.0 / (1.0 - BETA_TWO**step_count)
    for index in range(blocks):
        for copy in loads[index]:
            copy.wait()
        some = pl.ds(index * block, block)
        grad = (term[some, :].astype(jnp.float32) + below_ref[some, :].astype(jnp.float32)) + above_ref[
            some, :
        ].astype(jnp.float32)
        param = held[0, some, :]
        first = BETA_ONE * held[1, some, :] + (1.0 - BETA_ONE) * grad
        second = BETA_TWO * held[2, some, :] + (1.0 - BETA_TWO) * grad * grad
        direction = first * fixed_one / (jnp.sqrt(second * fixed_two) + EPS_ADAM)
        param = param - INNER_RATE * (direction + DECAY_RATE * param)
        made[1, some, :] = first
        made[2, some, :] = second
        if last:
            made[0, some, :] = held[3, some, :] - param
        else:
            made[0, some, :] = param
            low[some, :] = param.astype(jnp.bfloat16)
        for copy in stores[index]:
            copy.start()
    if last:
        own_ref, other_ref = results[2:]
        columns = own_ref.shape[1]
        groups = other_ref.shape[0] + 1
        for step in range(groups):
            start = pl.multiple_of(lax.rem(place[0] + step, groups) * columns, 128)
            if step == 0:
                own_ref[...] = made[0, :, pl.ds(start, columns)]
            else:
                other_ref[step - 1] = made[0, :, pl.ds(start, columns)].astype(jnp.bfloat16)
    for copies in stores:
        for copy in copies:
            copy.wait()


def outer_kernel(place, own_ref, *refs, piece, groups, chained, extra):
    got_refs = refs[: groups - 1]
    arrays = refs[groups - 1 : groups + 2]
    results = refs[groups + 2 + chained + extra : groups + 6 + chained + extra]
    held, made, in_sems, out_sems = refs[-4:]
    rows, columns = own_ref.shape
    at = pl.ds(piece * rows, rows)
    start = pl.multiple_of(place[0] * columns, 128)
    sources = [arrays[0].at[at, pl.ds(start, columns)], arrays[1].at[at], arrays[2].at[at]]
    copies = [
        pltpu.make_async_copy(source, held.at[index], in_sems.at[index])
        for index, source in enumerate(sources)
    ]
    for copy in copies:
        copy.start()
    for copy in copies:
        copy.wait()
    share = own_ref[...]
    for index in range(groups - 1):
        share = share + got_refs[index][...].astype(jnp.float32)
    share = share / groups
    moment = OUTER_MOMENTUM * held[1] + share
    new_share = held[0] - OUTER_RATE * (share + OUTER_MOMENTUM * moment)
    made[0] = moment
    made[1] = share
    made[2] = AVERAGE_KEEP * held[2] + (1.0 - AVERAGE_KEEP) * new_share
    results[3][...] = new_share.astype(jnp.bfloat16)
    copies = [
        pltpu.make_async_copy(made.at[index], results[index].at[at], out_sems.at[index])
        for index in range(3)
    ]
    for copy in copies:
        copy.start()
    for copy in copies:
        copy.wait()


def join_kernel(place, *refs, piece, groups, chained):
    parts = refs[:groups]
    wide_hbm, low_hbm = refs[groups + chained : groups + chained + 2]
    wide, sems = refs[-2:]
    rows, columns = parts[0].shape
    at = pl.ds(piece * rows, rows)
    copies = []
    for step in range(groups):
        start = pl.multiple_of(lax.rem(place[0] + groups - step, groups) * columns, 128)
        wide[step] = parts[step][...].astype(jnp.float32)
        target = (at, pl.ds(start, columns))
        copies.append(pltpu.make_async_copy(wide.at[step], wide_hbm.at[target], sems.at[0, step]))
        copies.append(pltpu.make_async_copy(parts[step], low_hbm.at[target], sems.at[1, step]))
    for copy in copies:
        copy.start()
    for copy in copies:
        copy.wait()


def vmem(count):
    return [pl.BlockSpec(memory_space=pltpu.VMEM)] * count


def run_gather(lengths, picked, tokens_in, cot_in):
    steps, count = picked.shape
    _, places, width = tokens_in.shape
    tokens = count + -count % 16
    padded = jnp.pad(picked, ((0, 0), (0, tokens - count)), constant_values=NOWHERE)
    shape = jax.ShapeDtypeStruct
    made = pl.pallas_call(
        functools.partial(gather_kernel, steps=steps),
        in_specs=[pl.BlockSpec(memory_space=pltpu.SMEM)] + vmem(2) + anywhere(2),
        out_specs=vmem(2 * steps),
        out_shape=[shape((2, tokens, width), jnp.bfloat16)] * steps
        + [shape((2 * tokens, tokens), jnp.int32)] * steps,
        scratch_shapes=[
            pltpu.VMEM((steps, 2, places, width), jnp.bfloat16),
            pltpu.SemaphoreType.DMA((steps, 2)),
        ],
        compiler_params=pltpu.CompilerParams(vmem_limit_bytes=44 << 20),
        name="gather_rows",
    )(lengths, padded[:, :, None], padded[:, None, :], tokens_in, cot_in)
    return (made[:steps], made[steps:], padded[:, None, :])


def run_scatter(across, base, rows, step, chain, known):
    _, places, width = base.shape
    tokens = rows.shape[0]
    here = pl.BlockSpec((1, places, width), lambda index: (step, 0, 0))
    return pl.pallas_call(
        scatter_kernel,
        grid=(1,),
        in_specs=[
            pl.BlockSpec((1, 1, tokens), lambda index: (step, 0, 0)),
            here,
            pl.BlockSpec((tokens, width), lambda index: (0, 0)),
        ]
        + anywhere(len(chain) + len(known)),
        out_specs=here,
        out_shape=jax.ShapeDtypeStruct(base.shape, base.dtype),
        input_output_aliases=chain_aliases(3, chain),
        compiler_params=pltpu.CompilerParams(vmem_limit_bytes=56 << 20),
        cost_estimate=SMALL_COST,
        name="scatter_rows",
    )(across, base, rows, *chain, *known)


def run_attention(order, gathered, plan, both, vec_now, mask, known):
    _, tokens, width = both.shape
    shape = jax.ShapeDtypeStruct
    return pl.pallas_call(
        functools.partial(attention_kernel, order=order, extra=len(known)),
        in_specs=anywhere(1) + smem(len(plan)) + vmem(3) + anywhere(len(known)),
        out_specs=vmem(4),
        out_shape=[
            shape((tokens, 3 * width), jnp.bfloat16),
            shape((2 * tokens, 128), jnp.float32),
            shape((2, tokens, width), jnp.bfloat16),
            shape((tokens, width), jnp.float32),
        ],
        scratch_shapes=[
            pltpu.VMEM((4 * width, width), jnp.bfloat16),
            pltpu.SemaphoreType.DMA((4,)),
        ],
        compiler_params=pltpu.CompilerParams(vmem_limit_bytes=44 << 20),
        cost_estimate=pl.CostEstimate(
            flops=8 * tokens * width * width, bytes_accessed=8 * width * width, transcendentals=0
        ),
        name="attention",
    )(gathered, *plan, both, vec_now, mask, *known)


def run_feed_forward(order, gathered, both, vec_now, first_sum, keep):
    _, tokens, width = both.shape
    wide = gathered.shape[0]
    shape = jax.ShapeDtypeStruct
    kept = [shape((tokens, wide - 4 * width), jnp.bfloat16)] if keep else []
    return pl.pallas_call(
        functools.partial(feed_forward_kernel, keep=keep, order=order),
        in_specs=anywhere(1) + vmem(3),
        out_specs=vmem(4 + len(kept)),
        out_shape=[
            shape((tokens, width), jnp.bfloat16),
            shape((tokens, width), jnp.bfloat16),
            shape((tokens, width), jnp.float32),
            shape((2, width), jnp.float32),
        ]
        + kept,
        scratch_shapes=[
            pltpu.VMEM((wide - 4 * width, width), jnp.bfloat16),
            pltpu.SemaphoreType.DMA(((wide - 4 * width) // width,)),
        ],
        compiler_params=pltpu.CompilerParams(vmem_limit_bytes=44 << 20),
        cost_estimate=pl.CostEstimate(
            flops=8 * tokens * (wide - 4 * width) * width,
            bytes_accessed=2 * wide * width,
            transcendentals=0,
        ),
        name="feed_forward",
    )(gathered, both, vec_now, first_sum)


def smem(count):
    return [pl.BlockSpec(memory_space=pltpu.SMEM)] * count


def anywhere(count):
    return [pl.BlockSpec(memory_space=pl.ANY)] * count


def run_attention_back(order, gathered, starts, d_attn_low, proj, lse, mask, pair, got):
    tokens, width = d_attn_low.shape
    cuts = starts.shape[0]
    shape = jax.ShapeDtypeStruct
    return pl.pallas_call(
        functools.partial(attention_back_kernel, order=order),
        in_specs=anywhere(1) + smem(1) + vmem(4) + anywhere(2),
        out_specs=anywhere(2),
        out_shape=[
            shape((tokens, 3 * width), jnp.bfloat16),
            shape((2,) + pair.shape, jnp.bfloat16),
        ],
        scratch_shapes=[
            pltpu.VMEM((width, width), jnp.bfloat16),
            pltpu.VMEM((tokens, 3 * width), jnp.bfloat16),
            pltpu.SemaphoreType.DMA((1,)),
            pltpu.SemaphoreType.DMA((2,)),
            pltpu.SemaphoreType.DMA((cuts,)),
        ],
        compiler_params=pltpu.CompilerParams(vmem_limit_bytes=44 << 20),
        cost_estimate=pl.CostEstimate(
            flops=10 * tokens * width * width, bytes_accessed=4 * width * width, transcendentals=0
        ),
        name="attention_back",
    )(gathered, starts, d_attn_low, proj, lse, mask, pair, got)


def run_input_back(order, gathered, rows, d_proj, both, vec_now, base, known):
    _, tokens, width = both.shape
    cuts = rows.shape[0]
    shape = jax.ShapeDtypeStruct
    return pl.pallas_call(
        functools.partial(
            input_back_kernel, extra=len(known), order=order
        ),
        in_specs=anywhere(1) + smem(1) + vmem(4) + anywhere(len(known)),
        out_specs=vmem(2),
        out_shape=[
            shape((tokens, width), jnp.bfloat16),
            shape((1, width), jnp.float32),
        ],
        scratch_shapes=[
            pltpu.VMEM((cuts, 3 * width // cuts, width), jnp.bfloat16),
            pltpu.SemaphoreType.DMA((cuts,)),
        ],
        compiler_params=pltpu.CompilerParams(vmem_limit_bytes=44 << 20),
        cost_estimate=SMALL_COST,
        name="input_back",
    )(gathered, rows, d_proj, both, vec_now, base, *known)


def run_line(moves, below, above, terms, step, piece, passed, known):
    shape = jax.ShapeDtypeStruct(below.shape, jnp.bfloat16)
    return pl.pallas_call(
        functools.partial(line_kernel, step=step, piece=piece, passed=len(passed)),
        in_specs=smem(1) + vmem(2) + anywhere(1) + vmem(len(passed)) + anywhere(len(known)),
        out_specs=vmem(2 + len(passed)),
        out_shape=[shape, shape]
        + [jax.ShapeDtypeStruct(values.shape, values.dtype) for values in passed],
        scratch_shapes=[
            pltpu.VMEM((2,) + below.shape, jnp.bfloat16),
            pltpu.SemaphoreType.DMA((2,)),
        ],
        compiler_params=pltpu.CompilerParams(vmem_limit_bytes=16 << 20),
        cost_estimate=pl.CostEstimate(
            flops=LINE_FLOPS, bytes_accessed=6 * below.size * 2, transcendentals=0
        ),
        name="line",
    )(moves, below, above, terms, *passed, *known)


def chain_aliases(first, chain):
    return {first + index: index for index in range(len(chain))}


def run_update(place, below, above, terms, states, piece, step_count, last, groups, chain, known):
    rows, width = below.shape
    own = terms.shape[0] - PIECES + piece
    shape = jax.ShapeDtypeStruct
    wide = shape(states[0].shape, jnp.float32)
    columns = width // groups
    if last:
        out_shape = [wide, wide, shape((rows, columns), jnp.float32)]
        out_shape.append(shape((groups - 1, rows, columns), jnp.bfloat16))
        out_specs = anywhere(2) + vmem(2)
    else:
        out_shape = [wide, wide, wide, shape(states[0].shape, jnp.bfloat16)]
        out_specs = anywhere(4)
    operands = (place, below, above, terms, *states, *chain, *known)
    return pl.pallas_call(
        functools.partial(
            update_kernel,
            piece=piece,
            own=own,
            step_count=step_count,
            last=last,
            chained=len(chain),
            extra=len(known),
        ),
        in_specs=smem(1) + vmem(2) + anywhere(len(operands) - 3),
        out_specs=out_specs,
        out_shape=out_shape,
        scratch_shapes=[
            pltpu.VMEM((len(states), rows, width), jnp.float32),
            pltpu.VMEM((rows, width), jnp.bfloat16),
            pltpu.VMEM((3, rows, width), jnp.float32),
            pltpu.VMEM((rows, width), jnp.bfloat16),
            pltpu.SemaphoreType.DMA((4, len(states) + 1)),
            pltpu.SemaphoreType.DMA((4, 4)),
        ],
        input_output_aliases=chain_aliases(4 + len(states), chain),
        compiler_params=pltpu.CompilerParams(vmem_limit_bytes=52 << 20),
        cost_estimate=pl.CostEstimate(
            flops=LINE_FLOPS, bytes_accessed=24 * rows * width, transcendentals=0
        ),
        name="update",
    )(*operands)


def run_outer(place, own, got, arrays, piece, chain, known):
    rows, columns = own.shape
    shape = jax.ShapeDtypeStruct
    narrow = shape(arrays[1].shape, jnp.float32)
    operands = (place, own, *got, *arrays, *chain, *known)
    return pl.pallas_call(
        functools.partial(
            outer_kernel,
            piece=piece,
            groups=len(got) + 1,
            chained=len(chain),
            extra=len(known),
        ),
        in_specs=smem(1) + vmem(1 + len(got)) + anywhere(len(operands) - 2 - len(got)),
        out_specs=anywhere(3) + vmem(1),
        out_shape=[narrow] * 3 + [shape(own.shape, jnp.bfloat16)],
        scratch_shapes=[
            pltpu.VMEM((3, rows, columns), jnp.float32),
            pltpu.VMEM((3, rows, columns), jnp.float32),
            pltpu.SemaphoreType.DMA((3,)),
            pltpu.SemaphoreType.DMA((3,)),
        ],
        input_output_aliases=chain_aliases(5 + len(got), chain),
        compiler_params=pltpu.CompilerParams(vmem_limit_bytes=52 << 20),
        cost_estimate=pl.CostEstimate(
            flops=LINE_FLOPS, bytes_accessed=24 * rows * columns, transcendentals=0
        ),
        name="outer",
    )(*operands)


def run_join(place, parts, like, piece, chain):
    rows, columns = parts[0].shape
    groups = len(parts)
    operands = (place, *parts, *chain)
    return pl.pallas_call(
        functools.partial(join_kernel, piece=piece, groups=groups, chained=len(chain)),
        in_specs=smem(1) + vmem(groups) + anywhere(len(chain)),
        out_specs=anywhere(2),
        out_shape=[
            jax.ShapeDtypeStruct(like.shape, jnp.float32),
            jax.ShapeDtypeStruct(like.shape, jnp.bfloat16),
        ],
        scratch_shapes=[
            pltpu.VMEM((groups, rows, columns), jnp.float32),
            pltpu.SemaphoreType.DMA((2, groups)),
        ],
        input_output_aliases=chain_aliases(1 + groups, chain),
        compiler_params=pltpu.CompilerParams(vmem_limit_bytes=52 << 20),
        cost_estimate=pl.CostEstimate(
            flops=LINE_FLOPS, bytes_accessed=12 * rows * columns * groups, transcendentals=0
        ),
        name="join",
    )(*operands)


def run_products(
    info, needs, gathered, proj_parts, attn_parts, plane_h1, plane_d_down, pairs, piece, known
):
    count = info.shape[0]
    sources, tokens, width = plane_h1.shape
    shape = jax.ShapeDtypeStruct((count, piece, width), jnp.bfloat16)
    made = pl.pallas_call(
        functools.partial(feed_forward_products_kernel, extra=len(attn_parts)),
        in_specs=smem(2) + anywhere(2 + len(pairs) + len(attn_parts)),
        out_specs=vmem(1)[0],
        out_shape=shape,
        scratch_shapes=[
            pltpu.VMEM((2, sources * tokens, width), jnp.bfloat16),
            pltpu.VMEM((count, piece, width), jnp.bfloat16),
            pltpu.VMEM((count, piece, width), jnp.bfloat16),
            pltpu.SemaphoreType.DMA((2, sources)),
            pltpu.SemaphoreType.DMA((count,)),
            pltpu.SemaphoreType.DMA((count,)),
        ],
        compiler_params=pltpu.CompilerParams(vmem_limit_bytes=44 << 20),
        cost_estimate=pl.CostEstimate(
            flops=6 * count * sources * tokens * piece * width,
            bytes_accessed=6 * count * piece * width,
            transcendentals=0,
        ),
        name="feed_forward_products",
    )(info, needs, gathered, plane_d_down, *pairs, *attn_parts)
    operands = (info, needs, plane_h1, *proj_parts, *attn_parts, *pairs, *known, made)
    return pl.pallas_call(
        functools.partial(
            attention_products_kernel, sources=sources, extra=len(known)
        ),
        in_specs=smem(2) + anywhere(len(operands) - 2),
        out_specs=anywhere(1)[0],
        out_shape=shape,
        scratch_shapes=[
            pltpu.VMEM((2, sources * tokens, width), jnp.bfloat16),
            pltpu.VMEM((sources * tokens, 3 * width), jnp.bfloat16),
            pltpu.VMEM((sources * tokens, width), jnp.bfloat16),
            pltpu.VMEM((count, piece, width), jnp.bfloat16),
            pltpu.SemaphoreType.DMA((2, sources)),
            pltpu.SemaphoreType.DMA((2, sources)),
            pltpu.SemaphoreType.DMA((count,)),
        ],
        input_output_aliases={len(operands) - 1: 0},
        compiler_params=pltpu.CompilerParams(vmem_limit_bytes=44 << 20),
        cost_estimate=pl.CostEstimate(
            flops=2 * count * sources * tokens * piece * width,
            bytes_accessed=2 * count * piece * width,
            transcendentals=0,
        ),
        name="attention_products",
    )(*operands)


def pad_rows(rows):
    return jnp.pad(rows, ((0, -rows.shape[0] % 16), (0, 0)))


def swap(values, axis, delta):
    size = lax.axis_size(axis)
    return lax.ppermute(values, axis, [(i, i ^ delta) for i in range(size)])


def sum_over(values, axes):
    for axis in axes:
        parts = [values]
        parts += [swap(values, axis, delta) for delta in range(1, lax.axis_size(axis))]
        while len(parts) > 1:
            parts = [parts[at] + parts[at + 1] for at in range(0, len(parts), 2)]
        values = parts[0]
    return values


def gathered_rows(values):
    return lax.all_gather(pad_rows(values), ("dp", "fsdp"), axis=0, tiled=False)


def line_order(line):
    due = np.zeros((line, line), np.int32)
    for here in range(line):
        for there in range(line):
            if there > here:
                due[here, there] = line - 1 - there + here
            elif there < here:
                due[here, there] = there - here + line - 1
            else:
                due[here, there] = line
    return np.argsort(due, axis=1, kind="stable").astype(np.int32)


def line_slots(line, order):
    ups = np.zeros((line - 1, line), np.int32)
    downs = np.zeros((line - 1, line), np.int32)
    for step in range(line - 1):
        for here in range(line):
            if here <= step:
                ups[step, here] = list(order[here]).index(line - 1 - step + here)
            if line - 1 - here <= step:
                downs[step, here] = list(order[here]).index(step - (line - 1) + here)
    return ups, downs


def added(*parts):
    return sum(part.astype(jnp.float32) for part in parts)


def due_after(value, *marks):
    flag = sum(mark[(-1,) * mark.ndim].astype(jnp.float32) for mark in marks)
    return value + (flag != flag).astype(value.dtype)


def plane_order(planes):
    deltas = [0]
    bit = planes // 2
    while bit >= 1:
        deltas = deltas + [delta ^ bit for delta in deltas]
        bit //= 2
    return deltas


def plane_gather(values):
    values = values[None]
    bit = lax.axis_size("fsdp") // 2
    while bit >= 1:
        values = jnp.concatenate([values, swap(values, "fsdp", bit)], axis=0)
        bit //= 2
    return values


def plane_operands(plane_rows, vec_now):
    sel_rows = plane_rows[:, 0].astype(jnp.float32)
    cot_rows = plane_rows[:, 1].astype(jnp.float32)
    gate = jax.nn.sigmoid(jnp.sum(sel_rows * vec_now[2], axis=-1, keepdims=True))
    inverse = lax.rsqrt(row_mean(sel_rows * sel_rows) + EPS_NORM)
    h1 = (sel_rows * inverse * vec_now[0]).astype(jnp.bfloat16)
    return (h1, (gate * cot_rows).astype(jnp.bfloat16))


def send_to(target, values):
    planes = lax.axis_size("fsdp")
    return [values] + [
        lax.ppermute(values, "fsdp", [(target ^ delta, target)]) for delta in plane_order(planes)[1:]
    ]


def gradient_plan(shard_rows, model_width, columns):
    planes, line = lax.axis_size("fsdp"), lax.axis_size("dp")
    plane, here = lax.axis_index("fsdp"), lax.axis_index("dp")
    hidden_units = (columns - 4 * model_width) // 2
    edges = (3 * model_width, 4 * model_width, 4 * model_width + hidden_units)

    def kind_of(row):
        return sum((row >= edge).astype(jnp.int32) for edge in edges)

    piece = shard_rows // PIECES
    theres = jnp.asarray(line_order(line))[here]
    rows = (plane * line + theres)[:, None] * shard_rows + jnp.arange(PIECES) * piece
    rows = rows.reshape(-1)
    kinds = kind_of(rows)
    at = rows - 3 * model_width
    order = (planes, line, shard_rows)
    uppers = gathered_row(jnp.where(kinds == 2, rows, rows - hidden_units), order)
    lowers = gathered_row(jnp.minimum(rows + hidden_units, columns - piece), order)
    info = jnp.stack([kinds, jnp.where(kinds >= 2, uppers, at), lowers], axis=1)
    low, high = kind_of(plane * line * shard_rows), kind_of((plane + 1) * line * shard_rows - 1)
    ff = (high >= 2).astype(jnp.int32)
    has_proj = (low == 0).astype(jnp.int32)
    has_attn = ((low <= 1) & (high >= 1)).astype(jnp.int32)
    moves = jnp.asarray(np.stack(line_slots(line, line_order(line)), axis=-1))[:, here]
    return (info.astype(jnp.int32), jnp.stack([has_proj, has_attn, ff, ff]), moves)


def gradient_starts(shard_rows, model_width, split):
    line, here = lax.axis_size("dp"), lax.axis_index("dp")
    if split:
        return jnp.asarray(line_order(line) * shard_rows)[here]
    return jnp.arange(4, dtype=jnp.int32) * (3 * model_width // 4)


def in_planes(shard_rows, model_width):
    line = lax.axis_size("dp")
    return (shard_rows // PIECES) % 128 == 0 and line * shard_rows == 3 * model_width


def gradient_whole(columns, operands):
    hidden_units = columns[2].shape[1] // 2
    factors = (*columns[:2], columns[2][:, :hidden_units], columns[2][:, hidden_units:])
    products = [tn(factor, operand) for factor, operand in zip(factors, operands)]
    low = jnp.concatenate(products, axis=0).astype(jnp.bfloat16)
    share = lax.psum_scatter(low, ("fsdp", "dp"), scatter_dimension=0, tiled=True)
    return share.astype(jnp.float32)


def plane_terms(
    gathered, d_proj, d_attn_low, pairs, plane_h1, plane_d_down, info, needs, shard_rows, known
):
    attn_parts = send_to(1, d_attn_low)
    pairs = [pairs]
    bit = lax.axis_size("fsdp") // 4
    while bit >= 1:
        pairs.append(swap(jnp.concatenate(pairs, axis=0), "fsdp", bit))
        bit //= 2
    return run_products(
        info,
        needs,
        gathered,
        send_to(0, d_proj),
        attn_parts,
        plane_h1,
        plane_d_down,
        pairs,
        shard_rows // PIECES,
        known,
    )


def gradient_share(terms, moves, passed, meanwhile):
    line = lax.axis_size("dp")
    below, above = [None] * PIECES, [None] * PIECES
    for step in range(line - 1):
        for index in range(PIECES):
            if step == 0:
                up = down = terms[index]
            else:
                due = known[index] if step == line - 2 else ()
                given = passed if step == 1 and index == 0 else ()
                up, down, *given = run_line(
                    moves, below[index], above[index], terms, step, index, given, due
                )
                if step == 1 and index == 0:
                    known = meanwhile(up, given)
            below[index] = lax.ppermute(up, "dp", [(p, p + 1) for p in range(step + 1)])
            above[index] = lax.ppermute(
                down, "dp", [(line - 1 - p, line - 2 - p) for p in range(step + 1)]
            )
    return (below, above)


def adamw(param, grad, first, second, step_count, rate, decay):
    first = BETA_ONE * first + (1.0 - BETA_ONE) * grad
    second = BETA_TWO * second + (1.0 - BETA_TWO) * grad * grad
    fixed_one = 1.0 - BETA_ONE**step_count
    fixed_two = 1.0 - BETA_TWO**step_count
    direction = first / fixed_one / (jnp.sqrt(second / fixed_two) + EPS_ADAM)
    return (param - rate * (direction + decay * param), first, second)


def vector_rates():
    return jnp.array([[0.1], [0.1], [0.02]], dtype=jnp.float32)


def outer_whole(weights, master, outer_moment, smoothed_matrix_mean):
    groups = lax.axis_size("grp")
    here = lax.axis_index("grp")
    delta = weights - master
    col_width = weights.shape[1] // groups
    col_start = here * col_width
    diff_share = lax.dynamic_slice_in_dim(delta, col_start, col_width, 1)
    for step in range(1, groups):
        there = lax.rem(here + step, groups)
        part = lax.dynamic_slice_in_dim(delta, there * col_width, col_width, 1)
        diff_share = diff_share + shift_group(part.astype(jnp.bfloat16), step).astype(jnp.float32)
    diff_share = diff_share / groups
    moment_share = OUTER_MOMENTUM * outer_moment + diff_share
    base_share = lax.dynamic_slice_in_dim(weights, col_start, col_width, 1)
    new_share = base_share - OUTER_RATE * (diff_share + OUTER_MOMENTUM * moment_share)
    low_share = new_share.astype(jnp.bfloat16)
    weights_low = jnp.zeros(weights.shape, jnp.bfloat16)
    for step in range(groups):
        there = lax.rem(here + groups - step, groups)
        part = shift_group(low_share, step) if step else low_share
        weights_low = lax.dynamic_update_slice_in_dim(weights_low, part, there * col_width, 1)
    average_new = AVERAGE_KEEP * smoothed_matrix_mean + (1.0 - AVERAGE_KEEP) * new_share
    return (weights_low.astype(jnp.float32), weights_low, moment_share, diff_share, average_new)


def shift_group(values, step):
    groups = lax.axis_size("grp")
    return lax.ppermute(values, "grp", [(i, (i + step) % groups) for i in range(groups)])


def on_device(
    tokens,
    cotangent,
    lengths,
    selected,
    weights,
    vectors,
    first_moment,
    second_moment,
    vec_first,
    vec_second,
    outer_moment,
    smoothed_matrix_mean,
    vec_outer,
    vec_average,
):
    master = weights
    vec_now = vectors
    first_now = first_moment[0]
    second_now = second_moment[0]
    vfirst_now = vec_first[0]
    vsecond_now = vec_second[0]
    model_width = tokens.shape[2]
    planes, line = lax.axis_size("fsdp"), lax.axis_size("dp")
    shard_rows = weights.shape[0]
    info, needs, moves = gradient_plan(shard_rows, model_width, weights.shape[0] * planes * line)
    boths, masks, across = run_gather(lengths[:, 0], selected[:, 0], tokens, cotangent)
    plane_rows = plane_gather(boths[0])
    split = in_planes(shard_rows, model_width)
    starts = gradient_starts(shard_rows, model_width, split)
    order = (planes, line, shard_rows)
    weight_starts = gathered_row(starts, order)
    plan = (info, needs, moves, starts, weight_starts)
    groups = lax.axis_size("grp")
    place = lax.axis_index("grp").astype(jnp.int32)[None]
    shard_low = master.astype(jnp.bfloat16)
    activations, input_grad, outers = [], [], []
    for inner_step in range(INNER):
        both, mask = boths[inner_step], masks[inner_step]
        gathered = lax.all_gather(shard_low, ("dp", "fsdp"), axis=0, tiled=True)
        plane_h1, plane_d_down = plane_operands(plane_rows, vec_now)
        proj, lse, pair, first_sum = run_attention(
            order,
            gathered,
            plan,
            both,
            vec_now,
            mask,
            [plane_h1, plane_d_down, *activations, *input_grad],
        )
        d_attn_low, out_rows, base, grad_two, *kept = run_feed_forward(
            order, gathered, both, vec_now, first_sum, not split
        )
        got = swap(pair[None], "fsdp", planes // 2)
        d_proj, pairs = run_attention_back(
            order, gathered, starts, d_attn_low, proj, lse, mask, pair, got
        )
        following = list(boths[inner_step + 1 : inner_step + 2])
        last = not following
        step_count = STEP + inner_step
        results = []

        def input_step(marks):
            d_rows, grad_one = run_input_back(
                None if split else order, gathered, weight_starts, d_proj, both, vec_now, base, marks
            )
            results.append(jnp.concatenate([grad_one, grad_two], axis=0))
            return d_rows

        def scatter_step(d_rows, marks):
            activations[:] = [
                run_scatter(across, tokens, out_rows, inner_step, activations, marks)
            ]
            input_grad[:] = [
                run_scatter(across, cotangent, d_rows, inner_step, input_grad, marks)
            ]

        if split and last:
            d_rows = input_step([])
            results[0] = gathered_rows(results[0])

        def meanwhile(mark, passed):
            if not last:
                results.append(plane_gather(passed[0]))
                return (results[-1:], (), ())
            return ((), (), ())

        if split:
            terms = plane_terms(
                gathered,
                d_proj,
                d_attn_low,
                pairs,
                plane_h1,
                plane_d_down,
                info,
                needs,
                shard_rows,
                [d_rows] if last else (),
            )
            below, above = gradient_share(terms, moves, following, meanwhile)
            grad_mark = below[-1]
        else:
            grad_mark = gradient_whole(
                (d_proj, d_attn_low, *kept), (plane_h1[0], pair[0], pair[1], plane_d_down[0])
            )
            results.extend(plane_gather(values) for values in following)
        if split and last:
            made = []
            for index in range(PIECES):
                made.append(
                    run_update(
                        place,
                        below[index],
                        above[index],
                        terms,
                        (master, first_now, second_now, weights),
                        index,
                        step_count,
                        last,
                        groups,
                        made[-1][:2] if index else (),
                        [outers[0][3]] + input_grad if index == PIECES - 1 else activations,
                    )
                )
                own, other = made[-1][2:]
                if index == 0:
                    scatter_step(d_rows, [own])
                outers.append(
                    run_outer(
                        place,
                        own,
                        [shift_group(other[step - 1], step) for step in range(1, groups)],
                        (weights, outer_moment, smoothed_matrix_mean),
                        index,
                        outers[-1][:3] if index else (),
                        [],
                    )
                )
            first_now, second_now = made[-1][:2]
        else:
            grad_shard = grad_mark
            if split:
                own = (line - 1) * PIECES
                grad_shard = jnp.concatenate(
                    [
                        added(terms[own + index], below[index], above[index])
                        for index in range(PIECES)
                    ],
                    axis=0,
                )
            master, first_now, second_now = adamw(
                master, grad_shard, first_now, second_now, step_count, INNER_RATE, DECAY_RATE
            )
            shard_low = master.astype(jnp.bfloat16)
        if not last:
            plane_rows = results.pop()
        if split and last:
            grad_vec = jnp.sum(due_after(results[0][:, : vec_now.shape[0]], made[0][2]), axis=0)
            vec_now, vfirst_now, vsecond_now = adamw(
                vec_now, grad_vec, vfirst_now, vsecond_now, step_count, vector_rates(), 0.0
            )
            vec_diff = sum_over(vectors - vec_now, ("grp",)) / groups
        else:
            scatter_step(input_step([grad_mark]), [grad_mark])
            grad_vec = sum_over(due_after(results[0], grad_mark), ("fsdp", "dp"))
            vec_now, vfirst_now, vsecond_now = adamw(
                vec_now, grad_vec, vfirst_now, vsecond_now, step_count, vector_rates(), 0.0
            )
    if split:
        joined = []
        for index in range(PIECES):
            low = outers[index][3]
            parts = [low] + [shift_group(low, step) for step in range(1, groups)]
            joined = run_join(place, parts, weights, index, joined)
        weights_new, weights_low = joined
        outer_new, diff_new, average_new = outers[-1][:3]
    else:
        weights_new, weights_low, outer_new, diff_new, average_new = outer_whole(
            weights, master, outer_moment, smoothed_matrix_mean
        )
    if not split:
        vec_diff = sum_over(vectors - vec_now, ("grp",)) / groups
    vec_moment = OUTER_MOMENTUM * vec_outer + vec_diff
    vectors_new = vectors - OUTER_RATE * (vec_diff + OUTER_MOMENTUM * vec_moment)
    vec_average_new = AVERAGE_KEEP * vec_average + (1.0 - AVERAGE_KEEP) * vectors_new
    return (
        activations[0],
        input_grad[0],
        weights_new,
        weights_low,
        first_now[None],
        second_now[None],
        outer_new,
        diff_new,
        average_new,
        vectors_new,
        vfirst_now[None],
        vsecond_now[None, :2],
        vsecond_now[None, 2],
        vec_moment,
        vec_average_new,
    )


def solution(mesh):
    placed = (
        P(None, ("grp", "fsdp", "dp"), None),
        P(None, ("grp", "fsdp", "dp"), None),
        P(None, ("grp", "fsdp", "dp"), None),
        P(None, ("grp", "fsdp", "dp"), None),
        P(("fsdp", "dp"), None),
        P(),
        P("grp", ("fsdp", "dp"), None),
        P("grp", ("fsdp", "dp"), None),
        P("grp", None, None),
        P("grp", None, None),
        P(("fsdp", "dp"), "grp"),
        P(("fsdp", "dp"), "grp"),
        P(),
        P(),
    )
    return jax.shard_map(
        on_device,
        mesh=mesh,
        in_specs=placed,
        out_specs=(
            P(None, ("grp", "fsdp", "dp"), None),
            P(None, ("grp", "fsdp", "dp"), None),
            P(("fsdp", "dp"), None),
            P(("fsdp", "dp"), None),
            P("grp", ("fsdp", "dp"), None),
            P("grp", ("fsdp", "dp"), None),
            P(("fsdp", "dp"), "grp"),
            P(("fsdp", "dp"), "grp"),
            P(("fsdp", "dp"), "grp"),
            P(),
            P("grp", None, None),
            P("grp", None, None),
            P("grp", None),
            P(),
            P(),
        ),
        check_vma=False,
    )
```

```python
import functools
import math

import jax
import jax.numpy as jnp
import numpy as np
from jax import lax
from jax.experimental import pallas as pl
from jax.experimental.pallas import tpu as pltpu
from jax.sharding import PartitionSpec as P

HEAD = 64
INNER = 2
STEP = 5


EPS_NORM = 1e-06
EPS_ADAM = 1e-08
BETA_ONE = 0.9
BETA_TWO = 0.95
INNER_RATE = 0.03
DECAY_RATE = 0.1
OUTER_RATE = 0.7
OUTER_MOMENTUM = 0.9
AVERAGE_KEEP = 0.9
GELU_SCALE = float(np.sqrt(2.0 / np.pi))
GELU_CUBE = 0.044715
PIECES = 3
LINE_FLOPS = 10**10
SMALL_COST = pl.CostEstimate(flops=10**6, bytes_accessed=10**5, transcendentals=0)
NOWHERE = 1 << 20


def nt(left, right):
    return lax.dot_general(
        left, right, (((1,), (1,)), ((), ())), preferred_element_type=jnp.float32
    )


def nn(left, right):
    return lax.dot_general(
        left, right, (((1,), (0,)), ((), ())), preferred_element_type=jnp.float32
    )


def tn(left, right):
    return lax.dot_general(
        left, right, (((0,), (0,)), ((), ())), preferred_element_type=jnp.float32
    )


def gathered_row(row, order):
    planes, line, shard_rows = order
    shard = row // shard_rows
    return ((shard % line) * planes + shard // line) * shard_rows + row % shard_rows


class WeightCopy:
    def __init__(self, weights, held, sem, source, target, rows, order):
        unit = math.gcd(order[2], rows)
        self.parts = [
            pltpu.make_async_copy(
                weights.at[pl.ds(gathered_row(source * rows + at, order), unit)],
                held.at[pl.ds(target * rows + at, unit)],
                sem,
            )
            for at in range(0, rows, unit)
        ]
        self.whole = pltpu.make_async_copy(
            weights.at[pl.ds(0, rows)], held.at[pl.ds(target * rows, rows)], sem
        )

    def start(self):
        for part in self.parts:
            part.start()

    def wait(self):
        self.whole.wait()


def weight_copies(weights, held, sems, sources, rows, order):
    return [
        WeightCopy(weights, held, sems.at[target], source, target, rows, order)
        for target, source in enumerate(sources)
    ]


def two_heads(values):
    low = lax.broadcasted_iota(jnp.int32, values.shape, 1) < HEAD
    zero = jnp.zeros_like(values)
    return jnp.concatenate([jnp.where(low, values, zero), jnp.where(low, zero, values)], axis=0)


def one_block(values):
    rows = values.shape[0] // 2
    low = lax.broadcasted_iota(jnp.int32, (rows, values.shape[1]), 1) < HEAD
    return jnp.where(low, values[:rows], values[rows:])


def row_mean(values):
    return jnp.mean(values, axis=-1, keepdims=True)


def gelu_and_slope(pre):
    square = pre * pre
    tanh = jnp.tanh(GELU_SCALE * pre * (1.0 + GELU_CUBE * square))
    half = 0.5 * (1.0 + tanh)
    slope = half + 0.5 * pre * (1.0 - tanh * tanh) * (
        GELU_SCALE * (1.0 + 3.0 * GELU_CUBE * square)
    )
    return ((pre * half).astype(jnp.bfloat16), slope)


def gather_kernel(lengths, picked_ref, across_ref, tokens_hbm, cot_hbm, *refs, steps, extra):
    refs = refs[extra:]
    both_refs, mask_refs = refs[:steps], refs[steps : 2 * steps]
    held, sems = refs[2 * steps :]
    copies = [
        [
            pltpu.make_async_copy(source.at[step], held.at[step, at], sems.at[step, at])
            for at, source in enumerate((tokens_hbm, cot_hbm))
        ]
        for step in range(steps)
    ]
    for some in copies:
        for copy in some:
            copy.start()
    for step in range(steps):
        down, across = picked_ref[step], across_ref[step]
        segment_down, segment_across = jnp.zeros_like(down), jnp.zeros_like(across)
        end = jnp.int32(0)
        for slot in range(lengths.shape[1]):
            end = end + lengths[step, slot]
            segment_down += (down >= end).astype(jnp.int32)
            segment_across += (across >= end).astype(jnp.int32)
        allowed = (segment_down == segment_across) & (across <= down)
        allowed = allowed.astype(jnp.int32)
        mask_refs[step][...] = jnp.concatenate([allowed, allowed], axis=0)
        places = lax.broadcasted_iota(jnp.int32, (down.shape[0], held.shape[2]), 1)
        chosen = jnp.where(places == down, 1.0, 0.0).astype(jnp.bfloat16)
        for at in range(2):
            copies[step][at].wait()
            both_refs[step][at] = nn(chosen, held[step, at]).astype(jnp.bfloat16)


def scatter_kernel(across_ref, base_ref, rows_ref, *refs):
    out_ref, mark_ref = refs[-2:]
    mark_ref[...] = jnp.zeros_like(mark_ref)
    base = base_ref[0]
    across = across_ref[0]
    places = lax.broadcasted_iota(jnp.int32, (base.shape[0], across.shape[1]), 0)
    chosen = jnp.where(places == across, 1.0, 0.0)
    replaced = jnp.sum(chosen, axis=-1, keepdims=True) > 0.0
    rows = nn(chosen.astype(jnp.bfloat16), rows_ref[...]).astype(jnp.bfloat16)
    out_ref[0] = jnp.where(replaced, rows, base)


def attention_kernel(
    weights, mask_hbm, both_ref, vec_ref, *refs, order, extra
):
    proj_ref, lse_ref, pair_ref, first_ref, held, mask_ref, sems, mask_sem = refs[extra:]
    rows_ref = both_ref.at[0]
    width = both_ref.shape[2]
    copies = weight_copies(weights, held, sems, range(4), width, order)
    mask_copy = pltpu.make_async_copy(mask_hbm, mask_ref, mask_sem)
    mask_copy.start()
    for copy in copies:
        copy.start()
    xs = rows_ref[...].astype(jnp.float32)
    h1 = (xs * lax.rsqrt(row_mean(xs * xs) + EPS_NORM) * vec_ref[0:1, :]).astype(jnp.bfloat16)
    for index in range(3):
        copies[index].wait()
        proj_ref[:, index * width : (index + 1) * width] = nt(
            h1, held[pl.ds(index * width, width), :]
        ).astype(jnp.bfloat16)
    mask_copy.wait()
    allowed = mask_ref[...] > 0
    lane = lax.broadcasted_iota(jnp.int32, lse_ref.shape, 1)
    lse = jnp.zeros(lse_ref.shape, jnp.float32)
    for pair in range(width // 128):
        at = pair * 128
        queries = two_heads(proj_ref[:, at : at + 128])
        keys = proj_ref[:, width + at : width + at + 128]
        values = proj_ref[:, 2 * width + at : 2 * width + at + 128]
        scores = jnp.where(allowed, nt(queries, keys) * HEAD ** (-0.5), -1e30)
        top = jnp.max(scores, axis=-1, keepdims=True)
        total = top + jnp.log(jnp.sum(jnp.exp(scores - top), axis=-1, keepdims=True))
        lse = jnp.where(lane == pair, total, lse)
        probs_low = jnp.exp(scores - total).astype(jnp.bfloat16)
        pair_ref[0, :, at : at + 128] = one_block(nn(probs_low, values)).astype(jnp.bfloat16)
    lse_ref[...] = lse
    copies[3].wait()
    first_sum = xs + nt(pair_ref[0], held[pl.ds(3 * width, width), :])
    first_ref[...] = first_sum
    inverse = lax.rsqrt(row_mean(first_sum * first_sum) + EPS_NORM)
    pair_ref[1] = (first_sum * inverse * vec_ref[1:2, :]).astype(jnp.bfloat16)


def feed_forward_kernel(
    weights,
    both_ref,
    vec_ref,
    first_ref,
    d_attn_ref,
    out_ref,
    base_ref,
    grad_ref,
    *refs,
    keep,
    order,
):
    held, sems = refs[-2:]
    rows_ref, cot_ref = both_ref.at[0], both_ref.at[1]
    width = both_ref.shape[2]
    hidden = (weights.shape[0] - 4 * width) // 2
    parts = hidden // width
    matrices = []
    for part in range(parts):
        matrices += [4 + part, 4 + parts + part]
    copies = weight_copies(weights, held, sems, matrices, width, order)
    for copy in copies:
        copy.start()

    def matrix(index):
        return held[pl.ds(index * width, width), :]

    xs = rows_ref[...].astype(jnp.float32)
    cot = cot_ref[...].astype(jnp.float32)
    gate = jax.nn.sigmoid(jnp.sum(xs * vec_ref[2:3, :], axis=-1, keepdims=True))
    first_sum = first_ref[...]
    inverse = lax.rsqrt(row_mean(first_sum * first_sum) + EPS_NORM)
    normed = first_sum * inverse
    h2 = (normed * vec_ref[1:2, :]).astype(jnp.bfloat16)
    d_branch = gate * cot
    d_down = d_branch.astype(jnp.bfloat16)
    branch = first_sum - xs
    d_h2 = jnp.zeros_like(branch)
    for part in range(parts):
        at = part * width
        copies[2 * part].wait()
        act, slope = gelu_and_slope(nt(h2, matrix(2 * part)))
        copies[2 * part + 1].wait()
        branch = branch + nn(act, matrix(2 * part + 1))
        d_pre = (nt(d_down, matrix(2 * part + 1)) * slope).astype(jnp.bfloat16)
        if keep:
            refs[0][:, at : at + width] = d_pre
            refs[0][:, at + hidden : at + hidden + width] = act
        d_h2 = d_h2 + nn(d_pre, matrix(2 * part))
    out_ref[...] = (xs + gate * branch).astype(jnp.bfloat16)
    d_logit = jnp.sum(cot * branch, axis=-1, keepdims=True) * gate * (1.0 - gate)
    grad_ref[0:1, :] = jnp.sum(d_h2 * normed, axis=0, keepdims=True)
    grad_ref[1:2, :] = jnp.sum(d_logit * xs, axis=0, keepdims=True)
    d_normed = d_h2 * vec_ref[1:2, :]
    d_first = inverse * (d_normed - normed * row_mean(d_normed * normed))
    d_attn_ref[...] = (d_branch + d_first).astype(jnp.bfloat16)
    base_ref[...] = cot + d_first + d_logit * vec_ref[2:3, :]


def attention_back_kernel(
    weights,
    starts,
    d_attn_ref,
    proj_ref,
    lse_ref,
    mask_ref,
    pair_hbm,
    got_hbm,
    cuts_hbm,
    pairs_hbm,
    held,
    late_ref,
    weight_sems,
    pair_sems,
    cut_sems,
    *,
    order,
):
    width = held.shape[1]
    copies = weight_copies(weights, held, weight_sems, [3], width, order)
    pair_copies = [
        pltpu.make_async_copy(pair_hbm, pairs_hbm.at[0], pair_sems.at[0]),
        pltpu.make_async_copy(got_hbm.at[0], pairs_hbm.at[1], pair_sems.at[1]),
    ]
    for copy in copies + pair_copies:
        copy.start()
    copies[0].wait()
    d_mixed = nn(d_attn_ref[...], held[pl.ds(0, width), :]).astype(jnp.bfloat16)
    allowed = mask_ref[...] > 0
    for pair in range(width // 128):
        at = pair * 128
        queries = two_heads(proj_ref[:, at : at + 128])
        keys = proj_ref[:, width + at : width + at + 128]
        values = proj_ref[:, 2 * width + at : 2 * width + at + 128]
        d_pair = two_heads(d_mixed[:, at : at + 128])
        scores = jnp.where(allowed, nt(queries, keys) * HEAD ** (-0.5), -1e30)
        probs = jnp.exp(scores - lse_ref[:, pair : pair + 1])
        probs_low = probs.astype(jnp.bfloat16)
        d_probs = nt(d_pair, values)
        d_scores = probs * (d_probs - jnp.sum(d_probs * probs, axis=-1, keepdims=True))
        d_scores = d_scores.astype(jnp.bfloat16)
        late_ref[:, at : at + 128] = (one_block(nn(d_scores, keys)) * HEAD ** (-0.5)).astype(
            jnp.bfloat16
        )
        late_ref[:, width + at : width + at + 128] = (
            tn(d_scores, queries) * HEAD ** (-0.5)
        ).astype(jnp.bfloat16)
        late_ref[:, 2 * width + at : 2 * width + at + 128] = tn(probs_low, d_pair).astype(
            jnp.bfloat16
        )
    cuts = starts.shape[0]
    span = late_ref.shape[1] // cuts
    cut_copies = []
    for cut in range(cuts):
        start = pl.multiple_of(starts[cut], 128)
        cut_copies.append(
            pltpu.make_async_copy(
                late_ref.at[:, pl.ds(start, span)],
                cuts_hbm.at[:, pl.ds(cut * span, span)],
                cut_sems.at[cut],
            )
        )
    for copy in cut_copies:
        copy.start()
    for copy in cut_copies + pair_copies:
        copy.wait()


def input_back_kernel(
    weights, rows, cuts_ref, both_ref, vec_ref, base_ref, *refs, extra, order
):
    d_rows_ref, grad_ref, held, sems = refs[extra:]
    cuts, span, width = held.shape
    if order is None:
        copies = [
            pltpu.make_async_copy(
                weights.at[pl.ds(pl.multiple_of(rows[cut], 128), span)], held.at[cut], sems.at[cut]
            )
            for cut in range(cuts)
        ]
    else:
        copies = [
            WeightCopy(weights, held.at[cut], sems.at[cut], cut, 0, span, order)
            for cut in range(cuts)
        ]
    for copy in copies:
        copy.start()
    xs = both_ref[0].astype(jnp.float32)
    inverse = lax.rsqrt(row_mean(xs * xs) + EPS_NORM)
    normed = xs * inverse
    d_h1 = jnp.zeros(xs.shape, jnp.float32)
    for cut in range(cuts):
        copies[cut].wait()
        d_h1 = d_h1 + nn(cuts_ref[:, cut * span : (cut + 1) * span], held[cut])
    grad_ref[...] = jnp.sum(d_h1 * normed, axis=0, keepdims=True)
    d_normed = d_h1 * vec_ref[0:1, :]
    d_rows_ref[...] = (
        base_ref[...] + inverse * (d_normed - normed * row_mean(d_normed * normed))
    ).astype(jnp.bfloat16)


def plane_copies(refs, target, sems, tokens):
    return [
        pltpu.make_async_copy(ref, target.at[pl.ds(at * tokens, tokens)], sems.at[at])
        for at, ref in enumerate(refs)
    ]


def pair_refs_of(refs, index):
    return [ref.at[at, index] for ref in refs for at in range(ref.shape[0])]


def feed_forward_products_kernel(info, needs, weights, d_down_ref, *refs, extra):
    pair_refs = refs[: -7 - extra]
    out_ref, held, uppers, lowers, held_sems, upper_sems, lower_sems = refs[-7:]
    count, piece, _ = out_ref.shape
    sources, tokens, _ = d_down_ref.shape

    def row_copy(index, at, target, sems):
        start = pl.multiple_of(info[index, at], 16)
        return pltpu.make_async_copy(
            weights.at[pl.ds(start, piece)], target.at[index], sems.at[index]
        )

    def each_row_copy(index, act):
        @pl.when(info[index, 0] >= 2)
        def _():
            act(row_copy(index, 1, uppers, upper_sems))

        @pl.when(info[index, 0] == 2)
        def _():
            act(row_copy(index, 2, lowers, lower_sems))

    def each_held(act):
        @pl.when(needs[2] > 0)
        def _():
            copies = plane_copies(
                pair_refs_of(pair_refs, 1), held.at[0], held_sems.at[0], tokens
            ) + plane_copies(
                [d_down_ref.at[at] for at in range(sources)], held.at[1], held_sems.at[1], tokens
            )
            for copy in copies:
                act(copy)

    each_held(lambda copy: copy.start())

    @pl.loop(0, count)
    def _(index):
        each_row_copy(index, lambda copy: copy.start())

    each_held(lambda copy: copy.wait())

    @pl.loop(0, count)
    def _(index):
        each_row_copy(index, lambda copy: copy.wait())

        @pl.when(info[index, 0] == 2)
        def _():
            slope = gelu_and_slope(nt(uppers[index], held[0]))[1]
            d_pre = (nt(lowers[index], held[1]) * slope).astype(jnp.bfloat16)
            out_ref[index] = nn(d_pre, held[0]).astype(jnp.bfloat16)

        @pl.when(info[index, 0] == 3)
        def _():
            act = gelu_and_slope(nt(uppers[index], held[0]))[0]
            out_ref[index] = nn(act, held[1]).astype(jnp.bfloat16)


def attention_products_kernel(info, needs, h1_ref, *refs, sources, extra, first, last):
    proj_refs, attn_refs = refs[:sources], refs[sources : 2 * sources]
    pair_refs = refs[2 * sources : -10 - extra]
    near_ref, given_ref, out_ref, held, projs, attns, made, held_sems, factor_sems, out_sems = refs[-10:]
    _, piece, _ = made.shape
    tokens = h1_ref.shape[1]
    rights = ([h1_ref.at[at] for at in range(sources)], pair_refs_of(pair_refs, 0))
    columns = pl.ds(first * piece, (last - first) * piece)
    lefts = ([ref.at[:, columns] for ref in proj_refs], attn_refs)

    def each_operand(act):
        for kind, target in enumerate((projs, attns)):

            @pl.when(needs[kind] > 0)
            def _(kind=kind, target=target):
                copies = plane_copies(rights[kind], held.at[kind], held_sems.at[kind], tokens)
                copies += plane_copies(lefts[kind], target, factor_sems.at[kind], tokens)
                for copy in copies:
                    act(copy)

    def out_copy(index):
        return pltpu.make_async_copy(made.at[index - first], out_ref.at[index], out_sems.at[index])

    def passed_copy(index):
        source = near_ref if first else given_ref
        return pltpu.make_async_copy(source.at[index], out_ref.at[index], out_sems.at[index])

    def each_passed(act):
        for index in range(first if first else last):
            kind = info[index, 0]

            @pl.when((kind < 2) if first else (kind >= 2))
            def _(index=index):
                act(passed_copy(index))

    each_operand(lambda copy: copy.start())
    each_passed(lambda copy: copy.start())
    each_operand(lambda copy: copy.wait())
    for index in range(first, last):

        @pl.when(info[index, 0] == 0)
        def _(index=index):
            left = projs[:, (index - first) * piece : (index - first + 1) * piece]
            made[index - first] = tn(left, held[0]).astype(jnp.bfloat16)
            out_copy(index).start()

        @pl.when(info[index, 0] == 1)
        def _(index=index):
            left = attns[:, pl.ds(pl.multiple_of(info[index, 1], 128), piece)]
            made[index - first] = tn(left, held[1]).astype(jnp.bfloat16)
            out_copy(index).start()

    for index in range(first, last):

        @pl.when(info[index, 0] < 2)
        def _(index=index):
            out_copy(index).wait()

    each_passed(lambda copy: copy.wait())


def line_kernel(moves, below_ref, above_ref, terms_ref, *refs, step, piece, passed):
    up_ref, down_ref = refs[-4 - passed : -2 - passed]
    held, sems = refs[-2:]
    for source, target in zip(refs[:passed], refs[-2 - passed : -2]):
        target[...] = source[...]

    def each_copy(way, act):
        source = terms_ref.at[moves[step, way] * PIECES + piece]
        act(pltpu.make_async_copy(source, held.at[way], sems.at[way]))

    for way in range(2):
        each_copy(way, lambda copy: copy.start())
    for way, (came, leaves) in enumerate(((below_ref, up_ref), (above_ref, down_ref))):
        each_copy(way, lambda copy: copy.wait())
        leaves[...] = (held[way].astype(jnp.float32) + came[...].astype(jnp.float32)).astype(
            jnp.bfloat16
        )


def update_kernel(place, below_ref, above_ref, *refs, piece, own, step_count, last, chained, extra):
    arrays = refs[: 5 if last else 4]
    results = refs[len(arrays) + chained + extra : len(arrays) + chained + extra + 4]
    held, term, made, low, in_sems, out_sems = refs[-6:]
    rows = below_ref.shape[0]
    blocks = in_sems.shape[0]
    block = rows // blocks
    loads, stores = [], []
    for index in range(blocks):
        here = pl.ds(index * block, block)
        there = pl.ds(piece * rows + index * block, block)
        sources = [arrays[0].at[own, here]] + [array.at[there] for array in arrays[1:]]
        targets = [term.at[here]] + [held.at[at, here] for at in range(len(arrays) - 1)]
        loads.append(
            [
                pltpu.make_async_copy(source, target, in_sems.at[index, at])
                for at, (source, target) in enumerate(zip(sources, targets))
            ]
        )
        outs = [(made.at[1, here], results[0]), (made.at[2, here], results[1])]
        if not last:
            outs += [(made.at[0, here], results[2]), (low.at[here], results[3])]
        stores.append(
            [
                pltpu.make_async_copy(source, target.at[there], out_sems.at[index, at])
                for at, (source, target) in enumerate(outs)
            ]
        )
    for copies in loads:
        for copy in copies:
            copy.start()
    fixed_one = 1.0 / (1.0 - BETA_ONE**step_count)
    fixed_two = 1.0 / (1.0 - BETA_TWO**step_count)
    for index in range(blocks):
        for copy in loads[index]:
            copy.wait()
        some = pl.ds(index * block, block)
        grad = (term[some, :].astype(jnp.float32) + below_ref[some, :].astype(jnp.float32)) + above_ref[
            some, :
        ].astype(jnp.float32)
        param = held[0, some, :]
        first = BETA_ONE * held[1, some, :] + (1.0 - BETA_ONE) * grad
        second = BETA_TWO * held[2, some, :] + (1.0 - BETA_TWO) * grad * grad
        direction = first * fixed_one / (jnp.sqrt(second * fixed_two) + EPS_ADAM)
        param = param - INNER_RATE * (direction + DECAY_RATE * param)
        made[1, some, :] = first
        made[2, some, :] = second
        if last:
            made[0, some, :] = held[3, some, :] - param
        else:
            made[0, some, :] = param
            low[some, :] = param.astype(jnp.bfloat16)
        for copy in stores[index]:
            copy.start()
    if last:
        own_ref, other_ref = results[2:]
        columns = own_ref.shape[1]
        groups = other_ref.shape[0] + 1
        for step in range(groups):
            start = pl.multiple_of(lax.rem(place[0] + step, groups) * columns, 128)
            if step == 0:
                own_ref[...] = made[0, :, pl.ds(start, columns)]
            else:
                other_ref[step - 1] = made[0, :, pl.ds(start, columns)].astype(jnp.bfloat16)
    for copies in stores:
        for copy in copies:
            copy.wait()


def outer_kernel(place, own_ref, *refs, piece, groups, chained, extra):
    got_refs = refs[: groups - 1]
    arrays = refs[groups - 1 : groups + 2]
    results = refs[groups + 2 + chained + extra : groups + 6 + chained + extra]
    held, made, in_sems, out_sems = refs[-4:]
    rows, columns = own_ref.shape
    at = pl.ds(piece * rows, rows)
    start = pl.multiple_of(place[0] * columns, 128)
    sources = [arrays[0].at[at, pl.ds(start, columns)], arrays[1].at[at], arrays[2].at[at]]
    copies = [
        pltpu.make_async_copy(source, held.at[index], in_sems.at[index])
        for index, source in enumerate(sources)
    ]
    for copy in copies:
        copy.start()
    for copy in copies:
        copy.wait()
    share = own_ref[...]
    for index in range(groups - 1):
        share = share + got_refs[index][...].astype(jnp.float32)
    share = share / groups
    moment = OUTER_MOMENTUM * held[1] + share
    new_share = held[0] - OUTER_RATE * (share + OUTER_MOMENTUM * moment)
    made[0] = moment
    made[1] = share
    made[2] = AVERAGE_KEEP * held[2] + (1.0 - AVERAGE_KEEP) * new_share
    results[3][...] = new_share.astype(jnp.bfloat16)
    copies = [
        pltpu.make_async_copy(made.at[index], results[index].at[at], out_sems.at[index])
        for index in range(3)
    ]
    for copy in copies:
        copy.start()
    for copy in copies:
        copy.wait()


def join_kernel(place, *refs, piece, groups, chained):
    parts = refs[:groups]
    wide_hbm, low_hbm = refs[groups + chained : groups + chained + 2]
    wide, sems = refs[-2:]
    rows, columns = parts[0].shape
    at = pl.ds(piece * rows, rows)
    copies = []
    for step in range(groups):
        start = pl.multiple_of(lax.rem(place[0] + groups - step, groups) * columns, 128)
        wide[step] = parts[step][...].astype(jnp.float32)
        target = (at, pl.ds(start, columns))
        copies.append(pltpu.make_async_copy(wide.at[step], wide_hbm.at[target], sems.at[0, step]))
        copies.append(pltpu.make_async_copy(parts[step], low_hbm.at[target], sems.at[1, step]))
    for copy in copies:
        copy.start()
    for copy in copies:
        copy.wait()


def vmem(count):
    return [pl.BlockSpec(memory_space=pltpu.VMEM)] * count


def run_gather(lengths, picked, tokens_in, cot_in, plan):
    steps, count = picked.shape
    _, places, width = tokens_in.shape
    tokens = count + -count % 16
    padded = jnp.pad(picked, ((0, 0), (0, tokens - count)), constant_values=NOWHERE)
    shape = jax.ShapeDtypeStruct
    made = pl.pallas_call(
        functools.partial(gather_kernel, steps=steps, extra=len(plan)),
        in_specs=smem(1) + vmem(2) + anywhere(2) + smem(len(plan)),
        out_specs=vmem(2 * steps),
        out_shape=[shape((2, tokens, width), jnp.bfloat16)] * steps
        + [shape((2 * tokens, tokens), jnp.int32)] * steps,
        scratch_shapes=[
            pltpu.VMEM((steps, 2, places, width), jnp.bfloat16),
            pltpu.SemaphoreType.DMA((steps, 2)),
        ],
        compiler_params=pltpu.CompilerParams(vmem_limit_bytes=37 << 20),
        name="gather_rows",
    )(lengths, padded[:, :, None], padded[:, None, :], tokens_in, cot_in, *plan)
    return (made[:steps], made[steps:], padded[:, None, :])


def run_scatter(across, base, rows, step, chain, known):
    _, places, width = base.shape
    tokens = rows.shape[0]
    here = pl.BlockSpec((1, places, width), lambda index: (step, 0, 0))
    return pl.pallas_call(
        scatter_kernel,
        grid=(1,),
        in_specs=[
            pl.BlockSpec((1, 1, tokens), lambda index: (step, 0, 0)),
            here,
            pl.BlockSpec((tokens, width), lambda index: (0, 0)),
        ]
        + anywhere(len(chain) + len(known)),
        out_specs=[here, pl.BlockSpec((8, 128), lambda index: (0, 0))],
        out_shape=[
            jax.ShapeDtypeStruct(base.shape, base.dtype),
            jax.ShapeDtypeStruct((8, 128), jnp.float32),
        ],
        input_output_aliases=chain_aliases(3, chain),
        compiler_params=pltpu.CompilerParams(vmem_limit_bytes=56 << 20),
        cost_estimate=SMALL_COST,
        name="scatter_rows",
    )(across, base, rows, *chain, *known)


def run_attention(order, gathered, both, vec_now, mask, known):
    _, tokens, width = both.shape
    shape = jax.ShapeDtypeStruct
    return pl.pallas_call(
        functools.partial(attention_kernel, order=order, extra=len(known)),
        in_specs=anywhere(2) + vmem(2) + anywhere(len(known)),
        out_specs=vmem(4),
        out_shape=[
            shape((tokens, 3 * width), jnp.bfloat16),
            shape((2 * tokens, 128), jnp.float32),
            shape((2, tokens, width), jnp.bfloat16),
            shape((tokens, width), jnp.float32),
        ],
        scratch_shapes=[
            pltpu.VMEM((4 * width, width), jnp.bfloat16),
            pltpu.VMEM(mask.shape, jnp.int32),
            pltpu.SemaphoreType.DMA((4,)),
            pltpu.SemaphoreType.DMA,
        ],
        compiler_params=pltpu.CompilerParams(vmem_limit_bytes=37 << 20),
        cost_estimate=pl.CostEstimate(
            flops=8 * tokens * width * width, bytes_accessed=8 * width * width, transcendentals=0
        ),
        name="attention",
    )(gathered, mask, both, vec_now, *known)


def run_feed_forward(order, gathered, both, vec_now, first_sum, keep):
    _, tokens, width = both.shape
    wide = gathered.shape[0]
    shape = jax.ShapeDtypeStruct
    kept = [shape((tokens, wide - 4 * width), jnp.bfloat16)] if keep else []
    return pl.pallas_call(
        functools.partial(feed_forward_kernel, keep=keep, order=order),
        in_specs=anywhere(1) + vmem(3),
        out_specs=vmem(4 + len(kept)),
        out_shape=[
            shape((tokens, width), jnp.bfloat16),
            shape((tokens, width), jnp.bfloat16),
            shape((tokens, width), jnp.float32),
            shape((2, width), jnp.float32),
        ]
        + kept,
        scratch_shapes=[
            pltpu.VMEM((wide - 4 * width, width), jnp.bfloat16),
            pltpu.SemaphoreType.DMA(((wide - 4 * width) // width,)),
        ],
        compiler_params=pltpu.CompilerParams(vmem_limit_bytes=37 << 20),
        cost_estimate=pl.CostEstimate(
            flops=8 * tokens * (wide - 4 * width) * width,
            bytes_accessed=2 * wide * width,
            transcendentals=0,
        ),
        name="feed_forward",
    )(gathered, both, vec_now, first_sum)


def smem(count):
    return [pl.BlockSpec(memory_space=pltpu.SMEM)] * count


def anywhere(count):
    return [pl.BlockSpec(memory_space=pl.ANY)] * count


def run_attention_back(order, gathered, starts, d_attn_low, proj, lse, mask, pair, got):
    tokens, width = d_attn_low.shape
    cuts = starts.shape[0]
    shape = jax.ShapeDtypeStruct
    return pl.pallas_call(
        functools.partial(attention_back_kernel, order=order),
        in_specs=anywhere(1) + smem(1) + vmem(4) + anywhere(2),
        out_specs=anywhere(2),
        out_shape=[
            shape((tokens, 3 * width), jnp.bfloat16),
            shape((2,) + pair.shape, jnp.bfloat16),
        ],
        scratch_shapes=[
            pltpu.VMEM((width, width), jnp.bfloat16),
            pltpu.VMEM((tokens, 3 * width), jnp.bfloat16),
            pltpu.SemaphoreType.DMA((1,)),
            pltpu.SemaphoreType.DMA((2,)),
            pltpu.SemaphoreType.DMA((cuts,)),
        ],
        compiler_params=pltpu.CompilerParams(vmem_limit_bytes=37 << 20),
        cost_estimate=pl.CostEstimate(
            flops=10 * tokens * width * width, bytes_accessed=4 * width * width, transcendentals=0
        ),
        name="attention_back",
    )(gathered, starts, d_attn_low, proj, lse, mask, pair, got)


def run_input_back(order, gathered, rows, d_proj, both, vec_now, base, known):
    _, tokens, width = both.shape
    cuts = rows.shape[0]
    shape = jax.ShapeDtypeStruct
    return pl.pallas_call(
        functools.partial(
            input_back_kernel, extra=len(known), order=order
        ),
        in_specs=anywhere(1) + smem(1) + vmem(4) + anywhere(len(known)),
        out_specs=vmem(2),
        out_shape=[
            shape((tokens, width), jnp.bfloat16),
            shape((1, width), jnp.float32),
        ],
        scratch_shapes=[
            pltpu.VMEM((cuts, 3 * width // cuts, width), jnp.bfloat16),
            pltpu.SemaphoreType.DMA((cuts,)),
        ],
        compiler_params=pltpu.CompilerParams(vmem_limit_bytes=37 << 20),
        cost_estimate=SMALL_COST,
        name="input_back",
    )(gathered, rows, d_proj, both, vec_now, base, *known)


def run_line(moves, below, above, terms, step, piece, passed, known):
    shape = jax.ShapeDtypeStruct(below.shape, jnp.bfloat16)
    return pl.pallas_call(
        functools.partial(line_kernel, step=step, piece=piece, passed=len(passed)),
        in_specs=smem(1) + vmem(2) + anywhere(1) + vmem(len(passed)) + anywhere(len(known)),
        out_specs=vmem(2 + len(passed)),
        out_shape=[shape, shape]
        + [jax.ShapeDtypeStruct(values.shape, values.dtype) for values in passed],
        scratch_shapes=[
            pltpu.VMEM((2,) + below.shape, jnp.bfloat16),
            pltpu.SemaphoreType.DMA((2,)),
        ],
        compiler_params=pltpu.CompilerParams(vmem_limit_bytes=16 << 20),
        cost_estimate=pl.CostEstimate(
            flops=LINE_FLOPS, bytes_accessed=6 * below.size * 2, transcendentals=0
        ),
        name="line",
    )(moves, below, above, terms, *passed, *known)


def chain_aliases(first, chain):
    return {first + index: index for index in range(len(chain))}


def run_update(place, below, above, terms, states, piece, step_count, last, groups, chain, known):
    rows, width = below.shape
    own = terms.shape[0] - PIECES + piece
    shape = jax.ShapeDtypeStruct
    wide = shape(states[0].shape, jnp.float32)
    columns = width // groups
    if last:
        out_shape = [wide, wide, shape((rows, columns), jnp.float32)]
        out_shape.append(shape((groups - 1, rows, columns), jnp.bfloat16))
        out_specs = anywhere(2) + vmem(2)
    else:
        out_shape = [wide, wide, wide, shape(states[0].shape, jnp.bfloat16)]
        out_specs = anywhere(4)
    operands = (place, below, above, terms, *states, *chain, *known)
    return pl.pallas_call(
        functools.partial(
            update_kernel,
            piece=piece,
            own=own,
            step_count=step_count,
            last=last,
            chained=len(chain),
            extra=len(known),
        ),
        in_specs=smem(1) + vmem(2) + anywhere(len(operands) - 3),
        out_specs=out_specs,
        out_shape=out_shape,
        scratch_shapes=[
            pltpu.VMEM((len(states), rows, width), jnp.float32),
            pltpu.VMEM((rows, width), jnp.bfloat16),
            pltpu.VMEM((3, rows, width), jnp.float32),
            pltpu.VMEM((rows, width), jnp.bfloat16),
            pltpu.SemaphoreType.DMA((4, len(states) + 1)),
            pltpu.SemaphoreType.DMA((4, 4)),
        ],
        input_output_aliases=chain_aliases(4 + len(states), chain),
        compiler_params=pltpu.CompilerParams(vmem_limit_bytes=52 << 20),
        cost_estimate=pl.CostEstimate(
            flops=LINE_FLOPS, bytes_accessed=24 * rows * width, transcendentals=0
        ),
        name="update",
    )(*operands)


def run_outer(place, own, got, arrays, piece, chain, known):
    rows, columns = own.shape
    shape = jax.ShapeDtypeStruct
    narrow = shape(arrays[1].shape, jnp.float32)
    operands = (place, own, *got, *arrays, *chain, *known)
    return pl.pallas_call(
        functools.partial(
            outer_kernel,
            piece=piece,
            groups=len(got) + 1,
            chained=len(chain),
            extra=len(known),
        ),
        in_specs=smem(1) + vmem(1 + len(got)) + anywhere(len(operands) - 2 - len(got)),
        out_specs=anywhere(3) + vmem(1),
        out_shape=[narrow] * 3 + [shape(own.shape, jnp.bfloat16)],
        scratch_shapes=[
            pltpu.VMEM((3, rows, columns), jnp.float32),
            pltpu.VMEM((3, rows, columns), jnp.float32),
            pltpu.SemaphoreType.DMA((3,)),
            pltpu.SemaphoreType.DMA((3,)),
        ],
        input_output_aliases=chain_aliases(5 + len(got), chain),
        compiler_params=pltpu.CompilerParams(vmem_limit_bytes=52 << 20),
        cost_estimate=pl.CostEstimate(
            flops=LINE_FLOPS, bytes_accessed=24 * rows * columns, transcendentals=0
        ),
        name="outer",
    )(*operands)


def run_join(place, parts, like, piece, chain):
    rows, columns = parts[0].shape
    groups = len(parts)
    operands = (place, *parts, *chain)
    return pl.pallas_call(
        functools.partial(join_kernel, piece=piece, groups=groups, chained=len(chain)),
        in_specs=smem(1) + vmem(groups) + anywhere(len(chain)),
        out_specs=anywhere(2),
        out_shape=[
            jax.ShapeDtypeStruct(like.shape, jnp.float32),
            jax.ShapeDtypeStruct(like.shape, jnp.bfloat16),
        ],
        scratch_shapes=[
            pltpu.VMEM((groups, rows, columns), jnp.float32),
            pltpu.SemaphoreType.DMA((2, groups)),
        ],
        input_output_aliases=chain_aliases(1 + groups, chain),
        compiler_params=pltpu.CompilerParams(vmem_limit_bytes=52 << 20),
        cost_estimate=pl.CostEstimate(
            flops=LINE_FLOPS, bytes_accessed=12 * rows * columns * groups, transcendentals=0
        ),
        name="join",
    )(*operands)


def run_products(
    info, needs, gathered, proj_parts, attn_parts, plane_h1, plane_d_down, pairs, piece, known
):
    count = info.shape[0]
    sources, tokens, width = plane_h1.shape
    shape = jax.ShapeDtypeStruct((count, piece, width), jnp.bfloat16)
    made = pl.pallas_call(
        functools.partial(feed_forward_products_kernel, extra=len(attn_parts)),
        in_specs=smem(2) + anywhere(2 + len(pairs) + len(attn_parts)),
        out_specs=vmem(1)[0],
        out_shape=shape,
        scratch_shapes=[
            pltpu.VMEM((2, sources * tokens, width), jnp.bfloat16),
            pltpu.VMEM((count, piece, width), jnp.bfloat16),
            pltpu.VMEM((count, piece, width), jnp.bfloat16),
            pltpu.SemaphoreType.DMA((2, sources)),
            pltpu.SemaphoreType.DMA((count,)),
            pltpu.SemaphoreType.DMA((count,)),
        ],
        compiler_params=pltpu.CompilerParams(vmem_limit_bytes=37 << 20),
        cost_estimate=pl.CostEstimate(
            flops=6 * count * sources * tokens * piece * width,
            bytes_accessed=6 * count * piece * width,
            transcendentals=0,
        ),
        name="feed_forward_products",
    )(info, needs, gathered, plane_d_down, *pairs, *attn_parts)
    near = made
    for first, last in ((0, PIECES), (PIECES, count)):
        known = () if first else known
        operands = (info, needs, plane_h1, *proj_parts, *attn_parts, *pairs, *known, near, made)
        blocks = last - first
        found = pl.pallas_call(
            functools.partial(
                attention_products_kernel,
                sources=sources,
                extra=len(known),
                first=first,
                last=last,
            ),
            in_specs=smem(2) + anywhere(len(operands) - 2),
            out_specs=anywhere(1)[0],
            out_shape=jax.ShapeDtypeStruct((count if first else last, piece, width), jnp.bfloat16),
            scratch_shapes=[
                pltpu.VMEM((2, sources * tokens, width), jnp.bfloat16),
                pltpu.VMEM((sources * tokens, blocks * piece), jnp.bfloat16),
                pltpu.VMEM((sources * tokens, width), jnp.bfloat16),
                pltpu.VMEM((blocks, piece, width), jnp.bfloat16),
                pltpu.SemaphoreType.DMA((2, sources)),
                pltpu.SemaphoreType.DMA((2, sources)),
                pltpu.SemaphoreType.DMA((count,)),
            ],
            input_output_aliases={len(operands) - 1: 0} if first else {},
            compiler_params=pltpu.CompilerParams(vmem_limit_bytes=16 << 20),
            cost_estimate=SMALL_COST,
            name="attention_products",
        )(*operands)
        if first:
            return (near, found)
        near = found


def pad_rows(rows):
    return jnp.pad(rows, ((0, -rows.shape[0] % 16), (0, 0)))


def swap(values, axis, delta):
    size = lax.axis_size(axis)
    return lax.ppermute(values, axis, [(i, i ^ delta) for i in range(size)])


def sum_over(values, axes):
    for axis in axes:
        parts = [values]
        parts += [swap(values, axis, delta) for delta in range(1, lax.axis_size(axis))]
        while len(parts) > 1:
            parts = [parts[at] + parts[at + 1] for at in range(0, len(parts), 2)]
        values = parts[0]
    return values


def gathered_rows(values):
    return lax.all_gather(pad_rows(values), ("dp", "fsdp"), axis=0, tiled=False)


def line_order(line):
    due = np.zeros((line, line), np.int32)
    for here in range(line):
        for there in range(line):
            if there > here:
                due[here, there] = line - 1 - there + here
            elif there < here:
                due[here, there] = there - here + line - 1
            else:
                due[here, there] = line
    return np.argsort(due, axis=1, kind="stable").astype(np.int32)


def line_slots(line, order):
    ups = np.zeros((line - 1, line), np.int32)
    downs = np.zeros((line - 1, line), np.int32)
    for step in range(line - 1):
        for here in range(line):
            if here <= step:
                ups[step, here] = list(order[here]).index(line - 1 - step + here)
            if line - 1 - here <= step:
                downs[step, here] = list(order[here]).index(step - (line - 1) + here)
    return ups, downs


def added(*parts):
    return sum(part.astype(jnp.float32) for part in parts)


def due_after(value, *marks):
    flag = sum(mark[(-1,) * mark.ndim].astype(jnp.float32) for mark in marks)
    return value + (flag != flag).astype(value.dtype)


def plane_order(planes):
    deltas = [0]
    bit = planes // 2
    while bit >= 1:
        deltas = deltas + [delta ^ bit for delta in deltas]
        bit //= 2
    return deltas


def plane_gather(values):
    values = values[None]
    bit = lax.axis_size("fsdp") // 2
    while bit >= 1:
        values = jnp.concatenate([values, swap(values, "fsdp", bit)], axis=0)
        bit //= 2
    return values


def plane_operands(plane_rows, vec_now):
    sel_rows = plane_rows[:, 0].astype(jnp.float32)
    cot_rows = plane_rows[:, 1].astype(jnp.float32)
    gate = jax.nn.sigmoid(jnp.sum(sel_rows * vec_now[2], axis=-1, keepdims=True))
    inverse = lax.rsqrt(row_mean(sel_rows * sel_rows) + EPS_NORM)
    h1 = (sel_rows * inverse * vec_now[0]).astype(jnp.bfloat16)
    return (h1, (gate * cot_rows).astype(jnp.bfloat16))


def send_to(target, values):
    planes = lax.axis_size("fsdp")
    return [values] + [
        lax.ppermute(values, "fsdp", [(target ^ delta, target)]) for delta in plane_order(planes)[1:]
    ]


def gradient_plan(shard_rows, model_width, columns):
    planes, line = lax.axis_size("fsdp"), lax.axis_size("dp")
    plane, here = lax.axis_index("fsdp"), lax.axis_index("dp")
    hidden_units = (columns - 4 * model_width) // 2
    edges = (3 * model_width, 4 * model_width, 4 * model_width + hidden_units)

    def kind_of(row):
        return sum((row >= edge).astype(jnp.int32) for edge in edges)

    piece = shard_rows // PIECES
    theres = jnp.asarray(line_order(line))[here]
    rows = (plane * line + theres)[:, None] * shard_rows + jnp.arange(PIECES) * piece
    rows = rows.reshape(-1)
    kinds = kind_of(rows)
    at = rows - 3 * model_width
    order = (planes, line, shard_rows)
    uppers = gathered_row(jnp.where(kinds == 2, rows, rows - hidden_units), order)
    lowers = gathered_row(jnp.minimum(rows + hidden_units, columns - piece), order)
    info = jnp.stack([kinds, jnp.where(kinds >= 2, uppers, at), lowers], axis=1)
    low, high = kind_of(plane * line * shard_rows), kind_of((plane + 1) * line * shard_rows - 1)
    ff = (high >= 2).astype(jnp.int32)
    has_proj = (low == 0).astype(jnp.int32)
    has_attn = ((low <= 1) & (high >= 1)).astype(jnp.int32)
    moves = jnp.asarray(np.stack(line_slots(line, line_order(line)), axis=-1))[:, here]
    return (info.astype(jnp.int32), jnp.stack([has_proj, has_attn, ff, ff]), moves)


def gradient_starts(shard_rows, model_width, split):
    line, here = lax.axis_size("dp"), lax.axis_index("dp")
    if split:
        return jnp.asarray(line_order(line) * shard_rows)[here]
    return jnp.arange(4, dtype=jnp.int32) * (3 * model_width // 4)


def in_planes(shard_rows, model_width):
    line = lax.axis_size("dp")
    return (shard_rows // PIECES) % 128 == 0 and line * shard_rows == 3 * model_width


def gradient_whole(columns, operands):
    hidden_units = columns[2].shape[1] // 2
    factors = (*columns[:2], columns[2][:, :hidden_units], columns[2][:, hidden_units:])
    products = [tn(factor, operand) for factor, operand in zip(factors, operands)]
    low = jnp.concatenate(products, axis=0).astype(jnp.bfloat16)
    share = lax.psum_scatter(low, ("fsdp", "dp"), scatter_dimension=0, tiled=True)
    return share.astype(jnp.float32)


def plane_terms(
    gathered, d_proj, d_attn_low, pairs, plane_h1, plane_d_down, info, needs, shard_rows, known
):
    attn_parts = send_to(1, d_attn_low)
    pairs = [pairs]
    bit = lax.axis_size("fsdp") // 4
    while bit >= 1:
        pairs.append(swap(jnp.concatenate(pairs, axis=0), "fsdp", bit))
        bit //= 2
    return run_products(
        info,
        needs,
        gathered,
        send_to(0, d_proj),
        attn_parts,
        plane_h1,
        plane_d_down,
        pairs,
        shard_rows // PIECES,
        known,
    )


def gradient_share(near, terms, moves, passed, meanwhile):
    line = lax.axis_size("dp")
    below, above = [None] * PIECES, [None] * PIECES
    for step in range(line - 1):
        for index in range(PIECES):
            if step == 0:
                up = down = near[index]
            else:
                due = known[index] if step == line - 2 else ()
                given = passed if step == 1 and index == 0 else ()
                up, down, *given = run_line(
                    moves, below[index], above[index], terms, step, index, given, due
                )
                if step == 1 and index == 0:
                    known = meanwhile(up, given)
            below[index] = lax.ppermute(up, "dp", [(p, p + 1) for p in range(step + 1)])
            above[index] = lax.ppermute(
                down, "dp", [(line - 1 - p, line - 2 - p) for p in range(step + 1)]
            )
    return (below, above)


def adamw(param, grad, first, second, step_count, rate, decay):
    first = BETA_ONE * first + (1.0 - BETA_ONE) * grad
    second = BETA_TWO * second + (1.0 - BETA_TWO) * grad * grad
    fixed_one = 1.0 - BETA_ONE**step_count
    fixed_two = 1.0 - BETA_TWO**step_count
    direction = first / fixed_one / (jnp.sqrt(second / fixed_two) + EPS_ADAM)
    return (param - rate * (direction + decay * param), first, second)


def vector_rates():
    return jnp.array([[0.1], [0.1], [0.02]], dtype=jnp.float32)


def outer_whole(weights, master, outer_moment, smoothed_matrix_mean):
    groups = lax.axis_size("grp")
    here = lax.axis_index("grp")
    delta = weights - master
    col_width = weights.shape[1] // groups
    col_start = here * col_width
    diff_share = lax.dynamic_slice_in_dim(delta, col_start, col_width, 1)
    for step in range(1, groups):
        there = lax.rem(here + step, groups)
        part = lax.dynamic_slice_in_dim(delta, there * col_width, col_width, 1)
        diff_share = diff_share + shift_group(part.astype(jnp.bfloat16), step).astype(jnp.float32)
    diff_share = diff_share / groups
    moment_share = OUTER_MOMENTUM * outer_moment + diff_share
    base_share = lax.dynamic_slice_in_dim(weights, col_start, col_width, 1)
    new_share = base_share - OUTER_RATE * (diff_share + OUTER_MOMENTUM * moment_share)
    low_share = new_share.astype(jnp.bfloat16)
    weights_low = jnp.zeros(weights.shape, jnp.bfloat16)
    for step in range(groups):
        there = lax.rem(here + groups - step, groups)
        part = shift_group(low_share, step) if step else low_share
        weights_low = lax.dynamic_update_slice_in_dim(weights_low, part, there * col_width, 1)
    average_new = AVERAGE_KEEP * smoothed_matrix_mean + (1.0 - AVERAGE_KEEP) * new_share
    return (weights_low.astype(jnp.float32), weights_low, moment_share, diff_share, average_new)


def shift_group(values, step):
    groups = lax.axis_size("grp")
    return lax.ppermute(values, "grp", [(i, (i + step) % groups) for i in range(groups)])


def on_device(
    tokens,
    cotangent,
    lengths,
    selected,
    weights,
    vectors,
    first_moment,
    second_moment,
    vec_first,
    vec_second,
    outer_moment,
    smoothed_matrix_mean,
    vec_outer,
    vec_average,
):
    master = weights
    vec_now = vectors
    first_now = first_moment[0]
    second_now = second_moment[0]
    vfirst_now = vec_first[0]
    vsecond_now = vec_second[0]
    model_width = tokens.shape[2]
    planes, line = lax.axis_size("fsdp"), lax.axis_size("dp")
    shard_rows = weights.shape[0]
    info, needs, moves = gradient_plan(shard_rows, model_width, weights.shape[0] * planes * line)
    split = in_planes(shard_rows, model_width)
    starts = gradient_starts(shard_rows, model_width, split)
    order = (planes, line, shard_rows)
    weight_starts = gathered_row(starts, order)
    plan = (info, needs, moves, starts, weight_starts)
    boths, masks, across = run_gather(lengths[:, 0], selected[:, 0], tokens, cotangent, plan)
    plane_rows = plane_gather(boths[0])
    groups = lax.axis_size("grp")
    place = lax.axis_index("grp").astype(jnp.int32)[None]
    shard_low = master.astype(jnp.bfloat16)
    activations, input_grad, outers = [], [], []
    for inner_step in range(INNER):
        both, mask = boths[inner_step], masks[inner_step]
        gathered = lax.all_gather(shard_low, ("dp", "fsdp"), axis=0, tiled=True)
        plane_h1, plane_d_down = plane_operands(plane_rows, vec_now)
        proj, lse, pair, first_sum = run_attention(
            order,
            gathered,
            both,
            vec_now,
            mask,
            [plane_h1, plane_d_down, *activations[1:], *input_grad[1:]],
        )
        d_attn_low, out_rows, base, grad_two, *kept = run_feed_forward(
            order, gathered, both, vec_now, first_sum, not split
        )
        got = swap(pair[None], "fsdp", planes // 2)
        d_proj, pairs = run_attention_back(
            order, gathered, starts, d_attn_low, proj, lse, mask, pair, got
        )
        following = list(boths[inner_step + 1 : inner_step + 2])
        last = not following
        step_count = STEP + inner_step
        results = []

        def input_step(marks):
            d_rows, grad_one = run_input_back(
                None if split else order, gathered, weight_starts, d_proj, both, vec_now, base, marks
            )
            results.append(jnp.concatenate([grad_one, grad_two], axis=0))
            return d_rows

        def scatter_step(d_rows, marks):
            activations[:] = run_scatter(
                across, tokens, out_rows, inner_step, activations[:1], marks
            )
            input_grad[:] = run_scatter(
                across, cotangent, d_rows, inner_step, input_grad[:1], marks
            )

        if split and last:
            d_rows = input_step([])
            results[0] = gathered_rows(results[0])

        def meanwhile(mark, passed):
            if not last:
                results.append(plane_gather(passed[0]))
                return (results[-1:], (), ())
            return ((), (), ())

        if split:
            near, terms = plane_terms(
                gathered,
                d_proj,
                d_attn_low,
                pairs,
                plane_h1,
                plane_d_down,
                info,
                needs,
                shard_rows,
                [d_rows] if last else (),
            )
            below, above = gradient_share(near, terms, moves, following, meanwhile)
            grad_mark = below[-1]
        else:
            grad_mark = gradient_whole(
                (d_proj, d_attn_low, *kept), (plane_h1[0], pair[0], pair[1], plane_d_down[0])
            )
            results.extend(plane_gather(values) for values in following)
        if split and last:
            made = []
            for index in range(PIECES):
                made.append(
                    run_update(
                        place,
                        below[index],
                        above[index],
                        terms,
                        (master, first_now, second_now, weights),
                        index,
                        step_count,
                        last,
                        groups,
                        made[-1][:2] if index else (),
                        [outers[0][3], input_grad[1]]
                        if index == PIECES - 1
                        else activations[1:],
                    )
                )
                own, other = made[-1][2:]
                if index == 0:
                    scatter_step(d_rows, [own])
                outers.append(
                    run_outer(
                        place,
                        own,
                        [shift_group(other[step - 1], step) for step in range(1, groups)],
                        (weights, outer_moment, smoothed_matrix_mean),
                        index,
                        outers[-1][:3] if index else (),
                        [],
                    )
                )
            first_now, second_now = made[-1][:2]
        else:
            grad_shard = grad_mark
            if split:
                own = (line - 1) * PIECES
                grad_shard = jnp.concatenate(
                    [
                        added(terms[own + index], below[index], above[index])
                        for index in range(PIECES)
                    ],
                    axis=0,
                )
            master, first_now, second_now = adamw(
                master, grad_shard, first_now, second_now, step_count, INNER_RATE, DECAY_RATE
            )
            shard_low = master.astype(jnp.bfloat16)
        if not last:
            plane_rows = results.pop()
        if split and last:
            grad_vec = jnp.sum(due_after(results[0][:, : vec_now.shape[0]], made[0][2]), axis=0)
            vec_now, vfirst_now, vsecond_now = adamw(
                vec_now, grad_vec, vfirst_now, vsecond_now, step_count, vector_rates(), 0.0
            )
            vec_diff = sum_over(vectors - vec_now, ("grp",)) / groups
        else:
            scatter_step(input_step([grad_mark]), [grad_mark])
            grad_vec = sum_over(due_after(results[0], grad_mark), ("fsdp", "dp"))
            vec_now, vfirst_now, vsecond_now = adamw(
                vec_now, grad_vec, vfirst_now, vsecond_now, step_count, vector_rates(), 0.0
            )
    if split:
        joined = []
        for index in range(PIECES):
            low = outers[index][3]
            parts = [low] + [shift_group(low, step) for step in range(1, groups)]
            joined = run_join(place, parts, weights, index, joined)
        weights_new, weights_low = joined
        outer_new, diff_new, average_new = outers[-1][:3]
    else:
        weights_new, weights_low, outer_new, diff_new, average_new = outer_whole(
            weights, master, outer_moment, smoothed_matrix_mean
        )
    if not split:
        vec_diff = sum_over(vectors - vec_now, ("grp",)) / groups
    vec_moment = OUTER_MOMENTUM * vec_outer + vec_diff
    vectors_new = vectors - OUTER_RATE * (vec_diff + OUTER_MOMENTUM * vec_moment)
    vec_average_new = AVERAGE_KEEP * vec_average + (1.0 - AVERAGE_KEEP) * vectors_new
    return (
        activations[0],
        input_grad[0],
        weights_new,
        weights_low,
        first_now[None],
        second_now[None],
        outer_new,
        diff_new,
        average_new,
        vectors_new,
        vfirst_now[None],
        vsecond_now[None, :2],
        vsecond_now[None, 2],
        vec_moment,
        vec_average_new,
    )


def solution(mesh):
    placed = (
        P(None, ("grp", "fsdp", "dp"), None),
        P(None, ("grp", "fsdp", "dp"), None),
        P(None, ("grp", "fsdp", "dp"), None),
        P(None, ("grp", "fsdp", "dp"), None),
        P(("fsdp", "dp"), None),
        P(),
        P("grp", ("fsdp", "dp"), None),
        P("grp", ("fsdp", "dp"), None),
        P("grp", None, None),
        P("grp", None, None),
        P(("fsdp", "dp"), "grp"),
        P(("fsdp", "dp"), "grp"),
        P(),
        P(),
    )
    return jax.shard_map(
        on_device,
        mesh=mesh,
        in_specs=placed,
        out_specs=(
            P(None, ("grp", "fsdp", "dp"), None),
            P(None, ("grp", "fsdp", "dp"), None),
            P(("fsdp", "dp"), None),
            P(("fsdp", "dp"), None),
            P("grp", ("fsdp", "dp"), None),
            P("grp", ("fsdp", "dp"), None),
            P(("fsdp", "dp"), "grp"),
            P(("fsdp", "dp"), "grp"),
            P(("fsdp", "dp"), "grp"),
            P(),
            P("grp", None, None),
            P("grp", None, None),
            P("grp", None),
            P(),
            P(),
        ),
        check_vma=False,
    )
```

```python
import functools
import math

import jax
import jax.numpy as jnp
import numpy as np
from jax import lax
from jax.experimental import pallas as pl
from jax.experimental.pallas import tpu as pltpu
from jax.sharding import PartitionSpec as P

HEAD = 64
INNER = 2
STEP = 5


EPS_NORM = 1e-06
EPS_ADAM = 1e-08
BETA_ONE = 0.9
BETA_TWO = 0.95
INNER_RATE = 0.03
DECAY_RATE = 0.1
OUTER_RATE = 0.7
OUTER_MOMENTUM = 0.9
AVERAGE_KEEP = 0.9
GELU_SCALE = float(np.sqrt(2.0 / np.pi))
GELU_CUBE = 0.044715
PIECES = 3
LINE_FLOPS = 10**10
SMALL_COST = pl.CostEstimate(flops=10**6, bytes_accessed=10**5, transcendentals=0)
NOWHERE = 1 << 20


def nt(left, right):
    return lax.dot_general(
        left, right, (((1,), (1,)), ((), ())), preferred_element_type=jnp.float32
    )


def nn(left, right):
    return lax.dot_general(
        left, right, (((1,), (0,)), ((), ())), preferred_element_type=jnp.float32
    )


def tn(left, right):
    return lax.dot_general(
        left, right, (((0,), (0,)), ((), ())), preferred_element_type=jnp.float32
    )


def gathered_row(row, order):
    planes, line, shard_rows = order
    shard = row // shard_rows
    return ((shard % line) * planes + shard // line) * shard_rows + row % shard_rows


class WeightCopy:
    def __init__(self, weights, held, sem, source, target, rows, order):
        unit = math.gcd(order[2], rows)
        self.parts = [
            pltpu.make_async_copy(
                weights.at[pl.ds(gathered_row(source * rows + at, order), unit)],
                held.at[pl.ds(target * rows + at, unit)],
                sem,
            )
            for at in range(0, rows, unit)
        ]
        self.whole = pltpu.make_async_copy(
            weights.at[pl.ds(0, rows)], held.at[pl.ds(target * rows, rows)], sem
        )

    def start(self):
        for part in self.parts:
            part.start()

    def wait(self):
        self.whole.wait()


def weight_copies(weights, held, sems, sources, rows, order):
    return [
        WeightCopy(weights, held, sems.at[target], source, target, rows, order)
        for target, source in enumerate(sources)
    ]


def two_heads(values):
    low = lax.broadcasted_iota(jnp.int32, values.shape, 1) < HEAD
    zero = jnp.zeros_like(values)
    return jnp.concatenate([jnp.where(low, values, zero), jnp.where(low, zero, values)], axis=0)


def one_block(values):
    rows = values.shape[0] // 2
    low = lax.broadcasted_iota(jnp.int32, (rows, values.shape[1]), 1) < HEAD
    return jnp.where(low, values[:rows], values[rows:])


def row_mean(values):
    return jnp.mean(values, axis=-1, keepdims=True)


def gelu_and_slope(pre):
    square = pre * pre
    tanh = jnp.tanh(GELU_SCALE * pre * (1.0 + GELU_CUBE * square))
    half = 0.5 * (1.0 + tanh)
    slope = half + 0.5 * pre * (1.0 - tanh * tanh) * (
        GELU_SCALE * (1.0 + 3.0 * GELU_CUBE * square)
    )
    return ((pre * half).astype(jnp.bfloat16), slope)


def gather_kernel(lengths, picked_ref, across_ref, tokens_hbm, cot_hbm, *refs, steps, extra):
    refs = refs[extra:]
    both_refs, mask_refs = refs[:steps], refs[steps : 2 * steps]
    held, sems = refs[2 * steps :]
    copies = [
        [
            pltpu.make_async_copy(source.at[step], held.at[step, at], sems.at[step, at])
            for at, source in enumerate((tokens_hbm, cot_hbm))
        ]
        for step in range(steps)
    ]
    for some in copies:
        for copy in some:
            copy.start()
    for step in range(steps):
        down, across = picked_ref[step], across_ref[step]
        segment_down, segment_across = jnp.zeros_like(down), jnp.zeros_like(across)
        end = jnp.int32(0)
        for slot in range(lengths.shape[1]):
            end = end + lengths[step, slot]
            segment_down += (down >= end).astype(jnp.int32)
            segment_across += (across >= end).astype(jnp.int32)
        allowed = (segment_down == segment_across) & (across <= down)
        allowed = allowed.astype(jnp.int32)
        mask_refs[step][...] = jnp.concatenate([allowed, allowed], axis=0)
        places = lax.broadcasted_iota(jnp.int32, (down.shape[0], held.shape[2]), 1)
        chosen = jnp.where(places == down, 1.0, 0.0).astype(jnp.bfloat16)
        for at in range(2):
            copies[step][at].wait()
            both_refs[step][at] = nn(chosen, held[step, at]).astype(jnp.bfloat16)


def scatter_kernel(across_ref, base_ref, rows_ref, *refs):
    out_ref, mark_ref = refs[-2:]
    mark_ref[...] = jnp.zeros_like(mark_ref)
    base = base_ref[0]
    across = across_ref[0]
    places = lax.broadcasted_iota(jnp.int32, (base.shape[0], across.shape[1]), 0)
    chosen = jnp.where(places == across, 1.0, 0.0)
    replaced = jnp.sum(chosen, axis=-1, keepdims=True) > 0.0
    rows = nn(chosen.astype(jnp.bfloat16), rows_ref[...]).astype(jnp.bfloat16)
    out_ref[0] = jnp.where(replaced, rows, base)


def attention_kernel(
    weights, mask_hbm, both_ref, vec_ref, *refs, order, extra
):
    proj_ref, lse_ref, pair_ref, first_ref, held, mask_ref, sems, mask_sem = refs[extra:]
    rows_ref = both_ref.at[0]
    width = both_ref.shape[2]
    copies = weight_copies(weights, held, sems, range(4), width, order)
    mask_copy = pltpu.make_async_copy(mask_hbm, mask_ref, mask_sem)
    mask_copy.start()
    for copy in copies:
        copy.start()
    xs = rows_ref[...].astype(jnp.float32)
    h1 = (xs * lax.rsqrt(row_mean(xs * xs) + EPS_NORM) * vec_ref[0:1, :]).astype(jnp.bfloat16)
    for index in range(3):
        copies[index].wait()
        proj_ref[:, index * width : (index + 1) * width] = nt(
            h1, held[pl.ds(index * width, width), :]
        ).astype(jnp.bfloat16)
    mask_copy.wait()
    allowed = mask_ref[...] > 0
    lane = lax.broadcasted_iota(jnp.int32, lse_ref.shape, 1)
    lse = jnp.zeros(lse_ref.shape, jnp.float32)
    for pair in range(width // 128):
        at = pair * 128
        queries = two_heads(proj_ref[:, at : at + 128])
        keys = proj_ref[:, width + at : width + at + 128]
        values = proj_ref[:, 2 * width + at : 2 * width + at + 128]
        scores = jnp.where(allowed, nt(queries, keys) * HEAD ** (-0.5), -1e30)
        top = jnp.max(scores, axis=-1, keepdims=True)
        total = top + jnp.log(jnp.sum(jnp.exp(scores - top), axis=-1, keepdims=True))
        lse = jnp.where(lane == pair, total, lse)
        probs_low = jnp.exp(scores - total).astype(jnp.bfloat16)
        pair_ref[0, :, at : at + 128] = one_block(nn(probs_low, values)).astype(jnp.bfloat16)
    lse_ref[...] = lse
    copies[3].wait()
    first_sum = xs + nt(pair_ref[0], held[pl.ds(3 * width, width), :])
    first_ref[...] = first_sum
    inverse = lax.rsqrt(row_mean(first_sum * first_sum) + EPS_NORM)
    pair_ref[1] = (first_sum * inverse * vec_ref[1:2, :]).astype(jnp.bfloat16)


def feed_forward_kernel(
    weights,
    both_ref,
    vec_ref,
    first_ref,
    d_attn_ref,
    out_ref,
    base_ref,
    grad_ref,
    *refs,
    keep,
    order,
):
    held, sems = refs[-2:]
    rows_ref, cot_ref = both_ref.at[0], both_ref.at[1]
    width = both_ref.shape[2]
    hidden = (weights.shape[0] - 4 * width) // 2
    parts = hidden // width
    matrices = []
    for part in range(parts):
        matrices += [4 + part, 4 + parts + part]
    copies = weight_copies(weights, held, sems, matrices, width, order)
    for copy in copies:
        copy.start()

    def matrix(index):
        return held[pl.ds(index * width, width), :]

    xs = rows_ref[...].astype(jnp.float32)
    cot = cot_ref[...].astype(jnp.float32)
    gate = jax.nn.sigmoid(jnp.sum(xs * vec_ref[2:3, :], axis=-1, keepdims=True))
    first_sum = first_ref[...]
    inverse = lax.rsqrt(row_mean(first_sum * first_sum) + EPS_NORM)
    normed = first_sum * inverse
    h2 = (normed * vec_ref[1:2, :]).astype(jnp.bfloat16)
    d_branch = gate * cot
    d_down = d_branch.astype(jnp.bfloat16)
    branch = first_sum - xs
    d_h2 = jnp.zeros_like(branch)
    for part in range(parts):
        at = part * width
        copies[2 * part].wait()
        act, slope = gelu_and_slope(nt(h2, matrix(2 * part)))
        copies[2 * part + 1].wait()
        branch = branch + nn(act, matrix(2 * part + 1))
        d_pre = (nt(d_down, matrix(2 * part + 1)) * slope).astype(jnp.bfloat16)
        if keep:
            refs[0][:, at : at + width] = d_pre
            refs[0][:, at + hidden : at + hidden + width] = act
        d_h2 = d_h2 + nn(d_pre, matrix(2 * part))
    out_ref[...] = (xs + gate * branch).astype(jnp.bfloat16)
    d_logit = jnp.sum(cot * branch, axis=-1, keepdims=True) * gate * (1.0 - gate)
    grad_ref[0:1, :] = jnp.sum(d_h2 * normed, axis=0, keepdims=True)
    grad_ref[1:2, :] = jnp.sum(d_logit * xs, axis=0, keepdims=True)
    d_normed = d_h2 * vec_ref[1:2, :]
    d_first = inverse * (d_normed - normed * row_mean(d_normed * normed))
    d_attn_ref[...] = (d_branch + d_first).astype(jnp.bfloat16)
    base_ref[...] = cot + d_first + d_logit * vec_ref[2:3, :]


def attention_back_kernel(
    weights,
    starts,
    d_attn_ref,
    proj_ref,
    lse_ref,
    mask_ref,
    pair_hbm,
    got_hbm,
    cuts_hbm,
    pairs_hbm,
    held,
    late_ref,
    weight_sems,
    pair_sems,
    cut_sems,
    *,
    order,
):
    width = held.shape[1]
    copies = weight_copies(weights, held, weight_sems, [3], width, order)
    pair_copies = [
        pltpu.make_async_copy(pair_hbm, pairs_hbm.at[0], pair_sems.at[0]),
        pltpu.make_async_copy(got_hbm.at[0], pairs_hbm.at[1], pair_sems.at[1]),
    ]
    for copy in copies + pair_copies:
        copy.start()
    copies[0].wait()
    d_mixed = nn(d_attn_ref[...], held[pl.ds(0, width), :]).astype(jnp.bfloat16)
    allowed = mask_ref[...] > 0
    for pair in range(width // 128):
        at = pair * 128
        queries = two_heads(proj_ref[:, at : at + 128])
        keys = proj_ref[:, width + at : width + at + 128]
        values = proj_ref[:, 2 * width + at : 2 * width + at + 128]
        d_pair = two_heads(d_mixed[:, at : at + 128])
        scores = jnp.where(allowed, nt(queries, keys) * HEAD ** (-0.5), -1e30)
        probs = jnp.exp(scores - lse_ref[:, pair : pair + 1])
        probs_low = probs.astype(jnp.bfloat16)
        d_probs = nt(d_pair, values)
        d_scores = probs * (d_probs - jnp.sum(d_probs * probs, axis=-1, keepdims=True))
        d_scores = d_scores.astype(jnp.bfloat16)
        late_ref[:, at : at + 128] = (one_block(nn(d_scores, keys)) * HEAD ** (-0.5)).astype(
            jnp.bfloat16
        )
        late_ref[:, width + at : width + at + 128] = (
            tn(d_scores, queries) * HEAD ** (-0.5)
        ).astype(jnp.bfloat16)
        late_ref[:, 2 * width + at : 2 * width + at + 128] = tn(probs_low, d_pair).astype(
            jnp.bfloat16
        )
    cuts = starts.shape[0]
    span = late_ref.shape[1] // cuts
    cut_copies = []
    for cut in range(cuts):
        start = pl.multiple_of(starts[cut], 128)
        cut_copies.append(
            pltpu.make_async_copy(
                late_ref.at[:, pl.ds(start, span)],
                cuts_hbm.at[:, pl.ds(cut * span, span)],
                cut_sems.at[cut],
            )
        )
    for copy in cut_copies:
        copy.start()
    for copy in cut_copies + pair_copies:
        copy.wait()


def input_back_kernel(
    weights, rows, cuts_ref, both_ref, vec_ref, base_ref, *refs, extra, order
):
    d_rows_ref, grad_ref, held, sems = refs[extra:]
    cuts, span, width = held.shape
    if order is None:
        copies = [
            pltpu.make_async_copy(
                weights.at[pl.ds(pl.multiple_of(rows[cut], 128), span)], held.at[cut], sems.at[cut]
            )
            for cut in range(cuts)
        ]
    else:
        copies = [
            WeightCopy(weights, held.at[cut], sems.at[cut], cut, 0, span, order)
            for cut in range(cuts)
        ]
    for copy in copies:
        copy.start()
    xs = both_ref[0].astype(jnp.float32)
    inverse = lax.rsqrt(row_mean(xs * xs) + EPS_NORM)
    normed = xs * inverse
    d_h1 = jnp.zeros(xs.shape, jnp.float32)
    for cut in range(cuts):
        copies[cut].wait()
        d_h1 = d_h1 + nn(cuts_ref[:, cut * span : (cut + 1) * span], held[cut])
    grad_ref[...] = jnp.sum(d_h1 * normed, axis=0, keepdims=True)
    d_normed = d_h1 * vec_ref[0:1, :]
    d_rows_ref[...] = (
        base_ref[...] + inverse * (d_normed - normed * row_mean(d_normed * normed))
    ).astype(jnp.bfloat16)


def plane_copies(refs, target, sems, tokens):
    return [
        pltpu.make_async_copy(ref, target.at[pl.ds(at * tokens, tokens)], sems.at[at])
        for at, ref in enumerate(refs)
    ]


def pair_refs_of(refs, index):
    return [ref.at[at, index] for ref in refs for at in range(ref.shape[0])]


def feed_forward_products_kernel(info, needs, weights, d_down_ref, *refs, extra):
    pair_refs = refs[: -7 - extra]
    out_ref, held, uppers, lowers, held_sems, upper_sems, lower_sems = refs[-7:]
    count, piece, _ = out_ref.shape
    sources, tokens, _ = d_down_ref.shape

    def row_copy(index, at, target, sems):
        start = pl.multiple_of(info[index, at], 16)
        return pltpu.make_async_copy(
            weights.at[pl.ds(start, piece)], target.at[index], sems.at[index]
        )

    def each_row_copy(index, act):
        @pl.when(info[index, 0] >= 2)
        def _():
            act(row_copy(index, 1, uppers, upper_sems))

        @pl.when(info[index, 0] == 2)
        def _():
            act(row_copy(index, 2, lowers, lower_sems))

    def each_held(act):
        @pl.when(needs[2] > 0)
        def _():
            copies = plane_copies(
                pair_refs_of(pair_refs, 1), held.at[0], held_sems.at[0], tokens
            ) + plane_copies(
                [d_down_ref.at[at] for at in range(sources)], held.at[1], held_sems.at[1], tokens
            )
            for copy in copies:
                act(copy)

    each_held(lambda copy: copy.start())

    @pl.loop(0, count)
    def _(index):
        each_row_copy(index, lambda copy: copy.start())

    each_held(lambda copy: copy.wait())

    @pl.loop(0, count)
    def _(index):
        each_row_copy(index, lambda copy: copy.wait())

        @pl.when(info[index, 0] == 2)
        def _():
            slope = gelu_and_slope(nt(uppers[index], held[0]))[1]
            d_pre = (nt(lowers[index], held[1]) * slope).astype(jnp.bfloat16)
            out_ref[index] = nn(d_pre, held[0]).astype(jnp.bfloat16)

        @pl.when(info[index, 0] == 3)
        def _():
            act = gelu_and_slope(nt(uppers[index], held[0]))[0]
            out_ref[index] = nn(act, held[1]).astype(jnp.bfloat16)


def attention_products_kernel(info, needs, h1_ref, *refs, sources, extra, first, last):
    proj_refs, attn_refs = refs[:sources], refs[sources : 2 * sources]
    pair_refs = refs[2 * sources : -10 - extra]
    near_ref, given_ref, out_ref, held, projs, attns, made, held_sems, factor_sems, out_sems = refs[-10:]
    _, piece, _ = made.shape
    tokens = h1_ref.shape[1]
    rights = ([h1_ref.at[at] for at in range(sources)], pair_refs_of(pair_refs, 0))
    columns = pl.ds(first * piece, (last - first) * piece)
    lefts = ([ref.at[:, columns] for ref in proj_refs], attn_refs)

    def each_operand(act):
        for kind, target in enumerate((projs, attns)):

            @pl.when(needs[kind] > 0)
            def _(kind=kind, target=target):
                copies = plane_copies(rights[kind], held.at[kind], held_sems.at[kind], tokens)
                copies += plane_copies(lefts[kind], target, factor_sems.at[kind], tokens)
                for copy in copies:
                    act(copy)

    def out_copy(index):
        return pltpu.make_async_copy(made.at[index - first], out_ref.at[index], out_sems.at[index])

    def passed_copy(index):
        source = near_ref if first else given_ref
        return pltpu.make_async_copy(source.at[index], out_ref.at[index], out_sems.at[index])

    def each_passed(act):
        for index in range(first if first else last):
            kind = info[index, 0]

            @pl.when((kind < 2) if first else (kind >= 2))
            def _(index=index):
                act(passed_copy(index))

    each_operand(lambda copy: copy.start())
    each_passed(lambda copy: copy.start())
    each_operand(lambda copy: copy.wait())
    for index in range(first, last):

        @pl.when(info[index, 0] == 0)
        def _(index=index):
            left = projs[:, (index - first) * piece : (index - first + 1) * piece]
            made[index - first] = tn(left, held[0]).astype(jnp.bfloat16)
            out_copy(index).start()

        @pl.when(info[index, 0] == 1)
        def _(index=index):
            left = attns[:, pl.ds(pl.multiple_of(info[index, 1], 128), piece)]
            made[index - first] = tn(left, held[1]).astype(jnp.bfloat16)
            out_copy(index).start()

    for index in range(first, last):

        @pl.when(info[index, 0] < 2)
        def _(index=index):
            out_copy(index).wait()

    each_passed(lambda copy: copy.wait())


def line_kernel(moves, below_ref, above_ref, terms_ref, *refs, step, piece, passed):
    up_ref, down_ref = refs[-4 - passed : -2 - passed]
    held, sems = refs[-2:]
    for source, target in zip(refs[:passed], refs[-2 - passed : -2]):
        target[...] = source[...]

    def each_copy(way, act):
        source = terms_ref.at[moves[step, way] * PIECES + piece]
        act(pltpu.make_async_copy(source, held.at[way], sems.at[way]))

    for way in range(2):
        each_copy(way, lambda copy: copy.start())
    for way, (came, leaves) in enumerate(((below_ref, up_ref), (above_ref, down_ref))):
        each_copy(way, lambda copy: copy.wait())
        leaves[...] = (held[way].astype(jnp.float32) + came[...].astype(jnp.float32)).astype(
            jnp.bfloat16
        )


def update_kernel(place, below_ref, above_ref, *refs, piece, own, step_count, last, chained, extra):
    arrays = refs[: 5 if last else 4]
    results = refs[len(arrays) + chained + extra : len(arrays) + chained + extra + 4]
    held, term, made, low, in_sems, out_sems = refs[-6:]
    rows = below_ref.shape[0]
    blocks = in_sems.shape[0]
    block = rows // blocks
    loads, stores = [], []
    for index in range(blocks):
        here = pl.ds(index * block, block)
        there = pl.ds(piece * rows + index * block, block)
        sources = [arrays[0].at[own, here]] + [array.at[there] for array in arrays[1:]]
        targets = [term.at[here]] + [held.at[at, here] for at in range(len(arrays) - 1)]
        loads.append(
            [
                pltpu.make_async_copy(source, target, in_sems.at[index, at])
                for at, (source, target) in enumerate(zip(sources, targets))
            ]
        )
        outs = [(made.at[1, here], results[0]), (made.at[2, here], results[1])]
        if not last:
            outs += [(made.at[0, here], results[2]), (low.at[here], results[3])]
        stores.append(
            [
                pltpu.make_async_copy(source, target.at[there], out_sems.at[index, at])
                for at, (source, target) in enumerate(outs)
            ]
        )
    for copies in loads:
        for copy in copies:
            copy.start()
    fixed_one = 1.0 / (1.0 - BETA_ONE**step_count)
    fixed_two = 1.0 / (1.0 - BETA_TWO**step_count)
    for index in range(blocks):
        for copy in loads[index]:
            copy.wait()
        some = pl.ds(index * block, block)
        grad = (term[some, :].astype(jnp.float32) + below_ref[some, :].astype(jnp.float32)) + above_ref[
            some, :
        ].astype(jnp.float32)
        param = held[0, some, :]
        first = BETA_ONE * held[1, some, :] + (1.0 - BETA_ONE) * grad
        second = BETA_TWO * held[2, some, :] + (1.0 - BETA_TWO) * grad * grad
        direction = first * fixed_one / (jnp.sqrt(second * fixed_two) + EPS_ADAM)
        param = param - INNER_RATE * (direction + DECAY_RATE * param)
        made[1, some, :] = first
        made[2, some, :] = second
        if last:
            made[0, some, :] = held[3, some, :] - param
        else:
            made[0, some, :] = param
            low[some, :] = param.astype(jnp.bfloat16)
        for copy in stores[index]:
            copy.start()
    if last:
        own_ref, other_ref = results[2:]
        columns = own_ref.shape[1]
        groups = other_ref.shape[0] + 1
        for step in range(groups):
            start = pl.multiple_of(lax.rem(place[0] + step, groups) * columns, 128)
            if step == 0:
                own_ref[...] = made[0, :, pl.ds(start, columns)]
            else:
                other_ref[step - 1] = made[0, :, pl.ds(start, columns)].astype(jnp.bfloat16)
    for copies in stores:
        for copy in copies:
            copy.wait()


def outer_kernel(place, own_ref, *refs, piece, groups, chained, extra):
    got_refs = refs[: groups - 1]
    arrays = refs[groups - 1 : groups + 2]
    results = refs[groups + 2 + chained + extra : groups + 6 + chained + extra]
    held, made, in_sems, out_sems = refs[-4:]
    rows, columns = own_ref.shape
    at = pl.ds(piece * rows, rows)
    start = pl.multiple_of(place[0] * columns, 128)
    sources = [arrays[0].at[at, pl.ds(start, columns)], arrays[1].at[at], arrays[2].at[at]]
    copies = [
        pltpu.make_async_copy(source, held.at[index], in_sems.at[index])
        for index, source in enumerate(sources)
    ]
    for copy in copies:
        copy.start()
    for copy in copies:
        copy.wait()
    share = own_ref[...]
    for index in range(groups - 1):
        share = share + got_refs[index][...].astype(jnp.float32)
    share = share / groups
    moment = OUTER_MOMENTUM * held[1] + share
    new_share = held[0] - OUTER_RATE * (share + OUTER_MOMENTUM * moment)
    made[0] = moment
    made[1] = share
    made[2] = AVERAGE_KEEP * held[2] + (1.0 - AVERAGE_KEEP) * new_share
    results[3][...] = new_share.astype(jnp.bfloat16)
    copies = [
        pltpu.make_async_copy(made.at[index], results[index].at[at], out_sems.at[index])
        for index in range(3)
    ]
    for copy in copies:
        copy.start()
    for copy in copies:
        copy.wait()


def join_kernel(place, *refs, piece, groups, chained):
    parts = refs[:groups]
    wide_hbm, low_hbm = refs[groups + chained : groups + chained + 2]
    wide, sems = refs[-2:]
    rows, columns = parts[0].shape
    at = pl.ds(piece * rows, rows)
    copies = []
    for step in range(groups):
        start = pl.multiple_of(lax.rem(place[0] + groups - step, groups) * columns, 128)
        wide[step] = parts[step][...].astype(jnp.float32)
        target = (at, pl.ds(start, columns))
        copies.append(pltpu.make_async_copy(wide.at[step], wide_hbm.at[target], sems.at[0, step]))
        copies.append(pltpu.make_async_copy(parts[step], low_hbm.at[target], sems.at[1, step]))
    for copy in copies:
        copy.start()
    for copy in copies:
        copy.wait()


def vmem(count):
    return [pl.BlockSpec(memory_space=pltpu.VMEM)] * count


def run_gather(lengths, picked, tokens_in, cot_in, plan):
    steps, count = picked.shape
    _, places, width = tokens_in.shape
    tokens = count + -count % 16
    padded = jnp.pad(picked, ((0, 0), (0, tokens - count)), constant_values=NOWHERE)
    shape = jax.ShapeDtypeStruct
    made = pl.pallas_call(
        functools.partial(gather_kernel, steps=steps, extra=len(plan)),
        in_specs=smem(1) + vmem(2) + anywhere(2) + smem(len(plan)),
        out_specs=vmem(2 * steps),
        out_shape=[shape((2, tokens, width), jnp.bfloat16)] * steps
        + [shape((2 * tokens, tokens), jnp.int32)] * steps,
        scratch_shapes=[
            pltpu.VMEM((steps, 2, places, width), jnp.bfloat16),
            pltpu.SemaphoreType.DMA((steps, 2)),
        ],
        compiler_params=pltpu.CompilerParams(vmem_limit_bytes=37 << 20),
        name="gather_rows",
    )(lengths, padded[:, :, None], padded[:, None, :], tokens_in, cot_in, *plan)
    return (made[:steps], made[steps:], padded[:, None, :])


def run_scatter(across, base, rows, step, chain, known):
    _, places, width = base.shape
    tokens = rows.shape[0]
    here = pl.BlockSpec((1, places, width), lambda index: (step, 0, 0))
    return pl.pallas_call(
        scatter_kernel,
        grid=(1,),
        in_specs=[
            pl.BlockSpec((1, 1, tokens), lambda index: (step, 0, 0)),
            here,
            pl.BlockSpec((tokens, width), lambda index: (0, 0)),
        ]
        + anywhere(len(chain) + len(known)),
        out_specs=[here, pl.BlockSpec((8, 128), lambda index: (0, 0))],
        out_shape=[
            jax.ShapeDtypeStruct(base.shape, base.dtype),
            jax.ShapeDtypeStruct((8, 128), jnp.float32),
        ],
        input_output_aliases=chain_aliases(3, chain),
        compiler_params=pltpu.CompilerParams(vmem_limit_bytes=56 << 20),
        cost_estimate=SMALL_COST,
        name="scatter_rows",
    )(across, base, rows, *chain, *known)


def run_attention(order, gathered, both, vec_now, mask, known):
    _, tokens, width = both.shape
    shape = jax.ShapeDtypeStruct
    return pl.pallas_call(
        functools.partial(attention_kernel, order=order, extra=len(known)),
        in_specs=anywhere(2) + vmem(2) + anywhere(len(known)),
        out_specs=vmem(4),
        out_shape=[
            shape((tokens, 3 * width), jnp.bfloat16),
            shape((2 * tokens, 128), jnp.float32),
            shape((2, tokens, width), jnp.bfloat16),
            shape((tokens, width), jnp.float32),
        ],
        scratch_shapes=[
            pltpu.VMEM((4 * width, width), jnp.bfloat16),
            pltpu.VMEM(mask.shape, jnp.int32),
            pltpu.SemaphoreType.DMA((4,)),
            pltpu.SemaphoreType.DMA,
        ],
        compiler_params=pltpu.CompilerParams(vmem_limit_bytes=37 << 20),
        cost_estimate=pl.CostEstimate(
            flops=8 * tokens * width * width, bytes_accessed=8 * width * width, transcendentals=0
        ),
        name="attention",
    )(gathered, mask, both, vec_now, *known)


def run_feed_forward(order, gathered, both, vec_now, first_sum, keep):
    _, tokens, width = both.shape
    wide = gathered.shape[0]
    shape = jax.ShapeDtypeStruct
    kept = [shape((tokens, wide - 4 * width), jnp.bfloat16)] if keep else []
    return pl.pallas_call(
        functools.partial(feed_forward_kernel, keep=keep, order=order),
        in_specs=anywhere(1) + vmem(3),
        out_specs=vmem(4 + len(kept)),
        out_shape=[
            shape((tokens, width), jnp.bfloat16),
            shape((tokens, width), jnp.bfloat16),
            shape((tokens, width), jnp.float32),
            shape((2, width), jnp.float32),
        ]
        + kept,
        scratch_shapes=[
            pltpu.VMEM((wide - 4 * width, width), jnp.bfloat16),
            pltpu.SemaphoreType.DMA(((wide - 4 * width) // width,)),
        ],
        compiler_params=pltpu.CompilerParams(vmem_limit_bytes=37 << 20),
        cost_estimate=pl.CostEstimate(
            flops=8 * tokens * (wide - 4 * width) * width,
            bytes_accessed=2 * wide * width,
            transcendentals=0,
        ),
        name="feed_forward",
    )(gathered, both, vec_now, first_sum)


def smem(count):
    return [pl.BlockSpec(memory_space=pltpu.SMEM)] * count


def anywhere(count):
    return [pl.BlockSpec(memory_space=pl.ANY)] * count


def run_attention_back(order, gathered, starts, d_attn_low, proj, lse, mask, pair, got):
    tokens, width = d_attn_low.shape
    cuts = starts.shape[0]
    shape = jax.ShapeDtypeStruct
    return pl.pallas_call(
        functools.partial(attention_back_kernel, order=order),
        in_specs=anywhere(1) + smem(1) + vmem(4) + anywhere(2),
        out_specs=anywhere(2),
        out_shape=[
            shape((tokens, 3 * width), jnp.bfloat16),
            shape((2,) + pair.shape, jnp.bfloat16),
        ],
        scratch_shapes=[
            pltpu.VMEM((width, width), jnp.bfloat16),
            pltpu.VMEM((tokens, 3 * width), jnp.bfloat16),
            pltpu.SemaphoreType.DMA((1,)),
            pltpu.SemaphoreType.DMA((2,)),
            pltpu.SemaphoreType.DMA((cuts,)),
        ],
        compiler_params=pltpu.CompilerParams(vmem_limit_bytes=37 << 20),
        cost_estimate=pl.CostEstimate(
            flops=10 * tokens * width * width, bytes_accessed=4 * width * width, transcendentals=0
        ),
        name="attention_back",
    )(gathered, starts, d_attn_low, proj, lse, mask, pair, got)


def run_input_back(order, gathered, rows, d_proj, both, vec_now, base, known):
    _, tokens, width = both.shape
    cuts = rows.shape[0]
    shape = jax.ShapeDtypeStruct
    return pl.pallas_call(
        functools.partial(
            input_back_kernel, extra=len(known), order=order
        ),
        in_specs=anywhere(1) + smem(1) + vmem(4) + anywhere(len(known)),
        out_specs=vmem(2),
        out_shape=[
            shape((tokens, width), jnp.bfloat16),
            shape((1, width), jnp.float32),
        ],
        scratch_shapes=[
            pltpu.VMEM((cuts, 3 * width // cuts, width), jnp.bfloat16),
            pltpu.SemaphoreType.DMA((cuts,)),
        ],
        compiler_params=pltpu.CompilerParams(vmem_limit_bytes=37 << 20),
        cost_estimate=SMALL_COST,
        name="input_back",
    )(gathered, rows, d_proj, both, vec_now, base, *known)


def run_line(moves, below, above, terms, step, piece, passed, known):
    shape = jax.ShapeDtypeStruct(below.shape, jnp.bfloat16)
    return pl.pallas_call(
        functools.partial(line_kernel, step=step, piece=piece, passed=len(passed)),
        in_specs=smem(1) + vmem(2) + anywhere(1) + vmem(len(passed)) + anywhere(len(known)),
        out_specs=vmem(2 + len(passed)),
        out_shape=[shape, shape]
        + [jax.ShapeDtypeStruct(values.shape, values.dtype) for values in passed],
        scratch_shapes=[
            pltpu.VMEM((2,) + below.shape, jnp.bfloat16),
            pltpu.SemaphoreType.DMA((2,)),
        ],
        compiler_params=pltpu.CompilerParams(vmem_limit_bytes=16 << 20),
        cost_estimate=pl.CostEstimate(
            flops=LINE_FLOPS, bytes_accessed=6 * below.size * 2, transcendentals=0
        ),
        name="line",
    )(moves, below, above, terms, *passed, *known)


def chain_aliases(first, chain):
    return {first + index: index for index in range(len(chain))}


def run_update(place, below, above, terms, states, piece, step_count, last, groups, chain, known):
    rows, width = below.shape
    own = terms.shape[0] - PIECES + piece
    shape = jax.ShapeDtypeStruct
    wide = shape(states[0].shape, jnp.float32)
    columns = width // groups
    if last:
        out_shape = [wide, wide, shape((rows, columns), jnp.float32)]
        out_shape.append(shape((groups - 1, rows, columns), jnp.bfloat16))
        out_specs = anywhere(2) + vmem(2)
    else:
        out_shape = [wide, wide, wide, shape(states[0].shape, jnp.bfloat16)]
        out_specs = anywhere(4)
    operands = (place, below, above, terms, *states, *chain, *known)
    return pl.pallas_call(
        functools.partial(
            update_kernel,
            piece=piece,
            own=own,
            step_count=step_count,
            last=last,
            chained=len(chain),
            extra=len(known),
        ),
        in_specs=smem(1) + vmem(2) + anywhere(len(operands) - 3),
        out_specs=out_specs,
        out_shape=out_shape,
        scratch_shapes=[
            pltpu.VMEM((len(states), rows, width), jnp.float32),
            pltpu.VMEM((rows, width), jnp.bfloat16),
            pltpu.VMEM((3, rows, width), jnp.float32),
            pltpu.VMEM((rows, width), jnp.bfloat16),
            pltpu.SemaphoreType.DMA((4, len(states) + 1)),
            pltpu.SemaphoreType.DMA((4, 4)),
        ],
        input_output_aliases=chain_aliases(4 + len(states), chain),
        compiler_params=pltpu.CompilerParams(vmem_limit_bytes=52 << 20),
        cost_estimate=pl.CostEstimate(
            flops=LINE_FLOPS, bytes_accessed=24 * rows * width, transcendentals=0
        ),
        name="update",
    )(*operands)


def run_outer(place, own, got, arrays, piece, chain, known):
    rows, columns = own.shape
    shape = jax.ShapeDtypeStruct
    narrow = shape(arrays[1].shape, jnp.float32)
    operands = (place, own, *got, *arrays, *chain, *known)
    return pl.pallas_call(
        functools.partial(
            outer_kernel,
            piece=piece,
            groups=len(got) + 1,
            chained=len(chain),
            extra=len(known),
        ),
        in_specs=smem(1) + vmem(1 + len(got)) + anywhere(len(operands) - 2 - len(got)),
        out_specs=anywhere(3) + vmem(1),
        out_shape=[narrow] * 3 + [shape(own.shape, jnp.bfloat16)],
        scratch_shapes=[
            pltpu.VMEM((3, rows, columns), jnp.float32),
            pltpu.VMEM((3, rows, columns), jnp.float32),
            pltpu.SemaphoreType.DMA((3,)),
            pltpu.SemaphoreType.DMA((3,)),
        ],
        input_output_aliases=chain_aliases(5 + len(got), chain),
        compiler_params=pltpu.CompilerParams(vmem_limit_bytes=52 << 20),
        cost_estimate=pl.CostEstimate(
            flops=LINE_FLOPS, bytes_accessed=24 * rows * columns, transcendentals=0
        ),
        name="outer",
    )(*operands)


def run_join(place, parts, like, piece, chain):
    rows, columns = parts[0].shape
    groups = len(parts)
    operands = (place, *parts, *chain)
    return pl.pallas_call(
        functools.partial(join_kernel, piece=piece, groups=groups, chained=len(chain)),
        in_specs=smem(1) + vmem(groups) + anywhere(len(chain)),
        out_specs=anywhere(2),
        out_shape=[
            jax.ShapeDtypeStruct(like.shape, jnp.float32),
            jax.ShapeDtypeStruct(like.shape, jnp.bfloat16),
        ],
        scratch_shapes=[
            pltpu.VMEM((groups, rows, columns), jnp.float32),
            pltpu.SemaphoreType.DMA((2, groups)),
        ],
        input_output_aliases=chain_aliases(1 + groups, chain),
        compiler_params=pltpu.CompilerParams(vmem_limit_bytes=52 << 20),
        cost_estimate=pl.CostEstimate(
            flops=LINE_FLOPS, bytes_accessed=12 * rows * columns * groups, transcendentals=0
        ),
        name="join",
    )(*operands)


def run_products(
    info, needs, gathered, proj_parts, attn_parts, plane_h1, plane_d_down, pairs, piece, known
):
    count = info.shape[0]
    sources, tokens, width = plane_h1.shape
    shape = jax.ShapeDtypeStruct((count, piece, width), jnp.bfloat16)
    made = pl.pallas_call(
        functools.partial(feed_forward_products_kernel, extra=len(attn_parts)),
        in_specs=smem(2) + anywhere(2 + len(pairs) + len(attn_parts)),
        out_specs=vmem(1)[0],
        out_shape=shape,
        scratch_shapes=[
            pltpu.VMEM((2, sources * tokens, width), jnp.bfloat16),
            pltpu.VMEM((count, piece, width), jnp.bfloat16),
            pltpu.VMEM((count, piece, width), jnp.bfloat16),
            pltpu.SemaphoreType.DMA((2, sources)),
            pltpu.SemaphoreType.DMA((count,)),
            pltpu.SemaphoreType.DMA((count,)),
        ],
        compiler_params=pltpu.CompilerParams(vmem_limit_bytes=37 << 20),
        cost_estimate=pl.CostEstimate(
            flops=6 * count * sources * tokens * piece * width,
            bytes_accessed=6 * count * piece * width,
            transcendentals=0,
        ),
        name="feed_forward_products",
    )(info, needs, gathered, plane_d_down, *pairs, *attn_parts)
    near = made
    for first, last in ((0, PIECES), (PIECES, count)):
        known = () if first else known
        operands = (info, needs, plane_h1, *proj_parts, *attn_parts, *pairs, *known, near, made)
        blocks = last - first
        found = pl.pallas_call(
            functools.partial(
                attention_products_kernel,
                sources=sources,
                extra=len(known),
                first=first,
                last=last,
            ),
            in_specs=smem(2) + anywhere(len(operands) - 2),
            out_specs=anywhere(1)[0],
            out_shape=jax.ShapeDtypeStruct((count if first else last, piece, width), jnp.bfloat16),
            scratch_shapes=[
                pltpu.VMEM((2, sources * tokens, width), jnp.bfloat16),
                pltpu.VMEM((sources * tokens, blocks * piece), jnp.bfloat16),
                pltpu.VMEM((sources * tokens, width), jnp.bfloat16),
                pltpu.VMEM((blocks, piece, width), jnp.bfloat16),
                pltpu.SemaphoreType.DMA((2, sources)),
                pltpu.SemaphoreType.DMA((2, sources)),
                pltpu.SemaphoreType.DMA((count,)),
            ],
            input_output_aliases={len(operands) - 1: 0} if first else {},
            compiler_params=pltpu.CompilerParams(vmem_limit_bytes=16 << 20),
            cost_estimate=SMALL_COST,
            name="attention_products",
        )(*operands)
        if first:
            return (near, found)
        near = found


def pad_rows(rows):
    return jnp.pad(rows, ((0, -rows.shape[0] % 16), (0, 0)))


def swap(values, axis, delta):
    size = lax.axis_size(axis)
    return lax.ppermute(values, axis, [(i, i ^ delta) for i in range(size)])


def sum_over(values, axes):
    for axis in axes:
        parts = [values]
        parts += [swap(values, axis, delta) for delta in range(1, lax.axis_size(axis))]
        while len(parts) > 1:
            parts = [parts[at] + parts[at + 1] for at in range(0, len(parts), 2)]
        values = parts[0]
    return values


def gathered_rows(values):
    return lax.all_gather(pad_rows(values), ("dp", "fsdp"), axis=0, tiled=False)


def line_order(line):
    due = np.zeros((line, line), np.int32)
    for here in range(line):
        for there in range(line):
            if there > here:
                due[here, there] = line - 1 - there + here
            elif there < here:
                due[here, there] = there - here + line - 1
            else:
                due[here, there] = line
    return np.argsort(due, axis=1, kind="stable").astype(np.int32)


def line_slots(line, order):
    ups = np.zeros((line - 1, line), np.int32)
    downs = np.zeros((line - 1, line), np.int32)
    for step in range(line - 1):
        for here in range(line):
            if here <= step:
                ups[step, here] = list(order[here]).index(line - 1 - step + here)
            if line - 1 - here <= step:
                downs[step, here] = list(order[here]).index(step - (line - 1) + here)
    return ups, downs


def added(*parts):
    return sum(part.astype(jnp.float32) for part in parts)


def due_after(value, *marks):
    flag = sum(mark[(-1,) * mark.ndim].astype(jnp.float32) for mark in marks)
    return value + (flag != flag).astype(value.dtype)


def plane_order(planes):
    deltas = [0]
    bit = planes // 2
    while bit >= 1:
        deltas = deltas + [delta ^ bit for delta in deltas]
        bit //= 2
    return deltas


def plane_gather(values):
    values = values[None]
    bit = lax.axis_size("fsdp") // 2
    while bit >= 1:
        values = jnp.concatenate([values, swap(values, "fsdp", bit)], axis=0)
        bit //= 2
    return values


def plane_operands(plane_rows, vec_now):
    sel_rows = plane_rows[:, 0].astype(jnp.float32)
    cot_rows = plane_rows[:, 1].astype(jnp.float32)
    gate = jax.nn.sigmoid(jnp.sum(sel_rows * vec_now[2], axis=-1, keepdims=True))
    inverse = lax.rsqrt(row_mean(sel_rows * sel_rows) + EPS_NORM)
    h1 = (sel_rows * inverse * vec_now[0]).astype(jnp.bfloat16)
    return (h1, (gate * cot_rows).astype(jnp.bfloat16))


def send_to(target, values):
    planes = lax.axis_size("fsdp")
    return [values] + [
        lax.ppermute(values, "fsdp", [(target ^ delta, target)]) for delta in plane_order(planes)[1:]
    ]


def gradient_plan(shard_rows, model_width, columns):
    planes, line = lax.axis_size("fsdp"), lax.axis_size("dp")
    plane, here = lax.axis_index("fsdp"), lax.axis_index("dp")
    hidden_units = (columns - 4 * model_width) // 2
    edges = (3 * model_width, 4 * model_width, 4 * model_width + hidden_units)

    def kind_of(row):
        return sum((row >= edge).astype(jnp.int32) for edge in edges)

    piece = shard_rows // PIECES
    theres = jnp.asarray(line_order(line))[here]
    rows = (plane * line + theres)[:, None] * shard_rows + jnp.arange(PIECES) * piece
    rows = rows.reshape(-1)
    kinds = kind_of(rows)
    at = rows - 3 * model_width
    order = (planes, line, shard_rows)
    uppers = gathered_row(jnp.where(kinds == 2, rows, rows - hidden_units), order)
    lowers = gathered_row(jnp.minimum(rows + hidden_units, columns - piece), order)
    info = jnp.stack([kinds, jnp.where(kinds >= 2, uppers, at), lowers], axis=1)
    low, high = kind_of(plane * line * shard_rows), kind_of((plane + 1) * line * shard_rows - 1)
    ff = (high >= 2).astype(jnp.int32)
    has_proj = (low == 0).astype(jnp.int32)
    has_attn = ((low <= 1) & (high >= 1)).astype(jnp.int32)
    moves = jnp.asarray(np.stack(line_slots(line, line_order(line)), axis=-1))[:, here]
    return (info.astype(jnp.int32), jnp.stack([has_proj, has_attn, ff, ff]), moves)


def gradient_starts(shard_rows, model_width, split):
    line, here = lax.axis_size("dp"), lax.axis_index("dp")
    if split:
        return jnp.asarray(line_order(line) * shard_rows)[here]
    return jnp.arange(4, dtype=jnp.int32) * (3 * model_width // 4)


def in_planes(shard_rows, model_width):
    line = lax.axis_size("dp")
    return (shard_rows // PIECES) % 128 == 0 and line * shard_rows == 3 * model_width


def gradient_whole(columns, operands):
    hidden_units = columns[2].shape[1] // 2
    factors = (*columns[:2], columns[2][:, :hidden_units], columns[2][:, hidden_units:])
    products = [tn(factor, operand) for factor, operand in zip(factors, operands)]
    low = jnp.concatenate(products, axis=0).astype(jnp.bfloat16)
    share = lax.psum_scatter(low, ("fsdp", "dp"), scatter_dimension=0, tiled=True)
    return share.astype(jnp.float32)


def plane_terms(
    gathered, d_proj, d_attn_low, pairs, plane_h1, plane_d_down, info, needs, shard_rows, known
):
    attn_parts = send_to(1, d_attn_low)
    pairs = [pairs]
    bit = lax.axis_size("fsdp") // 4
    while bit >= 1:
        pairs.append(swap(jnp.concatenate(pairs, axis=0), "fsdp", bit))
        bit //= 2
    return run_products(
        info,
        needs,
        gathered,
        send_to(0, d_proj),
        attn_parts,
        plane_h1,
        plane_d_down,
        pairs,
        shard_rows // PIECES,
        known,
    )


def gradient_share(near, terms, moves, passed, meanwhile):
    line = lax.axis_size("dp")
    below, above = [None] * PIECES, [None] * PIECES
    for step in range(line - 1):
        for index in range(PIECES):
            if step == 0:
                up = down = near[index]
            else:
                due = known[index] if step == line - 2 else ()
                given = passed if step == 1 and index == 0 else ()
                up, down, *given = run_line(
                    moves, below[index], above[index], terms, step, index, given, due
                )
                if step == 1 and index == 0:
                    known = meanwhile(up, given)
            below[index] = lax.ppermute(up, "dp", [(p, p + 1) for p in range(step + 1)])
            above[index] = lax.ppermute(
                down, "dp", [(line - 1 - p, line - 2 - p) for p in range(step + 1)]
            )
    return (below, above)


def adamw(param, grad, first, second, step_count, rate, decay):
    first = BETA_ONE * first + (1.0 - BETA_ONE) * grad
    second = BETA_TWO * second + (1.0 - BETA_TWO) * grad * grad
    fixed_one = 1.0 - BETA_ONE**step_count
    fixed_two = 1.0 - BETA_TWO**step_count
    direction = first / fixed_one / (jnp.sqrt(second / fixed_two) + EPS_ADAM)
    return (param - rate * (direction + decay * param), first, second)


def vector_rates():
    return jnp.array([[0.1], [0.1], [0.02]], dtype=jnp.float32)


def outer_whole(weights, master, outer_moment, smoothed_matrix_mean):
    groups = lax.axis_size("grp")
    here = lax.axis_index("grp")
    delta = weights - master
    col_width = weights.shape[1] // groups
    col_start = here * col_width
    diff_share = lax.dynamic_slice_in_dim(delta, col_start, col_width, 1)
    for step in range(1, groups):
        there = lax.rem(here + step, groups)
        part = lax.dynamic_slice_in_dim(delta, there * col_width, col_width, 1)
        diff_share = diff_share + shift_group(part.astype(jnp.bfloat16), step).astype(jnp.float32)
    diff_share = diff_share / groups
    moment_share = OUTER_MOMENTUM * outer_moment + diff_share
    base_share = lax.dynamic_slice_in_dim(weights, col_start, col_width, 1)
    new_share = base_share - OUTER_RATE * (diff_share + OUTER_MOMENTUM * moment_share)
    low_share = new_share.astype(jnp.bfloat16)
    weights_low = jnp.zeros(weights.shape, jnp.bfloat16)
    for step in range(groups):
        there = lax.rem(here + groups - step, groups)
        part = shift_group(low_share, step) if step else low_share
        weights_low = lax.dynamic_update_slice_in_dim(weights_low, part, there * col_width, 1)
    average_new = AVERAGE_KEEP * smoothed_matrix_mean + (1.0 - AVERAGE_KEEP) * new_share
    return (weights_low.astype(jnp.float32), weights_low, moment_share, diff_share, average_new)


def shift_group(values, step):
    groups = lax.axis_size("grp")
    return lax.ppermute(values, "grp", [(i, (i + step) % groups) for i in range(groups)])


def on_device(
    tokens,
    cotangent,
    lengths,
    selected,
    weights,
    vectors,
    first_moment,
    second_moment,
    vec_first,
    vec_second,
    outer_moment,
    smoothed_matrix_mean,
    vec_outer,
    vec_average,
):
    master = weights
    vec_now = vectors
    first_now = first_moment[0]
    second_now = second_moment[0]
    vfirst_now = vec_first[0]
    vsecond_now = vec_second[0]
    model_width = tokens.shape[2]
    planes, line = lax.axis_size("fsdp"), lax.axis_size("dp")
    shard_rows = weights.shape[0]
    info, needs, moves = gradient_plan(shard_rows, model_width, weights.shape[0] * planes * line)
    split = in_planes(shard_rows, model_width)
    starts = gradient_starts(shard_rows, model_width, split)
    order = (planes, line, shard_rows)
    weight_starts = gathered_row(starts, order)
    plan = (info, needs, moves, starts, weight_starts)
    boths, masks, across = run_gather(lengths[:, 0], selected[:, 0], tokens, cotangent, plan)
    plane_rows = plane_gather(boths[0])
    groups = lax.axis_size("grp")
    place = lax.axis_index("grp").astype(jnp.int32)[None]
    shard_low = master.astype(jnp.bfloat16)
    activations, input_grad, outers = [], [], []
    for inner_step in range(INNER):
        both, mask = boths[inner_step], masks[inner_step]
        gathered = lax.all_gather(shard_low, ("dp", "fsdp"), axis=0, tiled=True)
        plane_h1, plane_d_down = plane_operands(plane_rows, vec_now)
        proj, lse, pair, first_sum = run_attention(
            order,
            gathered,
            both,
            vec_now,
            mask,
            [plane_h1, plane_d_down, *activations[1:], *input_grad[1:]],
        )
        d_attn_low, out_rows, base, grad_two, *kept = run_feed_forward(
            order, gathered, both, vec_now, first_sum, not split
        )
        got = swap(pair[None], "fsdp", planes // 2)
        d_proj, pairs = run_attention_back(
            order, gathered, starts, d_attn_low, proj, lse, mask, pair, got
        )
        following = list(boths[inner_step + 1 : inner_step + 2])
        last = not following
        step_count = STEP + inner_step
        results = []

        def input_step(marks):
            d_rows, grad_one = run_input_back(
                None if split else order, gathered, weight_starts, d_proj, both, vec_now, base, marks
            )
            results.append(jnp.concatenate([grad_one, grad_two], axis=0))
            return d_rows

        def scatter_out(marks):
            activations[:] = run_scatter(
                across, tokens, out_rows, inner_step, activations[:1], marks
            )

        def scatter_grad(d_rows, marks):
            input_grad[:] = run_scatter(
                across, cotangent, d_rows, inner_step, input_grad[:1], marks
            )

        if split and last:
            d_rows = input_step([])
            results[0] = gathered_rows(results[0])

        def meanwhile(mark, passed):
            if not last:
                results.append(plane_gather(passed[0]))
                return (results[-1:], (), ())
            return ((), (), ())

        if split:
            near, terms = plane_terms(
                gathered,
                d_proj,
                d_attn_low,
                pairs,
                plane_h1,
                plane_d_down,
                info,
                needs,
                shard_rows,
                [d_rows] if last else (),
            )
            below, above = gradient_share(near, terms, moves, following, meanwhile)
            grad_mark = below[-1]
        else:
            grad_mark = gradient_whole(
                (d_proj, d_attn_low, *kept), (plane_h1[0], pair[0], pair[1], plane_d_down[0])
            )
            results.extend(plane_gather(values) for values in following)
        if split and last:
            made = []
            for index in range(PIECES):
                made.append(
                    run_update(
                        place,
                        below[index],
                        above[index],
                        terms,
                        (master, first_now, second_now, weights),
                        index,
                        step_count,
                        last,
                        groups,
                        made[-1][:2] if index else (),
                        [outers[0][3]] if index == PIECES - 1 else activations[1:],
                    )
                )
                own, other = made[-1][2:]
                if index == 0:
                    scatter_out([own])
                if index == PIECES - 1:
                    scatter_grad(d_rows, [own])
                outers.append(
                    run_outer(
                        place,
                        own,
                        [shift_group(other[step - 1], step) for step in range(1, groups)],
                        (weights, outer_moment, smoothed_matrix_mean),
                        index,
                        outers[-1][:3] if index else (),
                        input_grad[1:] if index == PIECES - 1 else [],
                    )
                )
            first_now, second_now = made[-1][:2]
        else:
            grad_shard = grad_mark
            if split:
                own = (line - 1) * PIECES
                grad_shard = jnp.concatenate(
                    [
                        added(terms[own + index], below[index], above[index])
                        for index in range(PIECES)
                    ],
                    axis=0,
                )
            master, first_now, second_now = adamw(
                master, grad_shard, first_now, second_now, step_count, INNER_RATE, DECAY_RATE
            )
            shard_low = master.astype(jnp.bfloat16)
        if not last:
            plane_rows = results.pop()
        if split and last:
            grad_vec = jnp.sum(due_after(results[0][:, : vec_now.shape[0]], made[0][2]), axis=0)
            vec_now, vfirst_now, vsecond_now = adamw(
                vec_now, grad_vec, vfirst_now, vsecond_now, step_count, vector_rates(), 0.0
            )
            vec_diff = sum_over(vectors - vec_now, ("grp",)) / groups
        else:
            scatter_out([grad_mark])
            scatter_grad(input_step([grad_mark]), [grad_mark])
            grad_vec = sum_over(due_after(results[0], grad_mark), ("fsdp", "dp"))
            vec_now, vfirst_now, vsecond_now = adamw(
                vec_now, grad_vec, vfirst_now, vsecond_now, step_count, vector_rates(), 0.0
            )
    if split:
        joined = []
        for index in range(PIECES):
            low = outers[index][3]
            parts = [low] + [shift_group(low, step) for step in range(1, groups)]
            joined = run_join(place, parts, weights, index, joined)
        weights_new, weights_low = joined
        outer_new, diff_new, average_new = outers[-1][:3]
    else:
        weights_new, weights_low, outer_new, diff_new, average_new = outer_whole(
            weights, master, outer_moment, smoothed_matrix_mean
        )
    if not split:
        vec_diff = sum_over(vectors - vec_now, ("grp",)) / groups
    vec_moment = OUTER_MOMENTUM * vec_outer + vec_diff
    vectors_new = vectors - OUTER_RATE * (vec_diff + OUTER_MOMENTUM * vec_moment)
    vec_average_new = AVERAGE_KEEP * vec_average + (1.0 - AVERAGE_KEEP) * vectors_new
    return (
        activations[0],
        input_grad[0],
        weights_new,
        weights_low,
        first_now[None],
        second_now[None],
        outer_new,
        diff_new,
        average_new,
        vectors_new,
        vfirst_now[None],
        vsecond_now[None, :2],
        vsecond_now[None, 2],
        vec_moment,
        vec_average_new,
    )


def solution(mesh):
    placed = (
        P(None, ("grp", "fsdp", "dp"), None),
        P(None, ("grp", "fsdp", "dp"), None),
        P(None, ("grp", "fsdp", "dp"), None),
        P(None, ("grp", "fsdp", "dp"), None),
        P(("fsdp", "dp"), None),
        P(),
        P("grp", ("fsdp", "dp"), None),
        P("grp", ("fsdp", "dp"), None),
        P("grp", None, None),
        P("grp", None, None),
        P(("fsdp", "dp"), "grp"),
        P(("fsdp", "dp"), "grp"),
        P(),
        P(),
    )
    return jax.shard_map(
        on_device,
        mesh=mesh,
        in_specs=placed,
        out_specs=(
            P(None, ("grp", "fsdp", "dp"), None),
            P(None, ("grp", "fsdp", "dp"), None),
            P(("fsdp", "dp"), None),
            P(("fsdp", "dp"), None),
            P("grp", ("fsdp", "dp"), None),
            P("grp", ("fsdp", "dp"), None),
            P(("fsdp", "dp"), "grp"),
            P(("fsdp", "dp"), "grp"),
            P(("fsdp", "dp"), "grp"),
            P(),
            P("grp", None, None),
            P("grp", None, None),
            P("grp", None),
            P(),
            P(),
        ),
        check_vma=False,
    )
```

```python
import functools
import math

import jax
import jax.numpy as jnp
import numpy as np
from jax import lax
from jax.experimental import pallas as pl
from jax.experimental.pallas import tpu as pltpu
from jax.sharding import PartitionSpec as P

HEAD = 64
INNER = 2
STEP = 5


EPS_NORM = 1e-06
EPS_ADAM = 1e-08
BETA_ONE = 0.9
BETA_TWO = 0.95
INNER_RATE = 0.03
DECAY_RATE = 0.1
OUTER_RATE = 0.7
OUTER_MOMENTUM = 0.9
AVERAGE_KEEP = 0.9
GELU_SCALE = float(np.sqrt(2.0 / np.pi))
GELU_CUBE = 0.044715
PIECES = 3
LINE_FLOPS = 10**10
SMALL_COST = pl.CostEstimate(flops=10**6, bytes_accessed=10**5, transcendentals=0)
NOWHERE = 1 << 20


def nt(left, right):
    return lax.dot_general(
        left, right, (((1,), (1,)), ((), ())), preferred_element_type=jnp.float32
    )


def nn(left, right):
    return lax.dot_general(
        left, right, (((1,), (0,)), ((), ())), preferred_element_type=jnp.float32
    )


def tn(left, right):
    return lax.dot_general(
        left, right, (((0,), (0,)), ((), ())), preferred_element_type=jnp.float32
    )


def gathered_row(row, order):
    planes, line, shard_rows = order
    shard = row // shard_rows
    return ((shard % line) * planes + shard // line) * shard_rows + row % shard_rows


class WeightCopy:
    def __init__(self, weights, held, sem, source, target, rows, order):
        unit = math.gcd(order[2], rows)
        self.parts = [
            pltpu.make_async_copy(
                weights.at[pl.ds(gathered_row(source * rows + at, order), unit)],
                held.at[pl.ds(target * rows + at, unit)],
                sem,
            )
            for at in range(0, rows, unit)
        ]
        self.whole = pltpu.make_async_copy(
            weights.at[pl.ds(0, rows)], held.at[pl.ds(target * rows, rows)], sem
        )

    def start(self):
        for part in self.parts:
            part.start()

    def wait(self):
        self.whole.wait()


def weight_copies(weights, held, sems, sources, rows, order):
    return [
        WeightCopy(weights, held, sems.at[target], source, target, rows, order)
        for target, source in enumerate(sources)
    ]


def two_heads(values):
    low = lax.broadcasted_iota(jnp.int32, values.shape, 1) < HEAD
    zero = jnp.zeros_like(values)
    return jnp.concatenate([jnp.where(low, values, zero), jnp.where(low, zero, values)], axis=0)


def one_block(values):
    rows = values.shape[0] // 2
    low = lax.broadcasted_iota(jnp.int32, (rows, values.shape[1]), 1) < HEAD
    return jnp.where(low, values[:rows], values[rows:])


def row_mean(values):
    return jnp.mean(values, axis=-1, keepdims=True)


def gelu_and_slope(pre):
    square = pre * pre
    tanh = jnp.tanh(GELU_SCALE * pre * (1.0 + GELU_CUBE * square))
    half = 0.5 * (1.0 + tanh)
    slope = half + 0.5 * pre * (1.0 - tanh * tanh) * (
        GELU_SCALE * (1.0 + 3.0 * GELU_CUBE * square)
    )
    return ((pre * half).astype(jnp.bfloat16), slope)


def gather_kernel(lengths, picked_ref, across_ref, tokens_hbm, cot_hbm, *refs, steps, extra):
    refs = refs[extra:]
    both_refs, mask_refs = refs[:steps], refs[steps : 2 * steps]
    held, sems = refs[2 * steps :]
    copies = [
        [
            pltpu.make_async_copy(source.at[step], held.at[step, at], sems.at[step, at])
            for at, source in enumerate((tokens_hbm, cot_hbm))
        ]
        for step in range(steps)
    ]
    for some in copies:
        for copy in some:
            copy.start()
    for step in range(steps):
        down, across = picked_ref[step], across_ref[step]
        segment_down, segment_across = jnp.zeros_like(down), jnp.zeros_like(across)
        end = jnp.int32(0)
        for slot in range(lengths.shape[1]):
            end = end + lengths[step, slot]
            segment_down += (down >= end).astype(jnp.int32)
            segment_across += (across >= end).astype(jnp.int32)
        allowed = (segment_down == segment_across) & (across <= down)
        allowed = allowed.astype(jnp.int32)
        mask_refs[step][...] = jnp.concatenate([allowed, allowed], axis=0)
        places = lax.broadcasted_iota(jnp.int32, (down.shape[0], held.shape[2]), 1)
        chosen = jnp.where(places == down, 1.0, 0.0).astype(jnp.bfloat16)
        for at in range(2):
            copies[step][at].wait()
            both_refs[step][at] = nn(chosen, held[step, at]).astype(jnp.bfloat16)


def scatter_kernel(across_ref, base_ref, rows_ref, *refs):
    out_ref, mark_ref = refs[-2:]
    mark_ref[...] = jnp.zeros_like(mark_ref)
    base = base_ref[0]
    across = across_ref[0]
    places = lax.broadcasted_iota(jnp.int32, (base.shape[0], across.shape[1]), 0)
    chosen = jnp.where(places == across, 1.0, 0.0)
    replaced = jnp.sum(chosen, axis=-1, keepdims=True) > 0.0
    rows = nn(chosen.astype(jnp.bfloat16), rows_ref[...]).astype(jnp.bfloat16)
    out_ref[0] = jnp.where(replaced, rows, base)


def attention_kernel(
    weights, mask_hbm, both_hbm, vec_ref, *refs, order, extra
):
    proj_ref, lse_ref, pair_ref, first_ref, held, mask_ref, rows_ref, sems, mask_sem, rows_sem = refs[
        extra:
    ]
    width = rows_ref.shape[1]
    rows_copy = pltpu.make_async_copy(both_hbm.at[0], rows_ref, rows_sem)
    rows_copy.start()
    copies = weight_copies(weights, held, sems, range(4), width, order)
    mask_copy = pltpu.make_async_copy(mask_hbm, mask_ref, mask_sem)
    mask_copy.start()
    for copy in copies:
        copy.start()
    rows_copy.wait()
    xs = rows_ref[...].astype(jnp.float32)
    h1 = (xs * lax.rsqrt(row_mean(xs * xs) + EPS_NORM) * vec_ref[0:1, :]).astype(jnp.bfloat16)
    for index in range(3):
        copies[index].wait()
        proj_ref[:, index * width : (index + 1) * width] = nt(
            h1, held[pl.ds(index * width, width), :]
        ).astype(jnp.bfloat16)
    mask_copy.wait()
    allowed = mask_ref[...] > 0
    lane = lax.broadcasted_iota(jnp.int32, lse_ref.shape, 1)
    lse = jnp.zeros(lse_ref.shape, jnp.float32)
    for pair in range(width // 128):
        at = pair * 128
        queries = two_heads(proj_ref[:, at : at + 128])
        keys = proj_ref[:, width + at : width + at + 128]
        values = proj_ref[:, 2 * width + at : 2 * width + at + 128]
        scores = jnp.where(allowed, nt(queries, keys) * HEAD ** (-0.5), -1e30)
        top = jnp.max(scores, axis=-1, keepdims=True)
        total = top + jnp.log(jnp.sum(jnp.exp(scores - top), axis=-1, keepdims=True))
        lse = jnp.where(lane == pair, total, lse)
        probs_low = jnp.exp(scores - total).astype(jnp.bfloat16)
        pair_ref[0, :, at : at + 128] = one_block(nn(probs_low, values)).astype(jnp.bfloat16)
    lse_ref[...] = lse
    copies[3].wait()
    first_sum = xs + nt(pair_ref[0], held[pl.ds(3 * width, width), :])
    first_ref[...] = first_sum
    inverse = lax.rsqrt(row_mean(first_sum * first_sum) + EPS_NORM)
    pair_ref[1] = (first_sum * inverse * vec_ref[1:2, :]).astype(jnp.bfloat16)


def feed_forward_kernel(
    weights,
    both_ref,
    vec_ref,
    first_ref,
    d_attn_ref,
    out_ref,
    base_ref,
    grad_ref,
    *refs,
    keep,
    order,
):
    held, sems = refs[-2:]
    rows_ref, cot_ref = both_ref.at[0], both_ref.at[1]
    width = both_ref.shape[2]
    hidden = (weights.shape[0] - 4 * width) // 2
    parts = hidden // width
    matrices = []
    for part in range(parts):
        matrices += [4 + part, 4 + parts + part]
    copies = weight_copies(weights, held, sems, matrices, width, order)
    for copy in copies:
        copy.start()

    def matrix(index):
        return held[pl.ds(index * width, width), :]

    xs = rows_ref[...].astype(jnp.float32)
    cot = cot_ref[...].astype(jnp.float32)
    gate = jax.nn.sigmoid(jnp.sum(xs * vec_ref[2:3, :], axis=-1, keepdims=True))
    first_sum = first_ref[...]
    inverse = lax.rsqrt(row_mean(first_sum * first_sum) + EPS_NORM)
    normed = first_sum * inverse
    h2 = (normed * vec_ref[1:2, :]).astype(jnp.bfloat16)
    d_branch = gate * cot
    d_down = d_branch.astype(jnp.bfloat16)
    branch = first_sum - xs
    d_h2 = jnp.zeros_like(branch)
    for part in range(parts):
        at = part * width
        copies[2 * part].wait()
        act, slope = gelu_and_slope(nt(h2, matrix(2 * part)))
        copies[2 * part + 1].wait()
        branch = branch + nn(act, matrix(2 * part + 1))
        d_pre = (nt(d_down, matrix(2 * part + 1)) * slope).astype(jnp.bfloat16)
        if keep:
            refs[0][:, at : at + width] = d_pre
            refs[0][:, at + hidden : at + hidden + width] = act
        d_h2 = d_h2 + nn(d_pre, matrix(2 * part))
    out_ref[...] = (xs + gate * branch).astype(jnp.bfloat16)
    d_logit = jnp.sum(cot * branch, axis=-1, keepdims=True) * gate * (1.0 - gate)
    grad_ref[0:1, :] = jnp.sum(d_h2 * normed, axis=0, keepdims=True)
    grad_ref[1:2, :] = jnp.sum(d_logit * xs, axis=0, keepdims=True)
    d_normed = d_h2 * vec_ref[1:2, :]
    d_first = inverse * (d_normed - normed * row_mean(d_normed * normed))
    d_attn_ref[...] = (d_branch + d_first).astype(jnp.bfloat16)
    base_ref[...] = cot + d_first + d_logit * vec_ref[2:3, :]


def attention_back_kernel(
    weights,
    starts,
    d_attn_ref,
    proj_ref,
    lse_ref,
    mask_hbm,
    pair_hbm,
    got_hbm,
    cuts_hbm,
    pairs_hbm,
    held,
    late_ref,
    weight_sems,
    pair_sems,
    cut_sems,
    mask_ref,
    mask_sem,
    *,
    order,
):
    width = held.shape[1]
    copies = weight_copies(weights, held, weight_sems, [3], width, order)
    pair_copies = [
        pltpu.make_async_copy(pair_hbm, pairs_hbm.at[0], pair_sems.at[0]),
        pltpu.make_async_copy(got_hbm.at[0], pairs_hbm.at[1], pair_sems.at[1]),
    ]
    mask_copy = pltpu.make_async_copy(mask_hbm, mask_ref, mask_sem)
    for copy in copies + [mask_copy] + pair_copies:
        copy.start()
    copies[0].wait()
    d_mixed = nn(d_attn_ref[...], held[pl.ds(0, width), :]).astype(jnp.bfloat16)
    mask_copy.wait()
    allowed = mask_ref[...] > 0
    for pair in range(width // 128):
        at = pair * 128
        queries = two_heads(proj_ref[:, at : at + 128])
        keys = proj_ref[:, width + at : width + at + 128]
        values = proj_ref[:, 2 * width + at : 2 * width + at + 128]
        d_pair = two_heads(d_mixed[:, at : at + 128])
        scores = jnp.where(allowed, nt(queries, keys) * HEAD ** (-0.5), -1e30)
        probs = jnp.exp(scores - lse_ref[:, pair : pair + 1])
        probs_low = probs.astype(jnp.bfloat16)
        d_probs = nt(d_pair, values)
        d_scores = probs * (d_probs - jnp.sum(d_probs * probs, axis=-1, keepdims=True))
        d_scores = d_scores.astype(jnp.bfloat16)
        late_ref[:, at : at + 128] = (one_block(nn(d_scores, keys)) * HEAD ** (-0.5)).astype(
            jnp.bfloat16
        )
        late_ref[:, width + at : width + at + 128] = (
            tn(d_scores, queries) * HEAD ** (-0.5)
        ).astype(jnp.bfloat16)
        late_ref[:, 2 * width + at : 2 * width + at + 128] = tn(probs_low, d_pair).astype(
            jnp.bfloat16
        )
    cuts = starts.shape[0]
    span = late_ref.shape[1] // cuts
    cut_copies = []
    for cut in range(cuts):
        start = pl.multiple_of(starts[cut], 128)
        cut_copies.append(
            pltpu.make_async_copy(
                late_ref.at[:, pl.ds(start, span)],
                cuts_hbm.at[:, pl.ds(cut * span, span)],
                cut_sems.at[cut],
            )
        )
    for copy in cut_copies:
        copy.start()
    for copy in cut_copies + pair_copies:
        copy.wait()


def input_back_kernel(
    weights, rows, cuts_ref, both_ref, vec_ref, base_ref, *refs, extra, order
):
    d_rows_ref, grad_ref, held, sems = refs[extra:]
    cuts, span, width = held.shape
    if order is None:
        copies = [
            pltpu.make_async_copy(
                weights.at[pl.ds(pl.multiple_of(rows[cut], 128), span)], held.at[cut], sems.at[cut]
            )
            for cut in range(cuts)
        ]
    else:
        copies = [
            WeightCopy(weights, held.at[cut], sems.at[cut], cut, 0, span, order)
            for cut in range(cuts)
        ]
    for copy in copies:
        copy.start()
    xs = both_ref[0].astype(jnp.float32)
    inverse = lax.rsqrt(row_mean(xs * xs) + EPS_NORM)
    normed = xs * inverse
    d_h1 = jnp.zeros(xs.shape, jnp.float32)
    for cut in range(cuts):
        copies[cut].wait()
        d_h1 = d_h1 + nn(cuts_ref[:, cut * span : (cut + 1) * span], held[cut])
    grad_ref[...] = jnp.sum(d_h1 * normed, axis=0, keepdims=True)
    d_normed = d_h1 * vec_ref[0:1, :]
    d_rows_ref[...] = (
        base_ref[...] + inverse * (d_normed - normed * row_mean(d_normed * normed))
    ).astype(jnp.bfloat16)


def plane_copies(refs, target, sems, tokens):
    return [
        pltpu.make_async_copy(ref, target.at[pl.ds(at * tokens, tokens)], sems.at[at])
        for at, ref in enumerate(refs)
    ]


def pair_refs_of(refs, index):
    return [ref.at[at, index] for ref in refs for at in range(ref.shape[0])]


def feed_forward_products_kernel(info, needs, weights, d_down_ref, *refs, extra):
    pair_refs = refs[: -7 - extra]
    out_ref, held, uppers, lowers, held_sems, upper_sems, lower_sems = refs[-7:]
    count, piece, _ = out_ref.shape
    sources, tokens, _ = d_down_ref.shape

    def row_copy(index, at, target, sems):
        start = pl.multiple_of(info[index, at], 16)
        return pltpu.make_async_copy(
            weights.at[pl.ds(start, piece)], target.at[index], sems.at[index]
        )

    def each_row_copy(index, act):
        @pl.when(info[index, 0] >= 2)
        def _():
            act(row_copy(index, 1, uppers, upper_sems))

        @pl.when(info[index, 0] == 2)
        def _():
            act(row_copy(index, 2, lowers, lower_sems))

    def each_held(act):
        @pl.when(needs[2] > 0)
        def _():
            copies = plane_copies(
                pair_refs_of(pair_refs, 1), held.at[0], held_sems.at[0], tokens
            ) + plane_copies(
                [d_down_ref.at[at] for at in range(sources)], held.at[1], held_sems.at[1], tokens
            )
            for copy in copies:
                act(copy)

    each_held(lambda copy: copy.start())

    @pl.loop(0, count)
    def _(index):
        each_row_copy(index, lambda copy: copy.start())

    each_held(lambda copy: copy.wait())

    @pl.loop(0, count)
    def _(index):
        each_row_copy(index, lambda copy: copy.wait())

        @pl.when(info[index, 0] == 2)
        def _():
            slope = gelu_and_slope(nt(uppers[index], held[0]))[1]
            d_pre = (nt(lowers[index], held[1]) * slope).astype(jnp.bfloat16)
            out_ref[index] = nn(d_pre, held[0]).astype(jnp.bfloat16)

        @pl.when(info[index, 0] == 3)
        def _():
            act = gelu_and_slope(nt(uppers[index], held[0]))[0]
            out_ref[index] = nn(act, held[1]).astype(jnp.bfloat16)


def attention_products_kernel(info, needs, h1_ref, *refs, sources, extra, first, last):
    proj_refs, attn_refs = refs[:sources], refs[sources : 2 * sources]
    pair_refs = refs[2 * sources : -10 - extra]
    near_ref, given_ref, out_ref, held, projs, attns, made, held_sems, factor_sems, out_sems = refs[-10:]
    _, piece, _ = made.shape
    tokens = h1_ref.shape[1]
    rights = ([h1_ref.at[at] for at in range(sources)], pair_refs_of(pair_refs, 0))
    columns = pl.ds(first * piece, (last - first) * piece)
    lefts = ([ref.at[:, columns] for ref in proj_refs], attn_refs)

    def each_operand(act):
        for kind, target in enumerate((projs, attns)):

            @pl.when(needs[kind] > 0)
            def _(kind=kind, target=target):
                copies = plane_copies(rights[kind], held.at[kind], held_sems.at[kind], tokens)
                copies += plane_copies(lefts[kind], target, factor_sems.at[kind], tokens)
                for copy in copies:
                    act(copy)

    def out_copy(index):
        return pltpu.make_async_copy(made.at[index - first], out_ref.at[index], out_sems.at[index])

    def passed_copy(index):
        source = near_ref if first else given_ref
        return pltpu.make_async_copy(source.at[index], out_ref.at[index], out_sems.at[index])

    def each_passed(act):
        for index in range(first if first else last):
            kind = info[index, 0]

            @pl.when((kind < 2) if first else (kind >= 2))
            def _(index=index):
                act(passed_copy(index))

    each_operand(lambda copy: copy.start())
    each_passed(lambda copy: copy.start())
    each_operand(lambda copy: copy.wait())
    for index in range(first, last):

        @pl.when(info[index, 0] == 0)
        def _(index=index):
            left = projs[:, (index - first) * piece : (index - first + 1) * piece]
            made[index - first] = tn(left, held[0]).astype(jnp.bfloat16)
            out_copy(index).start()

        @pl.when(info[index, 0] == 1)
        def _(index=index):
            left = attns[:, pl.ds(pl.multiple_of(info[index, 1], 128), piece)]
            made[index - first] = tn(left, held[1]).astype(jnp.bfloat16)
            out_copy(index).start()

    for index in range(first, last):

        @pl.when(info[index, 0] < 2)
        def _(index=index):
            out_copy(index).wait()

    each_passed(lambda copy: copy.wait())


def line_kernel(moves, below_ref, above_ref, terms_ref, *refs, step, piece, passed):
    up_ref, down_ref = refs[-4 - passed : -2 - passed]
    held, sems = refs[-2:]
    for source, target in zip(refs[:passed], refs[-2 - passed : -2]):
        target[...] = source[...]

    def each_copy(way, act):
        source = terms_ref.at[moves[step, way] * PIECES + piece]
        act(pltpu.make_async_copy(source, held.at[way], sems.at[way]))

    for way in range(2):
        each_copy(way, lambda copy: copy.start())
    for way, (came, leaves) in enumerate(((below_ref, up_ref), (above_ref, down_ref))):
        each_copy(way, lambda copy: copy.wait())
        leaves[...] = (held[way].astype(jnp.float32) + came[...].astype(jnp.float32)).astype(
            jnp.bfloat16
        )


def update_kernel(place, below_ref, above_ref, *refs, piece, own, step_count, last, chained, extra):
    arrays = refs[: 5 if last else 4]
    results = refs[len(arrays) + chained + extra : len(arrays) + chained + extra + 4]
    held, term, made, low, in_sems, out_sems = refs[-6:]
    rows = below_ref.shape[0]
    blocks = in_sems.shape[0]
    block = rows // blocks
    loads, stores = [], []
    for index in range(blocks):
        here = pl.ds(index * block, block)
        there = pl.ds(piece * rows + index * block, block)
        sources = [arrays[0].at[own, here]] + [array.at[there] for array in arrays[1:]]
        targets = [term.at[here]] + [held.at[at, here] for at in range(len(arrays) - 1)]
        loads.append(
            [
                pltpu.make_async_copy(source, target, in_sems.at[index, at])
                for at, (source, target) in enumerate(zip(sources, targets))
            ]
        )
        outs = [(made.at[1, here], results[0]), (made.at[2, here], results[1])]
        if not last:
            outs += [(made.at[0, here], results[2]), (low.at[here], results[3])]
        stores.append(
            [
                pltpu.make_async_copy(source, target.at[there], out_sems.at[index, at])
                for at, (source, target) in enumerate(outs)
            ]
        )
    for copies in loads:
        for copy in copies:
            copy.start()
    fixed_one = 1.0 / (1.0 - BETA_ONE**step_count)
    fixed_two = 1.0 / (1.0 - BETA_TWO**step_count)
    for index in range(blocks):
        for copy in loads[index]:
            copy.wait()
        some = pl.ds(index * block, block)
        grad = (term[some, :].astype(jnp.float32) + below_ref[some, :].astype(jnp.float32)) + above_ref[
            some, :
        ].astype(jnp.float32)
        param = held[0, some, :]
        first = BETA_ONE * held[1, some, :] + (1.0 - BETA_ONE) * grad
        second = BETA_TWO * held[2, some, :] + (1.0 - BETA_TWO) * grad * grad
        direction = first * fixed_one / (jnp.sqrt(second * fixed_two) + EPS_ADAM)
        param = param - INNER_RATE * (direction + DECAY_RATE * param)
        made[1, some, :] = first
        made[2, some, :] = second
        if last:
            made[0, some, :] = held[3, some, :] - param
        else:
            made[0, some, :] = param
            low[some, :] = param.astype(jnp.bfloat16)
        for copy in stores[index]:
            copy.start()
    if last:
        own_ref, other_ref = results[2:]
        columns = own_ref.shape[1]
        groups = other_ref.shape[0] + 1
        for step in range(groups):
            start = pl.multiple_of(lax.rem(place[0] + step, groups) * columns, 128)
            if step == 0:
                own_ref[...] = made[0, :, pl.ds(start, columns)]
            else:
                other_ref[step - 1] = made[0, :, pl.ds(start, columns)].astype(jnp.bfloat16)
    for copies in stores:
        for copy in copies:
            copy.wait()


def outer_kernel(place, own_ref, *refs, piece, groups, chained, extra):
    got_refs = refs[: groups - 1]
    arrays = refs[groups - 1 : groups + 2]
    results = refs[groups + 2 + chained + extra : groups + 6 + chained + extra]
    held, made, in_sems, out_sems = refs[-4:]
    rows, columns = own_ref.shape
    at = pl.ds(piece * rows, rows)
    start = pl.multiple_of(place[0] * columns, 128)
    sources = [arrays[0].at[at, pl.ds(start, columns)], arrays[1].at[at], arrays[2].at[at]]
    copies = [
        pltpu.make_async_copy(source, held.at[index], in_sems.at[index])
        for index, source in enumerate(sources)
    ]
    for copy in copies:
        copy.start()
    for copy in copies:
        copy.wait()
    share = own_ref[...]
    for index in range(groups - 1):
        share = share + got_refs[index][...].astype(jnp.float32)
    share = share / groups
    moment = OUTER_MOMENTUM * held[1] + share
    new_share = held[0] - OUTER_RATE * (share + OUTER_MOMENTUM * moment)
    made[0] = moment
    made[1] = share
    made[2] = AVERAGE_KEEP * held[2] + (1.0 - AVERAGE_KEEP) * new_share
    results[3][...] = new_share.astype(jnp.bfloat16)
    copies = [
        pltpu.make_async_copy(made.at[index], results[index].at[at], out_sems.at[index])
        for index in range(3)
    ]
    for copy in copies:
        copy.start()
    for copy in copies:
        copy.wait()


def join_kernel(place, *refs, piece, groups, chained):
    parts = refs[:groups]
    wide_hbm, low_hbm = refs[groups + chained : groups + chained + 2]
    wide, sems = refs[-2:]
    rows, columns = parts[0].shape
    at = pl.ds(piece * rows, rows)
    copies = []
    for step in range(groups):
        start = pl.multiple_of(lax.rem(place[0] + groups - step, groups) * columns, 128)
        wide[step] = parts[step][...].astype(jnp.float32)
        target = (at, pl.ds(start, columns))
        copies.append(pltpu.make_async_copy(wide.at[step], wide_hbm.at[target], sems.at[0, step]))
        copies.append(pltpu.make_async_copy(parts[step], low_hbm.at[target], sems.at[1, step]))
    for copy in copies:
        copy.start()
    for copy in copies:
        copy.wait()


def vmem(count):
    return [pl.BlockSpec(memory_space=pltpu.VMEM)] * count


def run_gather(lengths, picked, tokens_in, cot_in, plan):
    steps, count = picked.shape
    _, places, width = tokens_in.shape
    tokens = count + -count % 16
    padded = jnp.pad(picked, ((0, 0), (0, tokens - count)), constant_values=NOWHERE)
    shape = jax.ShapeDtypeStruct
    made = pl.pallas_call(
        functools.partial(gather_kernel, steps=steps, extra=len(plan)),
        in_specs=smem(1) + vmem(2) + anywhere(2) + smem(len(plan)),
        out_specs=vmem(2 * steps),
        out_shape=[shape((2, tokens, width), jnp.bfloat16)] * steps
        + [shape((2 * tokens, tokens), jnp.int32)] * steps,
        scratch_shapes=[
            pltpu.VMEM((steps, 2, places, width), jnp.bfloat16),
            pltpu.SemaphoreType.DMA((steps, 2)),
        ],
        compiler_params=pltpu.CompilerParams(vmem_limit_bytes=37 << 20),
        name="gather_rows",
    )(lengths, padded[:, :, None], padded[:, None, :], tokens_in, cot_in, *plan)
    return (made[:steps], made[steps:], padded[:, None, :])


def run_scatter(across, base, rows, step, chain, known):
    _, places, width = base.shape
    tokens = rows.shape[0]
    here = pl.BlockSpec((1, places, width), lambda index: (step, 0, 0))
    return pl.pallas_call(
        scatter_kernel,
        grid=(1,),
        in_specs=[
            pl.BlockSpec((1, 1, tokens), lambda index: (step, 0, 0)),
            here,
            pl.BlockSpec((tokens, width), lambda index: (0, 0)),
        ]
        + anywhere(len(chain) + len(known)),
        out_specs=[here, pl.BlockSpec((8, 128), lambda index: (0, 0))],
        out_shape=[
            jax.ShapeDtypeStruct(base.shape, base.dtype),
            jax.ShapeDtypeStruct((8, 128), jnp.float32),
        ],
        input_output_aliases=chain_aliases(3, chain),
        compiler_params=pltpu.CompilerParams(vmem_limit_bytes=56 << 20),
        cost_estimate=SMALL_COST,
        name="scatter_rows",
    )(across, base, rows, *chain, *known)


def run_attention(order, gathered, both, vec_now, mask, known):
    _, tokens, width = both.shape
    shape = jax.ShapeDtypeStruct
    return pl.pallas_call(
        functools.partial(attention_kernel, order=order, extra=len(known)),
        in_specs=anywhere(3) + vmem(1) + anywhere(len(known)),
        out_specs=vmem(4),
        out_shape=[
            shape((tokens, 3 * width), jnp.bfloat16),
            shape((2 * tokens, 128), jnp.float32),
            shape((2, tokens, width), jnp.bfloat16),
            shape((tokens, width), jnp.float32),
        ],
        scratch_shapes=[
            pltpu.VMEM((4 * width, width), jnp.bfloat16),
            pltpu.VMEM(mask.shape, jnp.int32),
            pltpu.VMEM((tokens, width), jnp.bfloat16),
            pltpu.SemaphoreType.DMA((4,)),
            pltpu.SemaphoreType.DMA,
            pltpu.SemaphoreType.DMA,
        ],
        compiler_params=pltpu.CompilerParams(vmem_limit_bytes=37 << 20),
        cost_estimate=pl.CostEstimate(
            flops=8 * tokens * width * width, bytes_accessed=8 * width * width, transcendentals=0
        ),
        name="attention",
    )(gathered, mask, both, vec_now, *known)


def run_feed_forward(order, gathered, both, vec_now, first_sum, keep):
    _, tokens, width = both.shape
    wide = gathered.shape[0]
    shape = jax.ShapeDtypeStruct
    kept = [shape((tokens, wide - 4 * width), jnp.bfloat16)] if keep else []
    return pl.pallas_call(
        functools.partial(feed_forward_kernel, keep=keep, order=order),
        in_specs=anywhere(1) + vmem(3),
        out_specs=vmem(4 + len(kept)),
        out_shape=[
            shape((tokens, width), jnp.bfloat16),
            shape((tokens, width), jnp.bfloat16),
            shape((tokens, width), jnp.float32),
            shape((2, width), jnp.float32),
        ]
        + kept,
        scratch_shapes=[
            pltpu.VMEM((wide - 4 * width, width), jnp.bfloat16),
            pltpu.SemaphoreType.DMA(((wide - 4 * width) // width,)),
        ],
        compiler_params=pltpu.CompilerParams(vmem_limit_bytes=37 << 20),
        cost_estimate=pl.CostEstimate(
            flops=8 * tokens * (wide - 4 * width) * width,
            bytes_accessed=2 * wide * width,
            transcendentals=0,
        ),
        name="feed_forward",
    )(gathered, both, vec_now, first_sum)


def smem(count):
    return [pl.BlockSpec(memory_space=pltpu.SMEM)] * count


def anywhere(count):
    return [pl.BlockSpec(memory_space=pl.ANY)] * count


def run_attention_back(order, gathered, starts, d_attn_low, proj, lse, mask, pair, got):
    tokens, width = d_attn_low.shape
    cuts = starts.shape[0]
    shape = jax.ShapeDtypeStruct
    return pl.pallas_call(
        functools.partial(attention_back_kernel, order=order),
        in_specs=anywhere(1) + smem(1) + vmem(3) + anywhere(3),
        out_specs=anywhere(2),
        out_shape=[
            shape((tokens, 3 * width), jnp.bfloat16),
            shape((2,) + pair.shape, jnp.bfloat16),
        ],
        scratch_shapes=[
            pltpu.VMEM((width, width), jnp.bfloat16),
            pltpu.VMEM((tokens, 3 * width), jnp.bfloat16),
            pltpu.SemaphoreType.DMA((1,)),
            pltpu.SemaphoreType.DMA((2,)),
            pltpu.SemaphoreType.DMA((cuts,)),
            pltpu.VMEM(mask.shape, jnp.int32),
            pltpu.SemaphoreType.DMA,
        ],
        compiler_params=pltpu.CompilerParams(vmem_limit_bytes=37 << 20),
        cost_estimate=pl.CostEstimate(
            flops=10 * tokens * width * width, bytes_accessed=4 * width * width, transcendentals=0
        ),
        name="attention_back",
    )(gathered, starts, d_attn_low, proj, lse, mask, pair, got)


def run_input_back(order, gathered, rows, d_proj, both, vec_now, base, known):
    _, tokens, width = both.shape
    cuts = rows.shape[0]
    shape = jax.ShapeDtypeStruct
    return pl.pallas_call(
        functools.partial(
            input_back_kernel, extra=len(known), order=order
        ),
        in_specs=anywhere(1) + smem(1) + vmem(4) + anywhere(len(known)),
        out_specs=vmem(2),
        out_shape=[
            shape((tokens, width), jnp.bfloat16),
            shape((1, width), jnp.float32),
        ],
        scratch_shapes=[
            pltpu.VMEM((cuts, 3 * width // cuts, width), jnp.bfloat16),
            pltpu.SemaphoreType.DMA((cuts,)),
        ],
        compiler_params=pltpu.CompilerParams(vmem_limit_bytes=37 << 20),
        cost_estimate=SMALL_COST,
        name="input_back",
    )(gathered, rows, d_proj, both, vec_now, base, *known)


def run_line(moves, below, above, terms, step, piece, passed, known):
    shape = jax.ShapeDtypeStruct(below.shape, jnp.bfloat16)
    return pl.pallas_call(
        functools.partial(line_kernel, step=step, piece=piece, passed=len(passed)),
        in_specs=smem(1) + vmem(2) + anywhere(1) + vmem(len(passed)) + anywhere(len(known)),
        out_specs=vmem(2 + len(passed)),
        out_shape=[shape, shape]
        + [jax.ShapeDtypeStruct(values.shape, values.dtype) for values in passed],
        scratch_shapes=[
            pltpu.VMEM((2,) + below.shape, jnp.bfloat16),
            pltpu.SemaphoreType.DMA((2,)),
        ],
        compiler_params=pltpu.CompilerParams(vmem_limit_bytes=16 << 20),
        cost_estimate=pl.CostEstimate(
            flops=LINE_FLOPS, bytes_accessed=6 * below.size * 2, transcendentals=0
        ),
        name="line",
    )(moves, below, above, terms, *passed, *known)


def chain_aliases(first, chain):
    return {first + index: index for index in range(len(chain))}


def run_update(place, below, above, terms, states, piece, step_count, last, groups, chain, known):
    rows, width = below.shape
    own = terms.shape[0] - PIECES + piece
    shape = jax.ShapeDtypeStruct
    wide = shape(states[0].shape, jnp.float32)
    columns = width // groups
    if last:
        out_shape = [wide, wide, shape((rows, columns), jnp.float32)]
        out_shape.append(shape((groups - 1, rows, columns), jnp.bfloat16))
        out_specs = anywhere(2) + vmem(2)
    else:
        out_shape = [wide, wide, wide, shape(states[0].shape, jnp.bfloat16)]
        out_specs = anywhere(4)
    operands = (place, below, above, terms, *states, *chain, *known)
    return pl.pallas_call(
        functools.partial(
            update_kernel,
            piece=piece,
            own=own,
            step_count=step_count,
            last=last,
            chained=len(chain),
            extra=len(known),
        ),
        in_specs=smem(1) + vmem(2) + anywhere(len(operands) - 3),
        out_specs=out_specs,
        out_shape=out_shape,
        scratch_shapes=[
            pltpu.VMEM((len(states), rows, width), jnp.float32),
            pltpu.VMEM((rows, width), jnp.bfloat16),
            pltpu.VMEM((3, rows, width), jnp.float32),
            pltpu.VMEM((rows, width), jnp.bfloat16),
            pltpu.SemaphoreType.DMA((4, len(states) + 1)),
            pltpu.SemaphoreType.DMA((4, 4)),
        ],
        input_output_aliases=chain_aliases(4 + len(states), chain),
        compiler_params=pltpu.CompilerParams(vmem_limit_bytes=52 << 20),
        cost_estimate=pl.CostEstimate(
            flops=LINE_FLOPS, bytes_accessed=24 * rows * width, transcendentals=0
        ),
        name="update",
    )(*operands)


def run_outer(place, own, got, arrays, piece, chain, known):
    rows, columns = own.shape
    shape = jax.ShapeDtypeStruct
    narrow = shape(arrays[1].shape, jnp.float32)
    operands = (place, own, *got, *arrays, *chain, *known)
    return pl.pallas_call(
        functools.partial(
            outer_kernel,
            piece=piece,
            groups=len(got) + 1,
            chained=len(chain),
            extra=len(known),
        ),
        in_specs=smem(1) + vmem(1 + len(got)) + anywhere(len(operands) - 2 - len(got)),
        out_specs=anywhere(3) + vmem(1),
        out_shape=[narrow] * 3 + [shape(own.shape, jnp.bfloat16)],
        scratch_shapes=[
            pltpu.VMEM((3, rows, columns), jnp.float32),
            pltpu.VMEM((3, rows, columns), jnp.float32),
            pltpu.SemaphoreType.DMA((3,)),
            pltpu.SemaphoreType.DMA((3,)),
        ],
        input_output_aliases=chain_aliases(5 + len(got), chain),
        compiler_params=pltpu.CompilerParams(vmem_limit_bytes=52 << 20),
        cost_estimate=pl.CostEstimate(
            flops=LINE_FLOPS, bytes_accessed=24 * rows * columns, transcendentals=0
        ),
        name="outer",
    )(*operands)


def run_join(place, parts, like, piece, chain):
    rows, columns = parts[0].shape
    groups = len(parts)
    operands = (place, *parts, *chain)
    return pl.pallas_call(
        functools.partial(join_kernel, piece=piece, groups=groups, chained=len(chain)),
        in_specs=smem(1) + vmem(groups) + anywhere(len(chain)),
        out_specs=anywhere(2),
        out_shape=[
            jax.ShapeDtypeStruct(like.shape, jnp.float32),
            jax.ShapeDtypeStruct(like.shape, jnp.bfloat16),
        ],
        scratch_shapes=[
            pltpu.VMEM((groups, rows, columns), jnp.float32),
            pltpu.SemaphoreType.DMA((2, groups)),
        ],
        input_output_aliases=chain_aliases(1 + groups, chain),
        compiler_params=pltpu.CompilerParams(vmem_limit_bytes=52 << 20),
        cost_estimate=pl.CostEstimate(
            flops=LINE_FLOPS, bytes_accessed=12 * rows * columns * groups, transcendentals=0
        ),
        name="join",
    )(*operands)


def run_products(
    info, needs, gathered, proj_parts, attn_parts, plane_h1, plane_d_down, pairs, piece, known
):
    count = info.shape[0]
    sources, tokens, width = plane_h1.shape
    shape = jax.ShapeDtypeStruct((count, piece, width), jnp.bfloat16)
    made = pl.pallas_call(
        functools.partial(feed_forward_products_kernel, extra=len(attn_parts)),
        in_specs=smem(2) + anywhere(2 + len(pairs) + len(attn_parts)),
        out_specs=vmem(1)[0],
        out_shape=shape,
        scratch_shapes=[
            pltpu.VMEM((2, sources * tokens, width), jnp.bfloat16),
            pltpu.VMEM((count, piece, width), jnp.bfloat16),
            pltpu.VMEM((count, piece, width), jnp.bfloat16),
            pltpu.SemaphoreType.DMA((2, sources)),
            pltpu.SemaphoreType.DMA((count,)),
            pltpu.SemaphoreType.DMA((count,)),
        ],
        compiler_params=pltpu.CompilerParams(vmem_limit_bytes=37 << 20),
        cost_estimate=pl.CostEstimate(
            flops=6 * count * sources * tokens * piece * width,
            bytes_accessed=6 * count * piece * width,
            transcendentals=0,
        ),
        name="feed_forward_products",
    )(info, needs, gathered, plane_d_down, *pairs, *attn_parts)
    near = made
    for first, last in ((0, PIECES), (PIECES, count)):
        known = () if first else known
        operands = (info, needs, plane_h1, *proj_parts, *attn_parts, *pairs, *known, near, made)
        blocks = last - first
        found = pl.pallas_call(
            functools.partial(
                attention_products_kernel,
                sources=sources,
                extra=len(known),
                first=first,
                last=last,
            ),
            in_specs=smem(2) + anywhere(len(operands) - 2),
            out_specs=anywhere(1)[0],
            out_shape=jax.ShapeDtypeStruct((count if first else last, piece, width), jnp.bfloat16),
            scratch_shapes=[
                pltpu.VMEM((2, sources * tokens, width), jnp.bfloat16),
                pltpu.VMEM((sources * tokens, blocks * piece), jnp.bfloat16),
                pltpu.VMEM((sources * tokens, width), jnp.bfloat16),
                pltpu.VMEM((blocks, piece, width), jnp.bfloat16),
                pltpu.SemaphoreType.DMA((2, sources)),
                pltpu.SemaphoreType.DMA((2, sources)),
                pltpu.SemaphoreType.DMA((count,)),
            ],
            input_output_aliases={len(operands) - 1: 0} if first else {},
            compiler_params=pltpu.CompilerParams(vmem_limit_bytes=16 << 20),
            cost_estimate=SMALL_COST,
            name="attention_products",
        )(*operands)
        if first:
            return (near, found)
        near = found


def pad_rows(rows):
    return jnp.pad(rows, ((0, -rows.shape[0] % 16), (0, 0)))


def swap(values, axis, delta):
    size = lax.axis_size(axis)
    return lax.ppermute(values, axis, [(i, i ^ delta) for i in range(size)])


def sum_over(values, axes):
    for axis in axes:
        parts = [values]
        parts += [swap(values, axis, delta) for delta in range(1, lax.axis_size(axis))]
        while len(parts) > 1:
            parts = [parts[at] + parts[at + 1] for at in range(0, len(parts), 2)]
        values = parts[0]
    return values


def gathered_rows(values):
    return lax.all_gather(pad_rows(values), ("dp", "fsdp"), axis=0, tiled=False)


def line_order(line):
    due = np.zeros((line, line), np.int32)
    for here in range(line):
        for there in range(line):
            if there > here:
                due[here, there] = line - 1 - there + here
            elif there < here:
                due[here, there] = there - here + line - 1
            else:
                due[here, there] = line
    return np.argsort(due, axis=1, kind="stable").astype(np.int32)


def line_slots(line, order):
    ups = np.zeros((line - 1, line), np.int32)
    downs = np.zeros((line - 1, line), np.int32)
    for step in range(line - 1):
        for here in range(line):
            if here <= step:
                ups[step, here] = list(order[here]).index(line - 1 - step + here)
            if line - 1 - here <= step:
                downs[step, here] = list(order[here]).index(step - (line - 1) + here)
    return ups, downs


def added(*parts):
    return sum(part.astype(jnp.float32) for part in parts)


def due_after(value, *marks):
    flag = sum(mark[(-1,) * mark.ndim].astype(jnp.float32) for mark in marks)
    return value + (flag != flag).astype(value.dtype)


def plane_order(planes):
    deltas = [0]
    bit = planes // 2
    while bit >= 1:
        deltas = deltas + [delta ^ bit for delta in deltas]
        bit //= 2
    return deltas


def plane_gather(values):
    values = values[None]
    bit = lax.axis_size("fsdp") // 2
    while bit >= 1:
        values = jnp.concatenate([values, swap(values, "fsdp", bit)], axis=0)
        bit //= 2
    return values


def plane_operands(plane_rows, vec_now):
    sel_rows = plane_rows[:, 0].astype(jnp.float32)
    cot_rows = plane_rows[:, 1].astype(jnp.float32)
    gate = jax.nn.sigmoid(jnp.sum(sel_rows * vec_now[2], axis=-1, keepdims=True))
    inverse = lax.rsqrt(row_mean(sel_rows * sel_rows) + EPS_NORM)
    h1 = (sel_rows * inverse * vec_now[0]).astype(jnp.bfloat16)
    return (h1, (gate * cot_rows).astype(jnp.bfloat16))


def send_to(target, values):
    planes = lax.axis_size("fsdp")
    return [values] + [
        lax.ppermute(values, "fsdp", [(target ^ delta, target)]) for delta in plane_order(planes)[1:]
    ]


def gradient_plan(shard_rows, model_width, columns):
    planes, line = lax.axis_size("fsdp"), lax.axis_size("dp")
    plane, here = lax.axis_index("fsdp"), lax.axis_index("dp")
    hidden_units = (columns - 4 * model_width) // 2
    edges = (3 * model_width, 4 * model_width, 4 * model_width + hidden_units)

    def kind_of(row):
        return sum((row >= edge).astype(jnp.int32) for edge in edges)

    piece = shard_rows // PIECES
    theres = jnp.asarray(line_order(line))[here]
    rows = (plane * line + theres)[:, None] * shard_rows + jnp.arange(PIECES) * piece
    rows = rows.reshape(-1)
    kinds = kind_of(rows)
    at = rows - 3 * model_width
    order = (planes, line, shard_rows)
    uppers = gathered_row(jnp.where(kinds == 2, rows, rows - hidden_units), order)
    lowers = gathered_row(jnp.minimum(rows + hidden_units, columns - piece), order)
    info = jnp.stack([kinds, jnp.where(kinds >= 2, uppers, at), lowers], axis=1)
    low, high = kind_of(plane * line * shard_rows), kind_of((plane + 1) * line * shard_rows - 1)
    ff = (high >= 2).astype(jnp.int32)
    has_proj = (low == 0).astype(jnp.int32)
    has_attn = ((low <= 1) & (high >= 1)).astype(jnp.int32)
    moves = jnp.asarray(np.stack(line_slots(line, line_order(line)), axis=-1))[:, here]
    return (info.astype(jnp.int32), jnp.stack([has_proj, has_attn, ff, ff]), moves)


def gradient_starts(shard_rows, model_width, split):
    line, here = lax.axis_size("dp"), lax.axis_index("dp")
    if split:
        return jnp.asarray(line_order(line) * shard_rows)[here]
    return jnp.arange(4, dtype=jnp.int32) * (3 * model_width // 4)


def in_planes(shard_rows, model_width):
    line = lax.axis_size("dp")
    return (shard_rows // PIECES) % 128 == 0 and line * shard_rows == 3 * model_width


def gradient_whole(columns, operands):
    hidden_units = columns[2].shape[1] // 2
    factors = (*columns[:2], columns[2][:, :hidden_units], columns[2][:, hidden_units:])
    products = [tn(factor, operand) for factor, operand in zip(factors, operands)]
    low = jnp.concatenate(products, axis=0).astype(jnp.bfloat16)
    share = lax.psum_scatter(low, ("fsdp", "dp"), scatter_dimension=0, tiled=True)
    return share.astype(jnp.float32)


def plane_terms(
    gathered, d_proj, d_attn_low, pairs, plane_h1, plane_d_down, info, needs, shard_rows, known
):
    attn_parts = send_to(1, d_attn_low)
    pairs = [pairs]
    bit = lax.axis_size("fsdp") // 4
    while bit >= 1:
        pairs.append(swap(jnp.concatenate(pairs, axis=0), "fsdp", bit))
        bit //= 2
    return run_products(
        info,
        needs,
        gathered,
        send_to(0, d_proj),
        attn_parts,
        plane_h1,
        plane_d_down,
        pairs,
        shard_rows // PIECES,
        known,
    )


def gradient_share(near, terms, moves, passed, meanwhile):
    line = lax.axis_size("dp")
    below, above = [None] * PIECES, [None] * PIECES
    for step in range(line - 1):
        for index in range(PIECES):
            if step == 0:
                up = down = near[index]
            else:
                due = known[index] if step == line - 2 else ()
                given = passed if step == 1 and index == 0 else ()
                up, down, *given = run_line(
                    moves, below[index], above[index], terms, step, index, given, due
                )
                if step == 1 and index == 0:
                    known = meanwhile(up, given)
            below[index] = lax.ppermute(up, "dp", [(p, p + 1) for p in range(step + 1)])
            above[index] = lax.ppermute(
                down, "dp", [(line - 1 - p, line - 2 - p) for p in range(step + 1)]
            )
    return (below, above)


def adamw(param, grad, first, second, step_count, rate, decay):
    first = BETA_ONE * first + (1.0 - BETA_ONE) * grad
    second = BETA_TWO * second + (1.0 - BETA_TWO) * grad * grad
    fixed_one = 1.0 - BETA_ONE**step_count
    fixed_two = 1.0 - BETA_TWO**step_count
    direction = first / fixed_one / (jnp.sqrt(second / fixed_two) + EPS_ADAM)
    return (param - rate * (direction + decay * param), first, second)


def vector_rates():
    return jnp.array([[0.1], [0.1], [0.02]], dtype=jnp.float32)


def outer_whole(weights, master, outer_moment, smoothed_matrix_mean):
    groups = lax.axis_size("grp")
    here = lax.axis_index("grp")
    delta = weights - master
    col_width = weights.shape[1] // groups
    col_start = here * col_width
    diff_share = lax.dynamic_slice_in_dim(delta, col_start, col_width, 1)
    for step in range(1, groups):
        there = lax.rem(here + step, groups)
        part = lax.dynamic_slice_in_dim(delta, there * col_width, col_width, 1)
        diff_share = diff_share + shift_group(part.astype(jnp.bfloat16), step).astype(jnp.float32)
    diff_share = diff_share / groups
    moment_share = OUTER_MOMENTUM * outer_moment + diff_share
    base_share = lax.dynamic_slice_in_dim(weights, col_start, col_width, 1)
    new_share = base_share - OUTER_RATE * (diff_share + OUTER_MOMENTUM * moment_share)
    low_share = new_share.astype(jnp.bfloat16)
    weights_low = jnp.zeros(weights.shape, jnp.bfloat16)
    for step in range(groups):
        there = lax.rem(here + groups - step, groups)
        part = shift_group(low_share, step) if step else low_share
        weights_low = lax.dynamic_update_slice_in_dim(weights_low, part, there * col_width, 1)
    average_new = AVERAGE_KEEP * smoothed_matrix_mean + (1.0 - AVERAGE_KEEP) * new_share
    return (weights_low.astype(jnp.float32), weights_low, moment_share, diff_share, average_new)


def shift_group(values, step):
    groups = lax.axis_size("grp")
    return lax.ppermute(values, "grp", [(i, (i + step) % groups) for i in range(groups)])


def on_device(
    tokens,
    cotangent,
    lengths,
    selected,
    weights,
    vectors,
    first_moment,
    second_moment,
    vec_first,
    vec_second,
    outer_moment,
    smoothed_matrix_mean,
    vec_outer,
    vec_average,
):
    master = weights
    vec_now = vectors
    first_now = first_moment[0]
    second_now = second_moment[0]
    vfirst_now = vec_first[0]
    vsecond_now = vec_second[0]
    model_width = tokens.shape[2]
    planes, line = lax.axis_size("fsdp"), lax.axis_size("dp")
    shard_rows = weights.shape[0]
    info, needs, moves = gradient_plan(shard_rows, model_width, weights.shape[0] * planes * line)
    split = in_planes(shard_rows, model_width)
    starts = gradient_starts(shard_rows, model_width, split)
    order = (planes, line, shard_rows)
    weight_starts = gathered_row(starts, order)
    plan = (info, needs, moves, starts, weight_starts)
    boths, masks, across = run_gather(lengths[:, 0], selected[:, 0], tokens, cotangent, plan)
    plane_rows = plane_gather(boths[0])
    groups = lax.axis_size("grp")
    place = lax.axis_index("grp").astype(jnp.int32)[None]
    shard_low = master.astype(jnp.bfloat16)
    activations, input_grad, outers = [], [], []
    for inner_step in range(INNER):
        both, mask = boths[inner_step], masks[inner_step]
        gathered = lax.all_gather(shard_low, ("dp", "fsdp"), axis=0, tiled=True)
        plane_h1, plane_d_down = plane_operands(plane_rows, vec_now)
        proj, lse, pair, first_sum = run_attention(
            order,
            gathered,
            both,
            vec_now,
            mask,
            [plane_h1, plane_d_down, *activations[1:], *input_grad[1:]],
        )
        d_attn_low, out_rows, base, grad_two, *kept = run_feed_forward(
            order, gathered, both, vec_now, first_sum, not split
        )
        got = swap(pair[None], "fsdp", planes // 2)
        d_proj, pairs = run_attention_back(
            order, gathered, starts, d_attn_low, proj, lse, mask, pair, got
        )
        following = list(boths[inner_step + 1 : inner_step + 2])
        last = not following
        step_count = STEP + inner_step
        results = []

        def input_step(marks):
            d_rows, grad_one = run_input_back(
                None if split else order, gathered, weight_starts, d_proj, both, vec_now, base, marks
            )
            results.append(jnp.concatenate([grad_one, grad_two], axis=0))
            return d_rows

        def scatter_out(marks):
            activations[:] = run_scatter(
                across, tokens, out_rows, inner_step, activations[:1], marks
            )

        def scatter_grad(d_rows, marks):
            input_grad[:] = run_scatter(
                across, cotangent, d_rows, inner_step, input_grad[:1], marks
            )

        if split and last:
            d_rows = input_step([])
            results[0] = gathered_rows(results[0])

        def meanwhile(mark, passed):
            if not last:
                results.append(plane_gather(passed[0]))
                return (results[-1:], (), ())
            return ((), (), ())

        if split:
            near, terms = plane_terms(
                gathered,
                d_proj,
                d_attn_low,
                pairs,
                plane_h1,
                plane_d_down,
                info,
                needs,
                shard_rows,
                [d_rows] if last else (),
            )
            below, above = gradient_share(near, terms, moves, following, meanwhile)
            grad_mark = below[-1]
        else:
            grad_mark = gradient_whole(
                (d_proj, d_attn_low, *kept), (plane_h1[0], pair[0], pair[1], plane_d_down[0])
            )
            results.extend(plane_gather(values) for values in following)
        if split and last:
            made = []
            for index in range(PIECES):
                made.append(
                    run_update(
                        place,
                        below[index],
                        above[index],
                        terms,
                        (master, first_now, second_now, weights),
                        index,
                        step_count,
                        last,
                        groups,
                        made[-1][:2] if index else (),
                        [outers[0][3]] if index == PIECES - 1 else activations[1:],
                    )
                )
                own, other = made[-1][2:]
                if index == 0:
                    scatter_out([own])
                if index == PIECES - 1:
                    scatter_grad(d_rows, [own])
                outers.append(
                    run_outer(
                        place,
                        own,
                        [shift_group(other[step - 1], step) for step in range(1, groups)],
                        (weights, outer_moment, smoothed_matrix_mean),
                        index,
                        outers[-1][:3] if index else (),
                        input_grad[1:] if index == PIECES - 1 else [],
                    )
                )
            first_now, second_now = made[-1][:2]
        else:
            grad_shard = grad_mark
            if split:
                own = (line - 1) * PIECES
                grad_shard = jnp.concatenate(
                    [
                        added(terms[own + index], below[index], above[index])
                        for index in range(PIECES)
                    ],
                    axis=0,
                )
            master, first_now, second_now = adamw(
                master, grad_shard, first_now, second_now, step_count, INNER_RATE, DECAY_RATE
            )
            shard_low = master.astype(jnp.bfloat16)
        if not last:
            plane_rows = results.pop()
        if split and last:
            grad_vec = jnp.sum(due_after(results[0][:, : vec_now.shape[0]], made[0][2]), axis=0)
            vec_now, vfirst_now, vsecond_now = adamw(
                vec_now, grad_vec, vfirst_now, vsecond_now, step_count, vector_rates(), 0.0
            )
            vec_diff = sum_over(vectors - vec_now, ("grp",)) / groups
        else:
            scatter_out([grad_mark])
            scatter_grad(input_step([grad_mark]), [grad_mark])
            grad_vec = sum_over(due_after(results[0], grad_mark), ("fsdp", "dp"))
            vec_now, vfirst_now, vsecond_now = adamw(
                vec_now, grad_vec, vfirst_now, vsecond_now, step_count, vector_rates(), 0.0
            )
    if split:
        joined = []
        for index in range(PIECES):
            low = outers[index][3]
            parts = [low] + [shift_group(low, step) for step in range(1, groups)]
            joined = run_join(place, parts, weights, index, joined)
        weights_new, weights_low = joined
        outer_new, diff_new, average_new = outers[-1][:3]
    else:
        weights_new, weights_low, outer_new, diff_new, average_new = outer_whole(
            weights, master, outer_moment, smoothed_matrix_mean
        )
    if not split:
        vec_diff = sum_over(vectors - vec_now, ("grp",)) / groups
    vec_moment = OUTER_MOMENTUM * vec_outer + vec_diff
    vectors_new = vectors - OUTER_RATE * (vec_diff + OUTER_MOMENTUM * vec_moment)
    vec_average_new = AVERAGE_KEEP * vec_average + (1.0 - AVERAGE_KEEP) * vectors_new
    return (
        activations[0],
        input_grad[0],
        weights_new,
        weights_low,
        first_now[None],
        second_now[None],
        outer_new,
        diff_new,
        average_new,
        vectors_new,
        vfirst_now[None],
        vsecond_now[None, :2],
        vsecond_now[None, 2],
        vec_moment,
        vec_average_new,
    )


def solution(mesh):
    placed = (
        P(None, ("grp", "fsdp", "dp"), None),
        P(None, ("grp", "fsdp", "dp"), None),
        P(None, ("grp", "fsdp", "dp"), None),
        P(None, ("grp", "fsdp", "dp"), None),
        P(("fsdp", "dp"), None),
        P(),
        P("grp", ("fsdp", "dp"), None),
        P("grp", ("fsdp", "dp"), None),
        P("grp", None, None),
        P("grp", None, None),
        P(("fsdp", "dp"), "grp"),
        P(("fsdp", "dp"), "grp"),
        P(),
        P(),
    )
    return jax.shard_map(
        on_device,
        mesh=mesh,
        in_specs=placed,
        out_specs=(
            P(None, ("grp", "fsdp", "dp"), None),
            P(None, ("grp", "fsdp", "dp"), None),
            P(("fsdp", "dp"), None),
            P(("fsdp", "dp"), None),
            P("grp", ("fsdp", "dp"), None),
            P("grp", ("fsdp", "dp"), None),
            P(("fsdp", "dp"), "grp"),
            P(("fsdp", "dp"), "grp"),
            P(("fsdp", "dp"), "grp"),
            P(),
            P("grp", None, None),
            P("grp", None, None),
            P("grp", None),
            P(),
            P(),
        ),
        check_vma=False,
    )
```
